32 devices in a mesh: wide: 8 (over z, x), narrow: 4 (over y, core).
Axes of the slice: x: 2, y: 2, z: 4, core: 2. Of those that a mesh axis runs over, the one named last changes fastest.
Arguments:
- patches: bfloat16 [4096, 128, 384], P(('wide', 'narrow')), may hold values from -6 to 6
- visible: int32 [4096, 64], P(('wide', 'narrow')), may hold values from 0 to 127, as said below
- counts: int32 [4096], P(('wide', 'narrow')), may hold values from 13 to 64, as said below
- upstream: bfloat16 [4096, 64, 384], P(('wide', 'narrow')), may hold values from -6 to 6
- w_qkv: bfloat16 [384, 1152], replicated, may hold values from -0.3125 to 0.3125
- b_query: float32 [384], replicated, may hold values from -1.5 to 1.5
- b_value: float32 [384], replicated, may hold values from -1.5 to 1.5
- w_out: bfloat16 [384, 384], replicated, may hold values from -0.875 to 0.875
- b_out: float32 [384], replicated, may hold values from -1.5 to 1.5
- w_up: bfloat16 [384, 1536], replicated, may hold values from -0.3125 to 0.3125
- b_up: float32 [1536], replicated, may hold values from -1.5 to 1.5
- w_down: bfloat16 [1536, 384], replicated, may hold values from -0.15625 to 0.15625
- b_down: float32 [384], replicated, may hold values from -1.5 to 1.5
- gain_attn: float32 [384], replicated, may hold values from 0.25 to 1.75
- shift_attn: float32 [384], replicated, may hold values from -1.5 to 1.5
- gain_mlp: float32 [384], replicated, may hold values from 0.25 to 1.75
- shift_mlp: float32 [384], replicated, may hold values from -1.5 to 1.5
Outputs:
- encoded: bfloat16 [4096, 64, 384], P(('wide', 'narrow'))
- input_grad: bfloat16 [4096, 128, 384], P(('wide', 'narrow'))
- grad_w_qkv: float32 [384, 1152], replicated
- grad_b_query: float32 [384], replicated
- grad_b_value: float32 [384], replicated
- grad_w_out: float32 [384, 384], replicated
- grad_b_out: float32 [384], replicated
- grad_w_up: float32 [384, 1536], replicated
- grad_b_up: float32 [1536], replicated
- grad_w_down: float32 [1536, 384], replicated
- grad_b_down: float32 [384], replicated
- grad_gain_attn: float32 [384], replicated
- grad_shift_attn: float32 [384], replicated
- grad_gain_mlp: float32 [384], replicated
- grad_shift_mlp: float32 [384], replicated
The draws below stay inside these ranges and needn't reach their ends.
Inputs may be any that keep to these rules, and one draw needn't show every extreme that they name: Devices are numbered in the order of the blocks of 128 fields. For every field number l within a block, the counts of field l over all devices sum to exactly (77) times half the number of devices. Each row lists distinct patch numbers; the first counts[f] entries of row f are the visible patches of field f.
All inputs are finite; a program needn't handle non-finite values.
Results may differ from the reference program's by a relative error of at most 0.012.
The reference program's roundings to bfloat16 on the way count: a program that leaves them out, or rounds other values in their place, can miss the bound.
Values may be sent and summed in bfloat16 or wider, within the bound.
A program may use at most 384 MiB of HBM per device.

```python
import math
import jax
import jax.numpy as jnp
from jax import lax

D = 384
HEADS = 6
HD = 64
FF = 1536
NPATCH = 128
FLD_DEV = 128
VMAX = 64
CMIN = 13
FIELDS = 4096


def draw_counts(key, part):
    key = jax.random.fold_in(key, 11)
    device_count = FIELDS // FLD_DEV
    half_count = device_count // 2
    key_value, key_order = jax.random.split(key, 2)
    lower = jax.random.randint(key_value, (half_count, FLD_DEV), CMIN, VMAX + 1)
    lower = lower.at[0, 0].set(VMAX)
    paired = jnp.concatenate([lower, CMIN + VMAX - lower], axis=0)
    column_keys = jax.random.split(key_order, FLD_DEV)
    orders = jax.vmap(lambda column_key: jax.random.permutation(column_key, device_count))(column_keys)
    shuffled = jnp.take_along_axis(paired, jnp.transpose(orders).astype(jnp.int32), axis=0)
    return shuffled.reshape(FIELDS).astype(jnp.int32)


def draw_visible(key, part):
    key = jax.random.fold_in(key, 12)
    field_keys = jax.random.split(key, FIELDS)
    orders = jax.vmap(lambda field_key: jax.random.permutation(field_key, NPATCH))(field_keys)
    return orders[:, :VMAX].astype(jnp.int32)


def block_scale(own_key, extent, shards, smallest, largest):
    loudness, own = 1.0, jax.random.fold_in(own_key, 6)
    for dim, blocks in shards:
        heights = jnp.exp(jax.random.uniform(jax.random.fold_in(own, dim), (blocks,), jnp.float32, smallest / len(shards), largest / len(shards)))
        loudness = loudness * jnp.repeat(heights, extent[dim] // blocks).reshape([-1 if axis == dim else 1 for axis in range(len(extent))])
    return loudness


def centred(stream_key, shape, deviation, most, cuts=(), kind=jnp.bfloat16):
    entries = deviation * jax.random.normal(stream_key, shape, jnp.float32)
    if cuts:
        entries = entries * block_scale(stream_key, shape, cuts, -0.22, 0.18)
    return jnp.clip(entries, -most, most).astype(kind)


def setup_inputs(seed: int = 0) -> dict:
    keys = jax.random.split(jax.random.key(seed), 18)
    return {
        "patches": centred(keys[0], (FIELDS, NPATCH, D), 1.0, 6.0, ((0, 32),)),
        "visible": draw_visible(jax.random.fold_in(keys[17], 71), 0),
        "counts": draw_counts(jax.random.fold_in(keys[17], 71), 0),
        "upstream": centred(keys[3], (FIELDS, VMAX, D), 1.0, 6.0, ((0, 32),)),
        "w_qkv": centred(keys[4], (D, 3 * D), D ** -0.5, 0.3125),
        "b_query": centred(keys[5], (D,), 0.3, 1.5, (), jnp.float32),
        "b_value": centred(keys[6], (D,), 0.3, 1.5, (), jnp.float32),
        "w_out": centred(keys[7], (D, D), (D // 8) ** -0.5, 0.875),
        "b_out": centred(keys[8], (D,), 0.3, 1.5, (), jnp.float32),
        "w_up": centred(keys[9], (D, FF), D ** -0.5, 0.3125),
        "b_up": centred(keys[10], (FF,), 0.3, 1.5, (), jnp.float32),
        "w_down": centred(keys[11], (FF, D), FF ** -0.5, 0.15625),
        "b_down": centred(keys[12], (D,), 0.3, 1.5, (), jnp.float32),
        "gain_attn": jnp.clip(1.0 + 0.15 * jax.random.normal(keys[13], (D,), jnp.float32), 0.25, 1.75),
        "shift_attn": centred(keys[14], (D,), 0.3, 1.5, (), jnp.float32),
        "gain_mlp": jnp.clip(1.0 + 0.15 * jax.random.normal(keys[15], (D,), jnp.float32), 0.25, 1.75),
        "shift_mlp": centred(keys[16], (D,), 0.3, 1.5, (), jnp.float32),
    }


NORM_EPSILON = 1e-06
MASK_FILL = -1e+30

@jax.custom_vjp
def low(v):
    return lax.optimization_barrier(v.astype(jnp.bfloat16)).astype(jnp.float32)

@jax.custom_vjp
def low_back(v):
    return v

def low_keep(v):
    return (low(v), None)

def low_pass(kept, grad):
    return (grad,)

def back_keep(v):
    return (v, None)

def back_low(kept, grad):
    return (low(grad),)
low.defvjp(low_keep, low_pass)
low_back.defvjp(back_keep, back_low)

def layer_norm(values, gain, shift):
    row_mean = lax.optimization_barrier(jnp.mean(values, axis=-1, keepdims=True))
    centered = values - row_mean
    variance = lax.optimization_barrier(jnp.mean(centered * centered, axis=-1, keepdims=True))
    return centered * lax.rsqrt(variance + NORM_EPSILON) * gain + shift

def matmul(left, right):
    return jnp.einsum('...d,de->...e', left, right, precision=lax.Precision.HIGHEST)

def forward(inputs, live_mask, params):
    w_qkv, b_query, b_value, w_out, b_out, w_up, b_up, w_down, b_down, gain_attn, shift_attn, gain_mlp, shift_mlp = params
    fields, row_count, model_width = inputs.shape
    normed = low(layer_norm(inputs, gain_attn, shift_attn))
    qkv_bias = jnp.concatenate([b_query, jnp.zeros_like(b_query), b_value])
    packed = low_back(low(matmul(normed, w_qkv) + qkv_bias))
    packed = packed.reshape(fields, row_count, 3, HEADS, HD)
    queries = packed[:, :, 0]
    keys_all = packed[:, :, 1]
    values_all = packed[:, :, 2]
    scores = jnp.einsum('fqhe,fkhe->fhqk', queries, keys_all, precision=lax.Precision.HIGHEST)
    scores = low_back(scores * HD ** (-0.5))
    scores = jnp.where(live_mask[:, None, None, :] > 0, scores, MASK_FILL)
    row_max = lax.optimization_barrier(jnp.max(scores, axis=-1, keepdims=True))
    expo = jnp.exp(scores - row_max)
    probs = expo / lax.optimization_barrier(jnp.sum(expo, axis=-1, keepdims=True))
    probs_b = low(probs)
    mixed = jnp.einsum('fhqk,fkhe->fqhe', probs_b, values_all, precision=lax.Precision.HIGHEST)
    mixed = low_back(low(mixed.reshape(fields, row_count, model_width)))
    attended = low_back(matmul(mixed, w_out) + b_out)
    residual = inputs + attended
    normed2 = low(layer_norm(residual, gain_mlp, shift_mlp))
    up_proj = low_back(matmul(normed2, w_up) + b_up)
    act_b = low(jax.nn.gelu(up_proj, approximate=False))
    down_out = low_back(matmul(act_b, w_down) + b_down)
    return (residual + down_out) * live_mask[:, :, None]

def reference(patches, visible, counts, upstream, w_qkv, b_query, b_value, w_out, b_out, w_up, b_up, w_down, b_down, gain_attn, shift_attn, gain_mlp, shift_mlp):
    params = tuple((item.astype(jnp.float32) for item in (w_qkv, b_query, b_value, w_out, b_out, w_up, b_up, w_down, b_down, gain_attn, shift_attn, gain_mlp, shift_mlp)))
    group_size = math.gcd(FIELDS, max(1, 4096 // VMAX))
    step_count = FIELDS // group_size

    def blocked(array):
        return array.reshape((step_count, group_size) + array.shape[1:])

    def one_group(grad_total, element):
        grid, chosen, count_group, cotangent = element
        live_mask = (jnp.arange(VMAX)[None, :] < count_group[:, None]).astype(jnp.float32)

        def forward_group(grid_f, prm):
            gathered = jax.vmap(lambda grid_rows, picks: grid_rows[picks])(grid_f, chosen)
            return forward(gathered, live_mask, prm)
        encoded_group, pullback = jax.vjp(forward_group, grid.astype(jnp.float32), params)
        grid_grad, param_grad = pullback(cotangent.astype(jnp.float32))
        grad_total = jax.tree.map(lambda left, right: left + right, grad_total, param_grad)
        return (grad_total, (encoded_group.astype(jnp.bfloat16), grid_grad.astype(jnp.bfloat16)))
    zeros_tree = jax.tree.map(jnp.zeros_like, params)
    grad_total, (encoded_all, grads_all) = lax.scan(one_group, zeros_tree, (blocked(patches), blocked(visible), blocked(counts), blocked(upstream)))
    return (encoded_all.reshape(FIELDS, VMAX, D), grads_all.reshape(FIELDS, NPATCH, D), grad_total[0], grad_total[1], grad_total[2], grad_total[3], grad_total[4], grad_total[5], grad_total[6], grad_total[7], grad_total[8], grad_total[9], grad_total[10], grad_total[11], grad_total[12])
```

```python
import functools

import jax
import jax.numpy as jnp
from jax import lax
from jax.experimental import pallas as pl
from jax.experimental.pallas import tpu as pltpu
from jax.sharding import PartitionSpec as P

HEAD = 64
EPS = 1e-06
FILL = -1e30
ROWS = 512
TILE = 16
UNROLL = 4
GROUP = 8
CHUNK = 256
VMEM_BYTES = 60 * 1024 * 1024
f32 = jnp.float32
bf16 = jnp.bfloat16


def mm(left, right):
    return lax.dot_general(left, right, (((1,), (0,)), ((), ())), preferred_element_type=f32)


def mm_nt(left, right):
    return lax.dot_general(left, right, (((1,), (1,)), ((), ())), preferred_element_type=f32)


def mm_tn(left, right):
    return lax.dot_general(left, right, (((0,), (0,)), ((), ())), preferred_element_type=f32)


def row_norm(values):
    width = values.shape[-1]
    mean = jnp.sum(values, axis=-1, keepdims=True) * (1.0 / width)
    centered = values - mean
    variance = jnp.sum(centered * centered, axis=-1, keepdims=True) * (1.0 / width)
    rstd = lax.rsqrt(variance + EPS)
    return centered * rstd, rstd


def norm_back(grad, unit, rstd):
    width = grad.shape[-1]
    first = jnp.sum(grad, axis=-1, keepdims=True) * (1.0 / width)
    second = jnp.sum(grad * unit, axis=-1, keepdims=True) * (1.0 / width)
    return (grad - first - unit * second) * rstd


def fold(values):
    rows, width = values.shape
    return jnp.sum(values.reshape(rows // 8, 8, width), axis=0)


def head_mask(heads):
    size = heads * HEAD
    row = lax.broadcasted_iota(jnp.int32, (size, size), 0) // HEAD
    col = lax.broadcasted_iota(jnp.int32, (size, size), 1) // HEAD
    return row == col


def head_parts(width):
    parts, at = [], 0
    while at < width:
        size = min(4 * HEAD, width - at)
        parts.append((at, size))
        at += size
    return parts


def block_heads(values, at, size):
    part = values[:, at : at + size]
    count = size // HEAD
    tiled = jnp.concatenate([part] * count, axis=0)
    return jnp.where(head_mask(count), tiled, jnp.zeros((), tiled.dtype))


def heads_dot(left, stacked):
    parts = [
        mm_nt(left[:, at : at + size], block)
        for (at, size), block in zip(head_parts(left.shape[1]), stacked)
    ]
    return jnp.concatenate(parts, axis=1)


def heads_out(left, stacked):
    parts = [
        mm(left[:, at : at + size], block)
        for (at, size), block in zip(head_parts(left.shape[1]), stacked)
    ]
    return jnp.concatenate(parts, axis=1)


def heads_out_t(weights, values):
    window = weights.shape[1] // (values.shape[1] // HEAD)
    parts = []
    for at in range(0, values.shape[1], 2 * HEAD):
        pair = mm_tn(weights[:, at : at + 2 * HEAD], values[:, at : at + 2 * HEAD])
        lane = lax.broadcasted_iota(jnp.int32, (window, 2 * HEAD), 1)
        parts.append(jnp.where(lane < HEAD, pair[:window], pair[window:]))
    return jnp.concatenate(parts, axis=1)


def merge_store(ref, base, head, window):
    old = ref[pl.ds(base, TILE), :]
    row = lax.broadcasted_iota(jnp.int32, (TILE, window.shape[1]), 0)
    ref[pl.ds(base, TILE), :] = jnp.where(row >= head, window[:TILE], old)
    rest = window.shape[0] - TILE
    ref[pl.ds(base + TILE, rest), :] = window[TILE:]


def forward_kernel(
    fields, slots, width, hidden,
    counts, patches, visible, upstream,
    w_qkv, qkv_bias, w_out, b_out, w_up, b_up, w_down, b_down,
    gain_attn, shift_attn, gain_mlp, shift_mlp,
    starts, x_out, qkv_out, probs_out, att_out, mix_out, enc_out,
    g_up, g_down, g_out, gb_up, gb_down, gb_out, gg_mlp, gs_mlp,
    x_v, g_v, qkv_v, mix_v, probs_v, row_sems, probs_sems,
):
    def place(f, at):
        count = counts[f]
        head = lax.rem(at, TILE)
        at = jnp.where(head + count > slots, at + TILE - head, at)
        starts[f] = at
        return at + count

    total = lax.fori_loop(0, fields, place, 0)
    starts[fields] = total
    blocks = (total + ROWS - 1) // ROWS
    for ref in (g_up, g_down, g_out, gb_up, gb_down, gb_out, gg_mlp, gs_mlp):
        ref[...] = jnp.zeros_like(ref)

    def where_is(f):
        start = starts[f]
        head = lax.rem(start, TILE)
        return pl.multiple_of(start - head, TILE), head, counts[f]

    def pack(patch_blk, vis_blk, up_blk):
        step = pl.program_id(0)
        patch_row = lax.broadcasted_iota(jnp.int32, (patch_blk.shape[1], slots), 0)
        rows = lax.broadcasted_iota(jnp.int32, (slots, slots), 0)
        cols = lax.broadcasted_iota(jnp.int32, (slots, slots), 1)
        done = []
        for u in range(GROUP):
            base, head, count = where_is(step * GROUP + u)
            picks = pltpu.roll(vis_blk[pl.ds(u, 1), :], head, axis=1)[:, :slots]
            take = (patch_row == picks).astype(f32).astype(bf16)
            x_win = mm_tn(take, patch_blk[u]).astype(bf16)
            shift = ((rows - cols == head) & (cols < count)).astype(f32).astype(bf16)
            g_win = mm(shift, up_blk[u]).astype(bf16)
            done.append((base, head, x_win, g_win))
        for base, head, x_win, g_win in done:
            merge_store(x_v, base, head, x_win)
            merge_store(g_v, base, head, g_win)

    pltpu.emit_pipeline(
        pack,
        grid=(fields // GROUP,),
        in_specs=[
            pl.BlockSpec((GROUP,) + patches.shape[1:], lambda i: (i, 0, 0)),
            pl.BlockSpec((GROUP, visible.shape[1]), lambda i: (i, 0)),
            pl.BlockSpec((GROUP,) + upstream.shape[1:], lambda i: (i, 0, 0)),
        ],
    )(patches, visible, upstream)
    last, _, _ = where_is(fields - 1)
    tail = pl.multiple_of(last + slots, TILE)
    x_v[pl.ds(tail, ROWS), :] = jnp.zeros((ROWS, width), bf16)
    g_v[pl.ds(tail, ROWS), :] = jnp.zeros((ROWS, width), bf16)

    def block_copies(i):
        rows = pl.ds(pl.multiple_of(i * ROWS, ROWS), ROWS)
        return (
            pltpu.make_async_copy(x_v.at[rows], x_out.at[rows], row_sems.at[0, i]),
            pltpu.make_async_copy(qkv_v.at[rows], qkv_out.at[rows], row_sems.at[1, i]),
            pltpu.make_async_copy(g_v.at[rows], att_out.at[rows], row_sems.at[2, i]),
            pltpu.make_async_copy(mix_v.at[rows], mix_out.at[rows], row_sems.at[3, i]),
            pltpu.make_async_copy(x_v.at[rows], enc_out.at[rows], row_sems.at[4, i]),
        )

    def project(i, carry):
        rows = pl.ds(pl.multiple_of(i * ROWS, ROWS), ROWS)
        block_copies(i)[0].start()
        unit, _ = row_norm(x_v[rows, :].astype(f32))
        normed = (unit * gain_attn[...] + shift_attn[...]).astype(bf16)
        qkv_v[rows, :] = (mm(normed, w_qkv[...]) + qkv_bias[...]).astype(bf16)
        block_copies(i)[1].start()
        return carry

    lax.fori_loop(0, blocks, project, 0)
    edge = pl.multiple_of(blocks * ROWS, ROWS)
    qkv_v[pl.ds(edge, slots), :] = jnp.zeros((slots, 3 * width), bf16)

    def probs_copy(i):
        slot = lax.rem(i, 2)
        return pltpu.make_async_copy(
            probs_v.at[slot], probs_out.at[pl.ds(i * UNROLL, UNROLL)], probs_sems.at[slot]
        )

    def attend(i, carry):
        slot = lax.rem(i, 2)

        @pl.when(i >= 2)
        def _():
            probs_copy(i - 2).wait()

        done = []
        for u in range(UNROLL):
            base, head, count = where_is(i * UNROLL + u)
            window = pl.ds(base, slots)
            query = qkv_v[window, 0:width]
            key = qkv_v[window, width : 2 * width]
            value = qkv_v[window, 2 * width : 3 * width]
            stacked = [block_heads(query, at, size) for at, size in head_parts(width)]
            scores = heads_dot(key, stacked)
            row = lax.broadcasted_iota(jnp.int32, scores.shape, 0)
            scores = jnp.where((row >= head) & (row < head + count), scores, FILL)
            top = jnp.max(scores, axis=0, keepdims=True)
            expo = jnp.exp(scores - top)
            total_row = jnp.sum(expo, axis=0, keepdims=True)
            probs = (expo * (1.0 / total_row)).astype(bf16)
            probs_v[slot, u] = probs
            done.append((base, head, heads_out_t(probs, value).astype(bf16)))
        for base, head, mixed in done:
            merge_store(mix_v, base, head, mixed)
        probs_copy(i).start()
        return carry

    steps = fields // UNROLL
    lax.fori_loop(0, steps, attend, 0)
    probs_copy(steps - 2).wait()
    probs_copy(steps - 1).wait()
    mix_v[pl.ds(tail, ROWS), :] = jnp.zeros((ROWS, width), bf16)

    def feed(i, carry):
        rows = pl.ds(pl.multiple_of(i * ROWS, ROWS), ROWS)
        copies = block_copies(i)
        mixed = mix_v[rows, :]
        grad_b = g_v[rows, :]
        grad = grad_b.astype(f32)
        residual = x_v[rows, :].astype(f32) + (mm(mixed, w_out[...]) + b_out[...])
        unit, rstd = row_norm(residual)
        normed = (unit * gain_mlp[...] + shift_mlp[...]).astype(bf16)
        normed_t = normed.T
        grad_t = grad_b.T
        down = jnp.zeros((ROWS, width), f32)
        d_normed = jnp.zeros((ROWS, width), f32)
        for at in range(0, hidden, CHUNK):
            cols = slice(at, at + CHUNK)
            up = mm(normed, w_up[:, cols]) + b_up[:, cols]
            d_act = mm_nt(grad_b, w_down[cols, :])
            cdf = 0.5 + 0.5 * lax.erf(up * 0.7071067811865476)
            pdf = 0.3989422804014327 * jnp.exp(-0.5 * up * up)
            act = (up * cdf).astype(bf16)
            d_up_f = d_act * (cdf + up * pdf)
            d_up = d_up_f.astype(bf16)
            gb_up[:, cols] += fold(d_up_f)
            down += mm(act, w_down[cols, :])
            d_normed += mm_nt(d_up, w_up[:, cols])
            g_down[:, cols] += mm(grad_t, act)
            g_up[:, cols] += mm(normed_t, d_up)
        copies[0].wait()
        x_v[rows, :] = (residual + down + b_down[...]).astype(bf16)
        copies[4].start()
        gb_down[...] += fold(grad)
        gg_mlp[...] += fold(d_normed * unit)
        gs_mlp[...] += fold(d_normed)
        d_residual = grad + norm_back(d_normed * gain_mlp[...], unit, rstd)
        d_att = d_residual.astype(bf16)
        gb_out[...] += fold(d_residual)
        g_out[...] += mm_tn(mixed, d_att)
        g_v[rows, :] = d_att
        copies[2].start()
        mix_v[rows, :] = mm_nt(d_att, w_out[...]).astype(bf16)
        copies[3].start()
        return carry

    lax.fori_loop(0, blocks, feed, 0)

    def drain(i, carry):
        for copy in block_copies(i)[1:]:
            copy.wait()
        return carry

    lax.fori_loop(0, blocks, drain, 0)


def backward_kernel(
    fields, slots, width,
    counts, starts, visible, qkv, probs, att, mix, x_in, enc,
    w_qkv, gain_attn, shift_attn,
    encoded, input_grad, g_qkv, gb_qkv, gg_attn, gs_attn,
    qkv_v, mix_v, packed_v, din_v, probs_v, row_sems, probs_sems, enc_sem,
):
    total = starts[fields]
    blocks = (total + ROWS - 1) // ROWS
    for ref in (g_qkv, gb_qkv, gg_attn, gs_attn):
        ref[...] = jnp.zeros_like(ref)

    def where_is(f):
        start = starts[f]
        head = lax.rem(start, TILE)
        return pl.multiple_of(start - head, TILE), head, counts[f]

    def block_copies(i):
        rows = pl.ds(pl.multiple_of(i * ROWS, ROWS), ROWS)
        return (
            pltpu.make_async_copy(qkv.at[rows], qkv_v.at[rows], row_sems.at[0, i]),
            pltpu.make_async_copy(mix.at[rows], mix_v.at[rows], row_sems.at[1, i]),
        )

    def fetch(i, carry):
        for copy in block_copies(i):
            copy.start()
        return carry

    lax.fori_loop(0, blocks, fetch, 0)

    def probs_copy(i):
        slot = lax.rem(i, 2)
        return pltpu.make_async_copy(
            probs.at[pl.ds(i * UNROLL, UNROLL)], probs_v.at[slot], probs_sems.at[slot]
        )

    steps = fields // UNROLL
    probs_copy(0).start()
    edge = pl.multiple_of(blocks * ROWS, ROWS)
    qkv_v[pl.ds(edge, slots), :] = jnp.zeros((slots, 3 * width), bf16)
    mix_v[pl.ds(edge, slots), :] = jnp.zeros((slots, width), bf16)

    def arrive(i, carry):
        for copy in block_copies(i):
            copy.wait()
        return carry

    def attend(i, ready):
        slot = lax.rem(i, 2)
        base_last, _, _ = where_is(i * UNROLL + UNROLL - 1)
        need = jnp.minimum((base_last + slots - 1) // ROWS + 1, blocks)
        lax.fori_loop(ready, need, arrive, 0)

        @pl.when(i + 1 < steps)
        def _():
            probs_copy(i + 1).start()

        probs_copy(i).wait()
        done = []
        for u in range(UNROLL):
            base, head, count = where_is(i * UNROLL + u)
            window = pl.ds(base, slots)
            query = qkv_v[window, 0:width]
            key = qkv_v[window, width : 2 * width]
            value = qkv_v[window, 2 * width : 3 * width]
            grad = mix_v[window, :]
            row = lax.broadcasted_iota(jnp.int32, grad.shape, 0)
            grad = jnp.where((row >= head) & (row < head + count), grad, jnp.zeros((), bf16))
            weights_b = probs_v[slot, u]
            weights = weights_b.astype(f32)
            grad_blocks = [block_heads(grad, at, size) for at, size in head_parts(width)]
            query_blocks = [block_heads(query, at, size) for at, size in head_parts(width)]
            d_probs = heads_dot(value, grad_blocks)
            inner = jnp.sum(weights * d_probs, axis=0, keepdims=True)
            d_scores = (weights * (d_probs - inner)).astype(bf16)
            d_query = heads_out_t(d_scores, key) * (HEAD**-0.5)
            d_key = heads_out(d_scores, query_blocks)
            d_value = heads_out(weights_b, grad_blocks)
            done.append((base, head, d_query.astype(bf16), d_key.astype(bf16), d_value.astype(bf16)))
        for base, head, d_query, d_key, d_value in done:
            merge_store(packed_v.at[:, 0:width], base, head, d_query)
            merge_store(packed_v.at[:, width : 2 * width], base, head, d_key)
            merge_store(packed_v.at[:, 2 * width : 3 * width], base, head, d_value)
        return jnp.maximum(ready, need)

    ready = lax.fori_loop(0, steps, attend, 0)
    lax.fori_loop(ready, blocks, arrive, 0)
    last, _, _ = where_is(fields - 1)
    tail = pl.multiple_of(last + slots, TILE)
    packed_v[pl.ds(tail, ROWS), :] = jnp.zeros((ROWS, 3 * width), bf16)
    enc_v = mix_v

    def enc_copy(i):
        rows = pl.ds(pl.multiple_of(i * ROWS, ROWS), ROWS)
        return pltpu.make_async_copy(enc.at[rows], enc_v.at[rows], row_sems.at[2, i])

    def fetch_enc(i, carry):
        enc_copy(i).start()
        return carry

    lax.fori_loop(0, blocks, fetch_enc, 0)

    def project(x_blk, att_blk):
        i = pl.program_id(0)
        rows = pl.ds(pl.multiple_of(i * ROWS, ROWS), ROWS)
        packed = packed_v[rows, :]
        unit, rstd = row_norm(x_blk[...].astype(f32))
        normed = (unit * gain_attn[...] + shift_attn[...]).astype(bf16)
        g_qkv[...] += mm_tn(normed, packed)
        gb_qkv[...] += fold(packed.astype(f32))
        d_normed = mm_nt(packed, w_qkv[...])
        gg_attn[...] += fold(d_normed * unit)
        gs_attn[...] += fold(d_normed)
        d_in = att_blk[...].astype(f32) + norm_back(d_normed * gain_attn[...], unit, rstd)
        din_v[rows, :] = d_in.astype(bf16)

    pltpu.emit_pipeline(
        project,
        grid=(blocks,),
        in_specs=[
            pl.BlockSpec((ROWS, width), lambda i: (i, 0)),
            pl.BlockSpec((ROWS, width), lambda i: (i, 0)),
        ],
    )(x_in, att)

    def enc_arrive(i, carry):
        enc_copy(i).wait()
        return carry

    lax.fori_loop(0, blocks, enc_arrive, 0)
    din_v[pl.ds(edge, slots), :] = jnp.zeros((slots, width), bf16)
    enc_v[pl.ds(edge, slots), :] = jnp.zeros((slots, width), bf16)

    def unpack(vis_blk, enc_blk, grad_blk):
        step = pl.program_id(0)
        patch_row = lax.broadcasted_iota(jnp.int32, (grad_blk.shape[1], slots), 0)
        rows = lax.broadcasted_iota(jnp.int32, (slots, slots), 0)
        cols = lax.broadcasted_iota(jnp.int32, (slots, slots), 1)
        for u in range(GROUP):
            base, head, count = where_is(step * GROUP + u)
            window = pl.ds(base, slots)
            picks = pltpu.roll(vis_blk[pl.ds(u, 1), :], head, axis=1)[:, :slots]
            put = (patch_row == picks).astype(f32).astype(bf16)
            grad_blk[u] = mm(put, din_v[window, :]).astype(bf16)
            shift = ((cols - rows == head) & (rows < count)).astype(f32).astype(bf16)
            enc_blk[u] = mm(shift, enc_v[window, :]).astype(bf16)

    pltpu.emit_pipeline(
        unpack,
        grid=(fields // GROUP,),
        in_specs=[pl.BlockSpec((GROUP, visible.shape[1]), lambda i: (i, 0))],
        out_specs=[
            pl.BlockSpec((GROUP,) + encoded.shape[1:], lambda i: (i, 0, 0)),
            pl.BlockSpec((GROUP,) + input_grad.shape[1:], lambda i: (i, 0, 0)),
        ],
    )(visible, encoded, input_grad)


def local_block(
    patches, visible, counts, upstream, w_qkv, b_query, b_value, w_out, b_out,
    w_up, b_up, w_down, b_down, gain_attn, shift_attn, gain_mlp, shift_mlp,
):
    fields, patch_rows, width = patches.shape
    slots = visible.shape[1]
    hidden = w_up.shape[1]
    cap = (fields * slots + ROWS - 1) // ROWS * ROWS
    tall = cap + ROWS + slots
    blocks = tall // ROWS
    shape = jax.ShapeDtypeStruct
    hbm = pl.BlockSpec(memory_space=pl.ANY)
    vmem = pl.BlockSpec(memory_space=pltpu.VMEM)
    smem = pl.BlockSpec(memory_space=pltpu.SMEM)
    slot_iota = lax.broadcasted_iota(jnp.int32, visible.shape, 1)
    live_vis = jnp.where(slot_iota < counts[:, None], visible, -1)
    live_vis = jnp.pad(live_vis, ((0, 0), (0, 128 - slots)), constant_values=-1)
    scale = HEAD**-0.5
    w_scaled = jnp.concatenate([w_qkv[:, :width] * scale, w_qkv[:, width:]], axis=1)
    qkv_bias = jnp.concatenate([b_query * scale, jnp.zeros_like(b_query), b_value])
    row = lambda v: v[None, :]
    (
        starts, x_rows, qkv, probs, att, mix, enc,
        g_up, g_down, g_out, gb_up, gb_down, gb_out, gg_mlp, gs_mlp,
    ) = pl.pallas_call(
        functools.partial(forward_kernel, fields, slots, width, hidden),
        out_shape=[
            shape((fields + 1,), jnp.int32),
            shape((cap, width), bf16),
            shape((cap, 3 * width), bf16),
            shape((fields, slots, width), bf16),
            shape((cap, width), bf16),
            shape((cap, width), bf16),
            shape((cap, width), bf16),
            shape((width, hidden), f32),
            shape((width, hidden), f32),
            shape((width, width), f32),
            shape((8, hidden), f32),
            shape((8, width), f32),
            shape((8, width), f32),
            shape((8, width), f32),
            shape((8, width), f32),
        ],
        in_specs=[smem, hbm, hbm, hbm] + [vmem] * 12,
        out_specs=[smem] + [hbm] * 6 + [vmem] * 8,
        scratch_shapes=[
            pltpu.VMEM((tall, width), bf16),
            pltpu.VMEM((tall, width), bf16),
            pltpu.VMEM((cap + slots, 3 * width), bf16),
            pltpu.VMEM((tall, width), bf16),
            pltpu.VMEM((2, UNROLL, slots, width), bf16),
            pltpu.SemaphoreType.DMA((5, blocks)),
            pltpu.SemaphoreType.DMA((2,)),
        ],
        compiler_params=pltpu.CompilerParams(vmem_limit_bytes=VMEM_BYTES),
        name="forward_rows",
    )(
        counts, patches, live_vis, upstream,
        w_scaled, row(qkv_bias), w_out, row(b_out), w_up, row(b_up), w_down, row(b_down),
        row(gain_attn), row(shift_attn), row(gain_mlp), row(shift_mlp),
    )
    encoded, input_grad, g_qkv, gb_qkv, gg_attn, gs_attn = pl.pallas_call(
        functools.partial(backward_kernel, fields, slots, width),
        out_shape=[
            shape((fields, slots, width), bf16),
            shape((fields, patch_rows, width), bf16),
            shape((width, 3 * width), f32),
            shape((8, 3 * width), f32),
            shape((8, width), f32),
            shape((8, width), f32),
        ],
        in_specs=[smem, smem] + [hbm] * 7 + [vmem] * 3,
        out_specs=[hbm] * 2 + [vmem] * 4,
        scratch_shapes=[
            pltpu.VMEM((cap + slots, 3 * width), bf16),
            pltpu.VMEM((cap + slots, width), bf16),
            pltpu.VMEM((tall, 3 * width), bf16),
            pltpu.VMEM((cap + slots, width), bf16),
            pltpu.VMEM((2, UNROLL, slots, width), bf16),
            pltpu.SemaphoreType.DMA((3, blocks)),
            pltpu.SemaphoreType.DMA((2,)),
            pltpu.SemaphoreType.DMA,
        ],
        compiler_params=pltpu.CompilerParams(vmem_limit_bytes=VMEM_BYTES),
        name="backward_rows",
    )(
        counts, starts, live_vis, qkv, probs, att, mix, x_rows, enc,
        w_qkv, row(gain_attn), row(shift_attn),
    )
    return (
        encoded, input_grad, g_qkv, g_out, g_up, g_down,
        gb_qkv, gb_out, gb_up, gb_down, gg_attn, gs_attn, gg_mlp, gs_mlp,
    )


def per_device(*args):
    (
        encoded, input_grad, g_qkv, g_out, g_up, g_down,
        gb_qkv, gb_out, gb_up, gb_down, gg_attn, gs_attn, gg_mlp, gs_mlp,
    ) = local_block(*args)
    width = g_out.shape[0]
    small = [gb_qkv, gb_out, gb_up, gb_down, gg_attn, gs_attn, gg_mlp, gs_mlp]
    flat = jnp.concatenate([jnp.sum(v, axis=0) for v in small])
    g_qkv, g_out, g_up, g_down, flat = lax.psum(
        (g_qkv, g_out, g_up, g_down, flat), ("wide", "narrow")
    )
    out, at = [], 0
    for v in small:
        out.append(flat[at : at + v.shape[1]])
        at += v.shape[1]
    s_qkv, s_out, s_up, s_down, s_ga, s_sa, s_gm, s_sm = out
    return (
        encoded, input_grad, g_qkv, s_qkv[:width], s_qkv[2 * width :], g_out, s_out,
        g_up, s_up, g_down.T, s_down, s_ga, s_sa, s_gm, s_sm,
    )


def solution(mesh):
    rows = P(("wide", "narrow"))
    return jax.shard_map(
        per_device,
        mesh=mesh,
        in_specs=(rows,) * 4 + (P(),) * 13,
        out_specs=(rows,) * 2 + (P(),) * 13,
        check_vma=False,
    )
```

```python
import functools

import jax
import jax.numpy as jnp
from jax import lax
from jax.experimental import pallas as pl
from jax.experimental.pallas import tpu as pltpu
from jax.sharding import PartitionSpec as P

HEAD = 64
EPS = 1e-06
FILL = -1e30
ROWS = 512
TILE = 16
UNROLL = 8
GROUP = 8
CHUNK = 256
VMEM_BYTES = 60 * 1024 * 1024
f32 = jnp.float32
bf16 = jnp.bfloat16


LANES = 128


def mm(left, right):
    return lax.dot_general(left, right, (((1,), (0,)), ((), ())), preferred_element_type=f32)


def mm_nt(left, right):
    return lax.dot_general(left, right, (((1,), (1,)), ((), ())), preferred_element_type=f32)


def mm_tn(left, right):
    return lax.dot_general(left, right, (((0,), (0,)), ((), ())), preferred_element_type=f32)


def row_norm(values):
    width = values.shape[-1]
    mean = jnp.sum(values, axis=-1, keepdims=True) * (1.0 / width)
    centered = values - mean
    variance = jnp.sum(centered * centered, axis=-1, keepdims=True) * (1.0 / width)
    rstd = lax.rsqrt(variance + EPS)
    return centered * rstd, rstd


def norm_back(grad, unit, rstd):
    width = grad.shape[-1]
    first = jnp.sum(grad, axis=-1, keepdims=True) * (1.0 / width)
    second = jnp.sum(grad * unit, axis=-1, keepdims=True) * (1.0 / width)
    return (grad - first - unit * second) * rstd


def fold(values):
    rows, width = values.shape
    return jnp.sum(values.reshape(rows // 8, 8, width), axis=0)


def fill_mask(mask):
    row = lax.broadcasted_iota(jnp.int32, mask.shape, 0) // HEAD
    col = lax.broadcasted_iota(jnp.int32, mask.shape, 1) // HEAD
    mask[...] = (row == col).astype(f32).astype(bf16)


def head_parts(width):
    parts, at = [], 0
    while at < width:
        size = min(4 * HEAD, width - at)
        parts.append((at, size))
        at += size
    return parts


def block_heads(values, mask):
    blocks = []
    for at, size in head_parts(values.shape[1]):
        tiled = jnp.concatenate([values[:, at : at + size]] * (size // HEAD), axis=0)
        blocks.append(tiled * mask[:size, :size])
    return blocks


def heads_dot(left, stacked):
    parts = [
        mm_nt(left[:, at : at + size], block)
        for (at, size), block in zip(head_parts(left.shape[1]), stacked)
    ]
    return jnp.concatenate(parts, axis=1)


def heads_out(left, stacked):
    parts = [
        mm(left[:, at : at + size], block)
        for (at, size), block in zip(head_parts(left.shape[1]), stacked)
    ]
    return jnp.concatenate(parts, axis=1)


def heads_out_t(weights, values):
    window = weights[0].shape[0] // 2
    parts = []
    for k, at in enumerate(range(0, values.shape[1], 2 * HEAD)):
        pair = mm(weights[k], values[:, at : at + 2 * HEAD])
        lane = lax.broadcasted_iota(jnp.int32, (window, 2 * HEAD), 1)
        parts.append(jnp.where(lane < HEAD, pair[:window], pair[window:]))
    return jnp.concatenate(parts, axis=1)


def pairs_t(values):
    return [values[:, at : at + 2 * HEAD].T for at in range(0, values.shape[1], 2 * HEAD)]


def add_blocks(sums, at, values):
    rows = values.shape[0]
    for k in range(values.shape[1] // LANES):
        block = pl.ds(at + k * rows, rows)
        sums[block, :] += values[:, k * LANES : (k + 1) * LANES]


def add_vector(sums, at, partial):
    vector = jnp.sum(partial, axis=0, keepdims=True)
    for k in range(vector.shape[1] // LANES):
        sums[pl.ds(at + k, 1), :] = vector[:, k * LANES : (k + 1) * LANES]
    return at + vector.shape[1] // LANES


def merge_store(ref, base, head, window):
    old = ref[pl.ds(base, TILE), :]
    row = lax.broadcasted_iota(jnp.int32, (TILE, window.shape[1]), 0)
    ref[pl.ds(base, TILE), :] = jnp.where(row >= head, window[:TILE], old)
    rest = window.shape[0] - TILE
    ref[pl.ds(base + TILE, rest), :] = window[TILE:]


def mesh_bits(sizes):
    wide = [("wide", 1 << k) for k in range(sizes["wide"].bit_length() - 1)]
    narrow = [("narrow", 1 << k) for k in range(sizes["narrow"].bit_length() - 1)]
    return wide, narrow


def exchange_orders(sizes):
    wide, narrow = mesh_bits(sizes)
    first, last = narrow[:1], wide[-1:]
    middle = wide[:1] + narrow[1:] + wide[1:-1]
    return [first + middle[k:] + middle[:k] + last for k in range(min(3, len(middle)))]


def partner(axis, distance):
    mine = lax.axis_index(axis)
    side = lax.rem(mine // distance, 2)
    return side, {axis: mine + distance * (1 - 2 * side)}


def rows_of_parts(rows, orders):
    unit = TILE << len(orders[0])
    units, parts, at = rows // unit, [], 0
    for k in range(len(orders)):
        share = (units + len(orders) - 1 - k) // len(orders) * unit
        if share:
            parts.append((at, share))
        at += share
    return parts


class Reducer:
    def __init__(self, orders, rows, total, sent, got, summed, send_sems, recv_sems):
        self.orders, self.total, self.sent, self.got, self.summed = orders, total, sent, got, summed
        self.send_sems, self.recv_sems = send_sems, recv_sems
        self.stages = len(orders[0])
        self.parts = rows_of_parts(rows, orders)
        self.copies = []
        self.step = 0

    def greet(self):
        barrier = pltpu.get_barrier_semaphore()
        for axis, distance in self.orders[0]:
            _, other = partner(axis, distance)
            pl.semaphore_signal(barrier, inc=1, device_id=other, device_id_type=pl.DeviceIdType.MESH)
        pl.semaphore_wait(barrier, self.stages)

    def segment(self, part, stage):
        base, share = self.parts[part]
        for k in range(stage):
            side, _ = partner(*self.orders[part][k])
            base = base + side * (share >> (k + 1))
        return base, share >> stage

    def copy(self, part, stage, src, dst):
        axis, distance = self.orders[part][stage if stage < self.stages else 2 * self.stages - 1 - stage]
        _, other = partner(axis, distance)
        return pltpu.make_async_remote_copy(
            src_ref=src, dst_ref=dst,
            send_sem=self.send_sems.at[part, stage], recv_sem=self.recv_sems.at[part, stage],
            device_id=other, device_id_type=pl.DeviceIdType.MESH,
        )

    def slot(self, part, stage):
        base, share = self.parts[part]
        return pl.ds(base + share - (share >> stage), share >> (stage + 1))

    def halve(self, part, stage):
        base, size = self.segment(part, stage)
        side, _ = partner(*self.orders[part][stage])
        half = size // 2
        away = pl.ds(pl.multiple_of(base + (1 - side) * half, TILE), half)
        slot = self.slot(part, stage)
        self.sent[slot, :] = self.total[away, :].astype(bf16)
        return self.copy(part, stage, self.sent.at[slot], self.got.at[slot])

    def double(self, part, stage):
        level = 2 * self.stages - stage
        base, size = self.segment(part, level)
        here = pl.ds(pl.multiple_of(base, TILE), size)
        return self.copy(part, stage, self.summed.at[here], self.summed.at[here])

    def arrive(self, part, stage):
        self.copies[stage][part].wait()
        if stage < self.stages:
            base, size = self.segment(part, stage + 1)
            here = pl.ds(pl.multiple_of(base, TILE), size)
            value = self.total[here, :] + self.got[self.slot(part, stage), :].astype(f32)
            if stage + 1 < self.stages:
                self.total[here, :] = value
            else:
                self.summed[here, :] = value.astype(bf16)

    def advance(self):
        stage = self.step
        now = []
        for part in range(len(self.parts)):
            if stage:
                self.arrive(part, stage - 1)
            if stage < 2 * self.stages:
                copy = self.halve(part, stage) if stage < self.stages else self.double(part, stage)
                copy.start()
                now.append(copy)
        self.copies.append(now)
        self.step += 1

    @property
    def steps(self):
        return 2 * self.stages + 1


def padded_rows(rows, sizes):
    unit = TILE * sizes["wide"] * sizes["narrow"]
    return (rows + unit - 1) // unit * unit


def reducer_scratch(rows, sizes):
    orders = exchange_orders(sizes)
    flights = (len(orders), 2 * len(orders[0]))
    return [
        pltpu.VMEM((rows, LANES), bf16),
        pltpu.VMEM((rows, LANES), bf16),
        pltpu.VMEM((rows, LANES), bf16),
        pltpu.SemaphoreType.DMA(flights),
        pltpu.SemaphoreType.DMA(flights),
    ]


def sum_rows(width, hidden):
    up, out = width * hidden // LANES, width * width // LANES
    return 0, up, 2 * up, 2 * up + out


def forward_kernel(
    fields, slots, width, hidden,
    counts, patches, visible, upstream,
    w_qkv, qkv_bias, w_out, b_out, w_up, b_up, w_down, b_down,
    gain_attn, shift_attn, gain_mlp, shift_mlp,
    starts, x_out, qkv_out, probs_out, att_out, mix_out, enc_out,
    sums,
    x_v, g_v, qkv_v, mix_v, probs_v, act_v, dup_v, mask_v,
    gb_up, gb_down, gb_out, gg_mlp, gs_mlp, row_sems, probs_sems,
):
    up_at, down_at, out_at, vector_at = sum_rows(width, hidden)
    def place(f, at):
        count = counts[f]
        head = lax.rem(at, TILE)
        at = jnp.where(head + count > slots, at + TILE - head, at)
        starts[f] = at
        return at + count

    total = lax.fori_loop(0, fields, place, 0)
    starts[fields] = total
    blocks = (total + ROWS - 1) // ROWS
    for ref in (sums, gb_up, gb_down, gb_out, gg_mlp, gs_mlp):
        ref[...] = jnp.zeros_like(ref)
    fill_mask(mask_v)

    def where_is(f):
        start = starts[f]
        head = lax.rem(start, TILE)
        return pl.multiple_of(start - head, TILE), head, counts[f]

    def pack(patch_blk, vis_blk, up_blk):
        step = pl.program_id(0)
        patch_row = lax.broadcasted_iota(jnp.int32, (patch_blk.shape[1], slots), 0)
        rows = lax.broadcasted_iota(jnp.int32, (slots, slots), 0)
        cols = lax.broadcasted_iota(jnp.int32, (slots, slots), 1)
        places = [where_is(step * GROUP + u) for u in range(GROUP)]
        takes, shifts = [], []
        for u, (base, head, count) in enumerate(places):
            picks = pltpu.roll(vis_blk[pl.ds(u, 1), :], head, axis=1)[:, :slots]
            takes.append((patch_row == picks).astype(f32).astype(bf16))
            shifts.append(((rows - cols == head) & (cols < count)).astype(f32).astype(bf16))
        takes = [take.T for take in takes]
        x_wins = [mm(takes[u], patch_blk[u]).astype(bf16) for u in range(GROUP)]
        g_wins = [mm(shifts[u], up_blk[u]).astype(bf16) for u in range(GROUP)]
        for (base, head, _), x_win, g_win in zip(places, x_wins, g_wins):
            merge_store(x_v, base, head, x_win)
            merge_store(g_v, base, head, g_win)

    pltpu.emit_pipeline(
        pack,
        grid=(fields // GROUP,),
        in_specs=[
            pl.BlockSpec((GROUP,) + patches.shape[1:], lambda i: (i, 0, 0)),
            pl.BlockSpec((GROUP, visible.shape[1]), lambda i: (i, 0)),
            pl.BlockSpec((GROUP,) + upstream.shape[1:], lambda i: (i, 0, 0)),
        ],
    )(patches, visible, upstream)
    last, _, _ = where_is(fields - 1)
    tail = pl.multiple_of(last + slots, TILE)
    x_v[pl.ds(tail, ROWS), :] = jnp.zeros((ROWS, width), bf16)
    g_v[pl.ds(tail, ROWS), :] = jnp.zeros((ROWS, width), bf16)

    def block_copies(i):
        rows = pl.ds(pl.multiple_of(i * ROWS, ROWS), ROWS)
        return (
            pltpu.make_async_copy(x_v.at[rows], x_out.at[rows], row_sems.at[0, i]),
            pltpu.make_async_copy(qkv_v.at[rows], qkv_out.at[rows], row_sems.at[1, i]),
            pltpu.make_async_copy(g_v.at[rows], att_out.at[rows], row_sems.at[2, i]),
            pltpu.make_async_copy(mix_v.at[rows], mix_out.at[rows], row_sems.at[3, i]),
            pltpu.make_async_copy(x_v.at[rows], enc_out.at[rows], row_sems.at[4, i]),
        )

    def project(i, carry):
        rows = pl.ds(pl.multiple_of(i * ROWS, ROWS), ROWS)
        block_copies(i)[0].start()
        unit, _ = row_norm(x_v[rows, :].astype(f32))
        normed = (unit * gain_attn[...] + shift_attn[...]).astype(bf16)
        qkv_v[rows, :] = (mm(normed, w_qkv[...]) + qkv_bias[...]).astype(bf16)
        block_copies(i)[1].start()
        return carry

    lax.fori_loop(0, blocks, project, 0)
    edge = pl.multiple_of(blocks * ROWS, ROWS)
    qkv_v[pl.ds(edge, slots), :] = jnp.zeros((slots, 3 * width), bf16)

    def probs_copy(i):
        slot = lax.rem(i, 2)
        return pltpu.make_async_copy(
            probs_v.at[slot], probs_out.at[pl.ds(i * UNROLL, UNROLL)], probs_sems.at[slot]
        )

    def attend(i, carry):
        slot = lax.rem(i, 2)

        @pl.when(i >= 2)
        def _():
            probs_copy(i - 2).wait()

        places = [where_is(i * UNROLL + u) for u in range(UNROLL)]
        windows = [pl.ds(base, slots) for base, _, _ in places]
        scores = []
        for window in windows:
            stacked = block_heads(qkv_v[window, 0:width], mask_v)
            scores.append(heads_dot(qkv_v[window, width : 2 * width], stacked))
        weights = []
        for (_, head, count), score in zip(places, scores):
            row = lax.broadcasted_iota(jnp.int32, score.shape, 0)
            score = jnp.where((row >= head) & (row < head + count), score, FILL)
            expo = jnp.exp(score - jnp.max(score, axis=0, keepdims=True))
            total_row = jnp.sum(expo, axis=0, keepdims=True)
            weights.append((expo * (1.0 / total_row)).astype(bf16))
        for u, weight in enumerate(weights):
            probs_v[slot, u] = weight
        turned = [pairs_t(weight) for weight in weights]
        mixed = [
            heads_out_t(weight, qkv_v[window, 2 * width : 3 * width]).astype(bf16)
            for weight, window in zip(turned, windows)
        ]
        for (base, head, _), out in zip(places, mixed):
            merge_store(mix_v, base, head, out)
        probs_copy(i).start()
        return carry

    steps = fields // UNROLL
    lax.fori_loop(0, steps, attend, 0)
    probs_copy(steps - 2).wait()
    probs_copy(steps - 1).wait()
    mix_v[pl.ds(tail, ROWS), :] = jnp.zeros((ROWS, width), bf16)

    def feed(i, carry):
        rows = pl.ds(pl.multiple_of(i * ROWS, ROWS), ROWS)
        copies = block_copies(i)
        mixed = mix_v[rows, :]
        grad_b = g_v[rows, :]
        grad = grad_b.astype(f32)
        residual = x_v[rows, :].astype(f32) + (mm(mixed, w_out[...]) + b_out[...])
        unit, rstd = row_norm(residual)
        normed = (unit * gain_mlp[...] + shift_mlp[...]).astype(bf16)
        normed_t = normed.T
        grad_t = grad_b.T
        for at in range(0, hidden, CHUNK):
            cols = slice(at, at + CHUNK)
            up = mm(normed, w_up[:, cols]) + b_up[:, cols]
            d_act = mm_nt(grad_b, w_down[cols, :])
            cdf = 0.5 + 0.5 * lax.erf(up * 0.7071067811865476)
            pdf = 0.3989422804014327 * jnp.exp(-0.5 * up * up)
            act_v[:, cols] = (up * cdf).astype(bf16)
            d_up = d_act * (cdf + up * pdf)
            dup_v[:, cols] = d_up.astype(bf16)
            gb_up[:, cols] += fold(d_up)
        down = mm(act_v[...], w_down[...])
        d_normed = mm_nt(dup_v[...], w_up[...])
        add_blocks(sums, up_at, mm(normed_t, dup_v[...]))
        add_blocks(sums, down_at, mm(grad_t, act_v[...]))
        copies[0].wait()
        x_v[rows, :] = (residual + down + b_down[...]).astype(bf16)
        copies[4].start()
        gb_down[...] += fold(grad)
        gg_mlp[...] += fold(d_normed * unit)
        gs_mlp[...] += fold(d_normed)
        d_residual = grad + norm_back(d_normed * gain_mlp[...], unit, rstd)
        d_att = d_residual.astype(bf16)
        gb_out[...] += fold(d_residual)
        add_blocks(sums, out_at, mm_tn(mixed, d_att))
        g_v[rows, :] = d_att
        copies[2].start()
        mix_v[rows, :] = mm_nt(d_att, w_out[...]).astype(bf16)
        copies[3].start()
        return carry

    lax.fori_loop(0, blocks, feed, 0)
    at = vector_at
    for partial in (gb_up, gb_down, gb_out, gg_mlp, gs_mlp):
        at = add_vector(sums, at, partial[...])

    def drain(i, carry):
        for copy in block_copies(i)[1:]:
            copy.wait()
        return carry

    lax.fori_loop(0, blocks, drain, 0)


def backward_kernel(
    fields, slots, width,
    counts, starts, visible, qkv, probs, att, mix, x_in, enc,
    w_qkv, gain_attn, shift_attn,
    encoded, input_grad, sums,
    gb_qkv, gg_attn, gs_attn, qkv_v, mix_v, packed_v, din_v, probs_v, mask_v, row_sems, probs_sems,
):
    fill_mask(mask_v)
    total = starts[fields]
    blocks = (total + ROWS - 1) // ROWS
    for ref in (sums, gb_qkv, gg_attn, gs_attn):
        ref[...] = jnp.zeros_like(ref)

    def where_is(f):
        start = starts[f]
        head = lax.rem(start, TILE)
        return pl.multiple_of(start - head, TILE), head, counts[f]

    def block_copies(i):
        rows = pl.ds(pl.multiple_of(i * ROWS, ROWS), ROWS)
        return (
            pltpu.make_async_copy(qkv.at[rows], qkv_v.at[rows], row_sems.at[0, i]),
            pltpu.make_async_copy(mix.at[rows], mix_v.at[rows], row_sems.at[1, i]),
        )

    def fetch(i, carry):
        for copy in block_copies(i):
            copy.start()
        return carry

    lax.fori_loop(0, blocks, fetch, 0)

    def probs_copy(i):
        slot = lax.rem(i, 2)
        return pltpu.make_async_copy(
            probs.at[pl.ds(i * UNROLL, UNROLL)], probs_v.at[slot], probs_sems.at[slot]
        )

    steps = fields // UNROLL
    probs_copy(0).start()
    edge = pl.multiple_of(blocks * ROWS, ROWS)
    qkv_v[pl.ds(edge, slots), :] = jnp.zeros((slots, 3 * width), bf16)
    mix_v[pl.ds(edge, slots), :] = jnp.zeros((slots, width), bf16)

    def arrive(i, carry):
        for copy in block_copies(i):
            copy.wait()
        return carry

    def attend(i, ready):
        slot = lax.rem(i, 2)
        base_last, _, _ = where_is(i * UNROLL + UNROLL - 1)
        need = jnp.minimum((base_last + slots - 1) // ROWS + 1, blocks)
        lax.fori_loop(ready, need, arrive, 0)

        @pl.when(i + 1 < steps)
        def _():
            probs_copy(i + 1).start()

        probs_copy(i).wait()
        places = [where_is(i * UNROLL + u) for u in range(UNROLL)]
        windows = [pl.ds(base, slots) for base, _, _ in places]
        grads = []
        for (_, head, count), window in zip(places, windows):
            row = lax.broadcasted_iota(jnp.int32, (slots, width), 0)
            live = ((row >= head) & (row < head + count)).astype(f32).astype(bf16)
            grads.append(block_heads(mix_v[window, :] * live, mask_v))
        d_probs = [
            heads_dot(qkv_v[window, 2 * width : 3 * width], grad)
            for window, grad in zip(windows, grads)
        ]
        d_values = [
            heads_out(probs_v[slot, u], grad).astype(bf16) for u, grad in enumerate(grads)
        ]
        d_scores = []
        for u, d_prob in enumerate(d_probs):
            weights = probs_v[slot, u].astype(f32)
            weighted = weights * d_prob
            inner = jnp.sum(weighted, axis=0, keepdims=True)
            d_scores.append((weighted - weights * inner).astype(bf16))
        d_keys = [
            heads_out(d_score, block_heads(qkv_v[window, 0:width], mask_v)).astype(bf16)
            for window, d_score in zip(windows, d_scores)
        ]
        turned = [pairs_t(d_score) for d_score in d_scores]
        d_queries = [
            (heads_out_t(d_score, qkv_v[window, width : 2 * width]) * (HEAD**-0.5)).astype(bf16)
            for window, d_score in zip(windows, turned)
        ]
        for u, (base, head, _) in enumerate(places):
            merge_store(packed_v.at[:, 0:width], base, head, d_queries[u])
            merge_store(packed_v.at[:, width : 2 * width], base, head, d_keys[u])
            merge_store(packed_v.at[:, 2 * width : 3 * width], base, head, d_values[u])
        return jnp.maximum(ready, need)

    ready = lax.fori_loop(0, steps, attend, 0)
    lax.fori_loop(ready, blocks, arrive, 0)
    last, _, _ = where_is(fields - 1)
    tail = pl.multiple_of(last + slots, TILE)
    packed_v[pl.ds(tail, ROWS), :] = jnp.zeros((ROWS, 3 * width), bf16)
    enc_v = mix_v

    def enc_copy(i):
        rows = pl.ds(pl.multiple_of(i * ROWS, ROWS), ROWS)
        return pltpu.make_async_copy(enc.at[rows], enc_v.at[rows], row_sems.at[2, i])

    def fetch_enc(i, carry):
        enc_copy(i).start()
        return carry

    lax.fori_loop(0, blocks, fetch_enc, 0)

    def project(x_blk, att_blk):
        i = pl.program_id(0)
        rows = pl.ds(pl.multiple_of(i * ROWS, ROWS), ROWS)
        packed = packed_v[rows, :]
        unit, rstd = row_norm(x_blk[...].astype(f32))
        normed = (unit * gain_attn[...] + shift_attn[...]).astype(bf16)
        add_blocks(sums, 0, mm_tn(normed, packed))
        gb_qkv[...] += fold(packed.astype(f32))
        d_normed = mm_nt(packed, w_qkv[...])
        gg_attn[...] += fold(d_normed * unit)
        gs_attn[...] += fold(d_normed)
        d_in = att_blk[...].astype(f32) + norm_back(d_normed * gain_attn[...], unit, rstd)
        din_v[rows, :] = d_in.astype(bf16)

    pltpu.emit_pipeline(
        project,
        grid=(blocks,),
        in_specs=[
            pl.BlockSpec((ROWS, width), lambda i: (i, 0)),
            pl.BlockSpec((ROWS, width), lambda i: (i, 0)),
        ],
    )(x_in, att)

    at = 3 * width * width // LANES
    for partial in (gb_qkv, gg_attn, gs_attn):
        at = add_vector(sums, at, partial[...])

    def enc_arrive(i, carry):
        enc_copy(i).wait()
        return carry

    lax.fori_loop(0, blocks, enc_arrive, 0)
    din_v[pl.ds(edge, slots), :] = jnp.zeros((slots, width), bf16)
    enc_v[pl.ds(edge, slots), :] = jnp.zeros((slots, width), bf16)

    def unpack(vis_blk, enc_blk, grad_blk):
        step = pl.program_id(0)
        patch_row = lax.broadcasted_iota(jnp.int32, (grad_blk.shape[1], slots), 0)
        rows = lax.broadcasted_iota(jnp.int32, (slots, slots), 0)
        cols = lax.broadcasted_iota(jnp.int32, (slots, slots), 1)
        places = [where_is(step * GROUP + u) for u in range(GROUP)]
        puts, shifts = [], []
        for u, (base, head, count) in enumerate(places):
            picks = pltpu.roll(vis_blk[pl.ds(u, 1), :], head, axis=1)[:, :slots]
            puts.append((patch_row == picks).astype(f32).astype(bf16))
            shifts.append(((cols - rows == head) & (rows < count)).astype(f32).astype(bf16))
        for u, (base, _, _) in enumerate(places):
            grad_blk[u] = mm(puts[u], din_v[pl.ds(base, slots), :]).astype(bf16)
            enc_blk[u] = mm(shifts[u], enc_v[pl.ds(base, slots), :]).astype(bf16)

    pltpu.emit_pipeline(
        unpack,
        grid=(fields // GROUP,),
        in_specs=[pl.BlockSpec((GROUP, visible.shape[1]), lambda i: (i, 0))],
        out_specs=[
            pl.BlockSpec((GROUP,) + encoded.shape[1:], lambda i: (i, 0, 0)),
            pl.BlockSpec((GROUP,) + input_grad.shape[1:], lambda i: (i, 0, 0)),
        ],
    )(visible, encoded, input_grad)


def local_block(
    sizes,
    patches, visible, counts, upstream, w_qkv, b_query, b_value, w_out, b_out,
    w_up, b_up, w_down, b_down, gain_attn, shift_attn, gain_mlp, shift_mlp,
):
    fields, patch_rows, width = patches.shape
    slots = visible.shape[1]
    hidden = w_up.shape[1]
    cap = (fields * slots + ROWS - 1) // ROWS * ROWS
    tall = cap + ROWS + slots
    blocks = tall // ROWS
    shape = jax.ShapeDtypeStruct
    hbm = pl.BlockSpec(memory_space=pl.ANY)
    vmem = pl.BlockSpec(memory_space=pltpu.VMEM)
    smem = pl.BlockSpec(memory_space=pltpu.SMEM)
    slot_iota = lax.broadcasted_iota(jnp.int32, visible.shape, 1)
    live_vis = jnp.where(slot_iota < counts[:, None], visible, -1)
    live_vis = jnp.pad(live_vis, ((0, 0), (0, 128 - slots)), constant_values=-1)
    scale = HEAD**-0.5
    w_scaled = jnp.concatenate([w_qkv[:, :width] * scale, w_qkv[:, width:]], axis=1)
    qkv_bias = jnp.concatenate([b_query * scale, jnp.zeros_like(b_query), b_value])
    row = lambda v: v[None, :]
    (
        starts, x_rows, qkv, probs, att, mix, enc, sums,
    ) = pl.pallas_call(
        functools.partial(forward_kernel, fields, slots, width, hidden),
        out_shape=[
            shape((fields + 1,), jnp.int32),
            shape((cap, width), bf16),
            shape((cap, 3 * width), bf16),
            shape((fields, slots, width), bf16),
            shape((cap, width), bf16),
            shape((cap, width), bf16),
            shape((cap, width), bf16),
            shape((padded_rows(sum_rows(width, hidden)[3] + (hidden + 4 * width) // LANES, sizes), LANES), f32),
        ],
        in_specs=[smem, hbm, hbm, hbm] + [vmem] * 12,
        out_specs=[smem] + [hbm] * 6 + [vmem],
        scratch_shapes=[
            pltpu.VMEM((tall, width), bf16),
            pltpu.VMEM((tall, width), bf16),
            pltpu.VMEM((cap + slots, 3 * width), bf16),
            pltpu.VMEM((tall, width), bf16),
            pltpu.VMEM((2, UNROLL, slots, width), bf16),
            pltpu.VMEM((ROWS, hidden), bf16),
            pltpu.VMEM((ROWS, hidden), bf16),
            pltpu.VMEM((4 * HEAD, 4 * HEAD), bf16),
            pltpu.VMEM((8, hidden), f32),
            pltpu.VMEM((8, width), f32),
            pltpu.VMEM((8, width), f32),
            pltpu.VMEM((8, width), f32),
            pltpu.VMEM((8, width), f32),
            pltpu.SemaphoreType.DMA((5, blocks)),
            pltpu.SemaphoreType.DMA((2,)),
        ],
        compiler_params=pltpu.CompilerParams(vmem_limit_bytes=VMEM_BYTES),
        name="forward_rows",
    )(
        counts, patches, live_vis, upstream,
        w_scaled, row(qkv_bias), w_out, row(b_out), w_up, row(b_up), w_down, row(b_down),
        row(gain_attn), row(shift_attn), row(gain_mlp), row(shift_mlp),
    )
    encoded, input_grad, sums_b = pl.pallas_call(
        functools.partial(backward_kernel, fields, slots, width),
        out_shape=[
            shape((fields, slots, width), bf16),
            shape((fields, patch_rows, width), bf16),
            shape((padded_rows((3 * width * width + 5 * width) // LANES, sizes), LANES), f32),
        ],
        in_specs=[smem, smem] + [hbm] * 7 + [vmem] * 3,
        out_specs=[hbm] * 2 + [vmem],
        scratch_shapes=[
            pltpu.VMEM((8, 3 * width), f32),
            pltpu.VMEM((8, width), f32),
            pltpu.VMEM((8, width), f32),
            pltpu.VMEM((cap + slots, 3 * width), bf16),
            pltpu.VMEM((cap + slots, width), bf16),
            pltpu.VMEM((tall, 3 * width), bf16),
            pltpu.VMEM((cap + slots, width), bf16),
            pltpu.VMEM((2, UNROLL, slots, width), bf16),
            pltpu.VMEM((4 * HEAD, 4 * HEAD), bf16),
            pltpu.SemaphoreType.DMA((3, blocks)),
            pltpu.SemaphoreType.DMA((2,)),
        ],
        compiler_params=pltpu.CompilerParams(vmem_limit_bytes=VMEM_BYTES),
        name="backward_rows",
    )(
        counts, starts, live_vis, qkv, probs, att, mix, x_rows, enc,
        w_qkv, row(gain_attn), row(shift_attn),
    )
    return encoded, input_grad, sums, sums_b


def sum_kernel(
    orders, rows_a, rows_b, sums_a, sums_b, out_a, out_b, total_a, total_b,
    sent_a, got_a, summed_a, send_a, recv_a, sent_b, got_b, summed_b, send_b, recv_b,
):
    first = Reducer(orders, rows_a, total_a, sent_a, got_a, summed_a, send_a, recv_a)
    second = Reducer(orders, rows_b, total_b, sent_b, got_b, summed_b, send_b, recv_b)
    first.greet()
    total_a[...] = sums_a[...]
    total_b[...] = sums_b[...]
    for _ in range(first.steps):
        first.advance()
        second.advance()
    out_a[...] = summed_a[...]
    out_b[...] = summed_b[...]


def add_up(sizes, sums_a, sums_b):
    rows_a, rows_b = sums_a.shape[0], sums_b.shape[0]
    return pl.pallas_call(
        functools.partial(sum_kernel, exchange_orders(sizes), rows_a, rows_b),
        out_shape=[jax.ShapeDtypeStruct(v.shape, bf16) for v in (sums_a, sums_b)],
        scratch_shapes=[pltpu.VMEM(sums_a.shape, f32), pltpu.VMEM(sums_b.shape, f32)]
        + reducer_scratch(rows_a, sizes)
        + reducer_scratch(rows_b, sizes),
        compiler_params=pltpu.CompilerParams(
            collective_id=0, has_side_effects=True, vmem_limit_bytes=VMEM_BYTES
        ),
        name="sum_rows",
    )(sums_a, sums_b)


def unblock(blocked, at, rows, columns):
    part = blocked[at : at + rows * columns // LANES].astype(f32)
    return part.reshape(columns // LANES, rows, LANES).transpose(1, 0, 2).reshape(rows, columns)


def per_device(sizes, *args):
    encoded, input_grad, sums_a, sums_b = local_block(sizes, *args)
    total_a, total_b = add_up(sizes, sums_a, sums_b)
    width, hidden = args[9].shape
    up_at, down_at, out_at, vector_at = sum_rows(width, hidden)
    first = total_a[vector_at:].astype(f32).reshape(-1)
    second = total_b[3 * width * width // LANES :].astype(f32).reshape(-1)

    def take(flat, at, count):
        return flat[at : at + count]

    return (
        encoded, input_grad,
        unblock(total_b, 0, width, 3 * width), take(second, 0, width), take(second, 2 * width, width),
        unblock(total_a, out_at, width, width), take(first, hidden + width, width),
        unblock(total_a, up_at, width, hidden), take(first, 0, hidden),
        unblock(total_a, down_at, width, hidden).T, take(first, hidden, width),
        take(second, 3 * width, width), take(second, 4 * width, width),
        take(first, hidden + 2 * width, width), take(first, hidden + 3 * width, width),
    )


def solution(mesh):
    rows = P(("wide", "narrow"))
    return jax.shard_map(
        functools.partial(per_device, dict(mesh.shape)),
        mesh=mesh,
        in_specs=(rows,) * 4 + (P(),) * 13,
        out_specs=(rows,) * 2 + (P(),) * 13,
        check_vma=False,
    )
```

```python
import functools

import jax
import jax.numpy as jnp
from jax import lax
from jax.experimental import pallas as pl
from jax.experimental.pallas import tpu as pltpu
from jax.sharding import PartitionSpec as P

HEAD = 64
EPS = 1e-06
FILL = -1e30
ROWS = 512
TILE = 16
UNROLL = 8
GROUP = 8
CHUNK = 256
VMEM_BYTES = 60 * 1024 * 1024
f32 = jnp.float32
bf16 = jnp.bfloat16


LANES = 128


def mm(left, right):
    return lax.dot_general(left, right, (((1,), (0,)), ((), ())), preferred_element_type=f32)


def mm_nt(left, right):
    return lax.dot_general(left, right, (((1,), (1,)), ((), ())), preferred_element_type=f32)


def mm_tn(left, right):
    return lax.dot_general(left, right, (((0,), (0,)), ((), ())), preferred_element_type=f32)


def row_norm(values):
    width = values.shape[-1]
    mean = jnp.sum(values, axis=-1, keepdims=True) * (1.0 / width)
    centered = values - mean
    variance = jnp.sum(centered * centered, axis=-1, keepdims=True) * (1.0 / width)
    rstd = lax.rsqrt(variance + EPS)
    return centered * rstd, rstd


def norm_back(grad, unit, rstd):
    width = grad.shape[-1]
    first = jnp.sum(grad, axis=-1, keepdims=True) * (1.0 / width)
    second = jnp.sum(grad * unit, axis=-1, keepdims=True) * (1.0 / width)
    return (grad - first - unit * second) * rstd


def fold(values):
    rows, width = values.shape
    return jnp.sum(values.reshape(rows // 8, 8, width), axis=0)


def fill_mask(mask):
    row = lax.broadcasted_iota(jnp.int32, mask.shape, 0) // HEAD
    col = lax.broadcasted_iota(jnp.int32, mask.shape, 1) // HEAD
    mask[...] = (row == col).astype(f32).astype(bf16)


def head_parts(width):
    parts, at = [], 0
    while at < width:
        size = min(4 * HEAD, width - at)
        parts.append((at, size))
        at += size
    return parts


def block_heads(values, mask):
    blocks = []
    for at, size in head_parts(values.shape[1]):
        tiled = jnp.concatenate([values[:, at : at + size]] * (size // HEAD), axis=0)
        blocks.append(tiled * mask[:size, :size])
    return blocks


def heads_dot(left, stacked):
    parts = [
        mm_nt(left[:, at : at + size], block)
        for (at, size), block in zip(head_parts(left.shape[1]), stacked)
    ]
    return jnp.concatenate(parts, axis=1)


def heads_out(left, stacked):
    parts = [
        mm(left[:, at : at + size], block)
        for (at, size), block in zip(head_parts(left.shape[1]), stacked)
    ]
    return jnp.concatenate(parts, axis=1)


def heads_out_t(weights, values):
    window = weights[0].shape[0] // 2
    parts = []
    for k, at in enumerate(range(0, values.shape[1], 2 * HEAD)):
        pair = mm(weights[k], values[:, at : at + 2 * HEAD])
        lane = lax.broadcasted_iota(jnp.int32, (window, 2 * HEAD), 1)
        parts.append(jnp.where(lane < HEAD, pair[:window], pair[window:]))
    return jnp.concatenate(parts, axis=1)


def pairs_t(values):
    return [values[:, at : at + 2 * HEAD].T for at in range(0, values.shape[1], 2 * HEAD)]


def add_blocks(sums, at, values):
    rows = values.shape[0]
    for k in range(values.shape[1] // LANES):
        block = pl.ds(at + k * rows, rows)
        sums[block, :] += values[:, k * LANES : (k + 1) * LANES]


def add_vector(sums, at, partial):
    vector = jnp.sum(partial, axis=0, keepdims=True)
    for k in range(vector.shape[1] // LANES):
        sums[pl.ds(at + k, 1), :] = vector[:, k * LANES : (k + 1) * LANES]
    return at + vector.shape[1] // LANES


def row(ref, cols=slice(None)):
    return ref[cols].reshape(1, -1)


def shifted_picks(vis, head, count):
    slots = vis.shape[1]
    lane = lax.broadcasted_iota(jnp.int32, vis.shape, 1)
    live = jnp.where(lane < count, vis, -1)
    wide = jnp.concatenate([live, jnp.full((1, LANES - slots), -1, jnp.int32)], axis=1)
    return pltpu.roll(wide, head, axis=1)[:, :slots]


def merge_store(ref, base, head, window):
    old = ref[pl.ds(base, TILE), :]
    row = lax.broadcasted_iota(jnp.int32, (TILE, window.shape[1]), 0)
    ref[pl.ds(base, TILE), :] = jnp.where(row >= head, window[:TILE], old)
    rest = window.shape[0] - TILE
    ref[pl.ds(base + TILE, rest), :] = window[TILE:]


def mesh_bits(sizes):
    wide = [("wide", 1 << k) for k in range(sizes["wide"].bit_length() - 1)]
    narrow = [("narrow", 1 << k) for k in range(sizes["narrow"].bit_length() - 1)]
    return wide, narrow


def exchange_orders(sizes):
    wide, narrow = mesh_bits(sizes)
    first, last = narrow[:1], wide[-1:]
    middle = wide[:1] + narrow[1:] + wide[1:-1]
    return [first + middle[k:] + middle[:k] + last for k in range(min(3, len(middle)))]


def partner(axis, distance):
    mine = lax.axis_index(axis)
    side = lax.rem(mine // distance, 2)
    return side, {axis: mine + distance * (1 - 2 * side)}


def rows_of_parts(rows, orders):
    unit = TILE << len(orders[0])
    units, parts, at = rows // unit, [], 0
    for k in range(len(orders)):
        share = (units + len(orders) - 1 - k) // len(orders) * unit
        if share:
            parts.append((at, share))
        at += share
    return parts


class Reducer:
    def __init__(self, orders, rows, total, sent, got, summed, send_sems, recv_sems):
        self.orders, self.total, self.sent, self.got, self.summed = orders, total, sent, got, summed
        self.send_sems, self.recv_sems = send_sems, recv_sems
        self.stages = len(orders[0])
        self.parts = rows_of_parts(rows, orders)

    def greet(self):
        barrier = pltpu.get_barrier_semaphore()
        for axis, distance in self.orders[0]:
            _, other = partner(axis, distance)
            pl.semaphore_signal(barrier, inc=1, device_id=other, device_id_type=pl.DeviceIdType.MESH)
        pl.semaphore_wait(barrier, self.stages)

    def segment(self, part, stage):
        base, share = self.parts[part]
        for k in range(stage):
            side, _ = partner(*self.orders[part][k])
            base = base + side * (share >> (k + 1))
        return base, share >> stage

    def copy(self, part, stage, src, dst):
        axis, distance = self.orders[part][stage if stage < self.stages else 2 * self.stages - 1 - stage]
        _, other = partner(axis, distance)
        return pltpu.make_async_remote_copy(
            src_ref=src, dst_ref=dst,
            send_sem=self.send_sems.at[part, stage], recv_sem=self.recv_sems.at[part, stage],
            device_id=other, device_id_type=pl.DeviceIdType.MESH,
        )

    def slot(self, part, stage):
        base, share = self.parts[part]
        return pl.ds(base + share - (share >> stage), share >> (stage + 1))

    def flight(self, part, stage):
        if stage < self.stages:
            slot = self.slot(part, stage)
            return self.copy(part, stage, self.sent.at[slot], self.got.at[slot])
        level = 2 * self.stages - stage
        base, size = self.segment(part, level)
        here = pl.ds(pl.multiple_of(base, TILE), size)
        return self.copy(part, stage, self.summed.at[here], self.summed.at[here])

    def leave(self, part, stage):
        if stage < self.stages:
            base, size = self.segment(part, stage)
            side, _ = partner(*self.orders[part][stage])
            half = size // 2
            away = pl.ds(pl.multiple_of(base + (1 - side) * half, TILE), half)
            self.sent[self.slot(part, stage), :] = self.total[away, :].astype(bf16)
        self.flight(part, stage).start()

    def arrive(self, part, stage):
        self.flight(part, stage).wait()
        if stage < self.stages:
            base, size = self.segment(part, stage + 1)
            here = pl.ds(pl.multiple_of(base, TILE), size)
            value = self.total[here, :] + self.got[self.slot(part, stage), :].astype(f32)
            if stage + 1 < self.stages:
                self.total[here, :] = value
            else:
                self.summed[here, :] = value.astype(bf16)

    def advance(self, stage):
        for part in range(len(self.parts)):
            if stage:
                self.arrive(part, stage - 1)
            if stage < 2 * self.stages:
                self.leave(part, stage)

    @property
    def steps(self):
        return 2 * self.stages + 1


def padded_rows(rows, sizes):
    unit = TILE * sizes["wide"] * sizes["narrow"]
    return (rows + unit - 1) // unit * unit


def reducer_scratch(rows, sizes):
    orders = exchange_orders(sizes)
    flights = (len(orders), 2 * len(orders[0]))
    return [
        pltpu.VMEM((rows, LANES), bf16),
        pltpu.VMEM((rows, LANES), bf16),
        pltpu.VMEM((rows, LANES), bf16),
        pltpu.SemaphoreType.DMA(flights),
        pltpu.SemaphoreType.DMA(flights),
    ]


def sum_rows(width, hidden):
    up, out = width * hidden // LANES, width * width // LANES
    return 0, up, 2 * up, 2 * up + out


def forward_kernel(
    fields, slots, width, hidden,
    counts, patches, visible, upstream,
    w_qkv, b_query, b_value, w_out, b_out, w_up, b_up, w_down, b_down,
    gain_attn, shift_attn, gain_mlp, shift_mlp,
    starts, x_out, qkv_out, probs_out, att_out, mix_out, enc_out, sums,
    x_v, g_v, qkv_v, mix_v, probs_v, act_v, dup_v, mask_v,
    gb_up, gb_down, gb_out, gg_mlp, gs_mlp, window_sems, probs_sems,
):
    up_at, down_at, out_at, vector_at = sum_rows(width, hidden)
    def place(f, at):
        count = counts[f]
        head = lax.rem(at, TILE)
        at = jnp.where(head + count > slots, at + TILE - head, at)
        starts[f] = at
        return at + count

    lax.fori_loop(0, fields, place, 0)
    last = starts[fields - 1]
    tail = pl.multiple_of(last - lax.rem(last, TILE) + slots, TILE)
    blocks = (tail + ROWS - 1) // ROWS
    for ref in (sums, gb_up, gb_down, gb_out, gg_mlp, gs_mlp):
        ref[...] = jnp.zeros_like(ref)
    fill_mask(mask_v)

    def where_is(f):
        start = starts[f]
        head = lax.rem(start, TILE)
        return pl.multiple_of(start - head, TILE), head, counts[f]

    def pack(patch_blk, vis_blk, up_blk, x_blk):
        step = pl.program_id(0)
        patch_row = lax.broadcasted_iota(jnp.int32, (patch_blk.shape[1], slots), 0)
        rows = lax.broadcasted_iota(jnp.int32, (slots, slots), 0)
        cols = lax.broadcasted_iota(jnp.int32, (slots, slots), 1)
        places = [where_is(step * GROUP + u) for u in range(GROUP)]
        takes, shifts = [], []
        for u, (base, head, count) in enumerate(places):
            picks = shifted_picks(vis_blk[pl.ds(u, 1), :], head, count)
            takes.append((patch_row == picks).astype(f32).astype(bf16))
            shifts.append(((rows - cols == head) & (cols < count)).astype(f32).astype(bf16))
        takes = [take.T for take in takes]
        x_wins = [mm(takes[u], patch_blk[u]).astype(bf16) for u in range(GROUP)]
        g_wins = [mm(shifts[u], up_blk[u]).astype(bf16) for u in range(GROUP)]
        for u, x_win in enumerate(x_wins):
            x_blk[u] = x_win
        for (base, head, _), x_win, g_win in zip(places, x_wins, g_wins):
            merge_store(x_v, base, head, x_win)
            merge_store(g_v, base, head, g_win)

    pltpu.emit_pipeline(
        pack,
        grid=(fields // GROUP,),
        in_specs=[
            pl.BlockSpec((GROUP,) + patches.shape[1:], lambda i: (i, 0, 0)),
            pl.BlockSpec((GROUP, visible.shape[1]), lambda i: (i, 0)),
            pl.BlockSpec((GROUP,) + upstream.shape[1:], lambda i: (i, 0, 0)),
        ],
        out_specs=[pl.BlockSpec((GROUP, slots, width), lambda i: (i, 0, 0))],
    )(patches, visible, upstream, x_out)
    x_v[pl.ds(tail, ROWS), :] = jnp.zeros((ROWS, width), bf16)
    g_v[pl.ds(tail, ROWS), :] = jnp.zeros((ROWS, width), bf16)

    def window_copy(f, src, dst, kind):
        base, _, _ = where_is(f)
        return pltpu.make_async_copy(src.at[pl.ds(base, slots)], dst.at[f], window_sems.at[kind])

    def project(i, carry):
        rows = pl.ds(pl.multiple_of(i * ROWS, ROWS), ROWS)
        unit, _ = row_norm(x_v[rows, :].astype(f32))
        normed = (unit * row(gain_attn) + row(shift_attn)).astype(bf16)
        third = [slice(k * width, (k + 1) * width) for k in range(3)]
        query = mm(normed, w_qkv[:, third[0]]) + row(b_query)
        qkv_v[rows, third[0]] = (query * HEAD**-0.5).astype(bf16)
        qkv_v[rows, third[1]] = mm(normed, w_qkv[:, third[1]]).astype(bf16)
        qkv_v[rows, third[2]] = (mm(normed, w_qkv[:, third[2]]) + row(b_value)).astype(bf16)
        return carry

    lax.fori_loop(0, blocks, project, 0)

    def probs_copy(i):
        slot = lax.rem(i, 2)
        return pltpu.make_async_copy(
            probs_v.at[slot], probs_out.at[pl.ds(i * UNROLL, UNROLL)], probs_sems.at[slot]
        )

    def attend(i, carry):
        slot = lax.rem(i, 2)

        @pl.when(i >= 2)
        def _():
            probs_copy(i - 2).wait()

        for u in range(UNROLL):
            window_copy(i * UNROLL + u, qkv_v, qkv_out, 0).start()
        places = [where_is(i * UNROLL + u) for u in range(UNROLL)]
        windows = [pl.ds(base, slots) for base, _, _ in places]
        scores = []
        for window in windows:
            stacked = block_heads(qkv_v[window, 0:width], mask_v)
            scores.append(heads_dot(qkv_v[window, width : 2 * width], stacked))
        weights = []
        for (_, head, count), score in zip(places, scores):
            slot_row = lax.broadcasted_iota(jnp.int32, score.shape, 0)
            live = (slot_row >= head) & (slot_row < head + count)
            score = jnp.where(live, score, FILL)
            expo = jnp.exp(score - jnp.max(score, axis=0, keepdims=True))
            total_row = jnp.sum(expo, axis=0, keepdims=True)
            weights.append((expo * (1.0 / total_row)).astype(bf16))
        for u, weight in enumerate(weights):
            probs_v[slot, u] = weight
        turned = [pairs_t(weight) for weight in weights]
        mixed = [
            heads_out_t(weight, qkv_v[window, 2 * width : 3 * width]).astype(bf16)
            for weight, window in zip(turned, windows)
        ]
        for (base, head, _), out in zip(places, mixed):
            merge_store(mix_v, base, head, out)
        probs_copy(i).start()
        return carry

    steps = fields // UNROLL
    lax.fori_loop(0, steps, attend, 0)
    probs_copy(steps - 2).wait()
    probs_copy(steps - 1).wait()
    mix_v[pl.ds(tail, ROWS), :] = jnp.zeros((ROWS, width), bf16)

    def feed(i, sent):
        rows = pl.ds(pl.multiple_of(i * ROWS, ROWS), ROWS)
        mixed = mix_v[rows, :]
        grad_b = g_v[rows, :]
        grad = grad_b.astype(f32)
        residual = x_v[rows, :].astype(f32) + (mm(mixed, w_out[...]) + row(b_out))
        unit, rstd = row_norm(residual)
        normed = (unit * row(gain_mlp) + row(shift_mlp)).astype(bf16)
        normed_t = normed.T
        grad_t = grad_b.T
        for at in range(0, hidden, CHUNK):
            cols = slice(at, at + CHUNK)
            up = mm(normed, w_up[:, cols]) + row(b_up, cols)
            d_act = mm_nt(grad_b, w_down[cols, :])
            cdf = 0.5 + 0.5 * lax.erf(up * 0.7071067811865476)
            pdf = 0.3989422804014327 * jnp.exp(-0.5 * up * up)
            act_v[:, cols] = (up * cdf).astype(bf16)
            d_up = d_act * (cdf + up * pdf)
            dup_v[:, cols] = d_up.astype(bf16)
            gb_up[:, cols] += fold(d_up)
        down = mm(act_v[...], w_down[...])
        d_normed = mm_nt(dup_v[...], w_up[...])
        add_blocks(sums, up_at, mm(normed_t, dup_v[...]))
        add_blocks(sums, down_at, mm(grad_t, act_v[...]))
        x_v[rows, :] = (residual + down + row(b_down)).astype(bf16)
        gb_down[...] += fold(grad)
        gg_mlp[...] += fold(d_normed * unit)
        gs_mlp[...] += fold(d_normed)
        d_residual = grad + norm_back(d_normed * row(gain_mlp), unit, rstd)
        d_att = d_residual.astype(bf16)
        gb_out[...] += fold(d_residual)
        add_blocks(sums, out_at, mm_tn(mixed, d_att))
        g_v[rows, :] = d_att
        mix_v[rows, :] = mm_nt(d_att, w_out[...]).astype(bf16)

        def finished(f):
            base, _, _ = where_is(jnp.minimum(f, fields - 1))
            return (f < fields) & (base + slots <= (i + 1) * ROWS)

        def send(f):
            window_copy(f, g_v, att_out, 1).start()
            window_copy(f, mix_v, mix_out, 2).start()
            window_copy(f, x_v, enc_out, 3).start()
            return f + 1

        return lax.while_loop(finished, send, sent)

    lax.fori_loop(0, blocks, feed, 0)
    at = vector_at
    for partial in (gb_up, gb_down, gb_out, gg_mlp, gs_mlp):
        at = add_vector(sums, at, partial[...])

    for kind, ref in enumerate((qkv_out, att_out, mix_out, enc_out)):
        pltpu.make_async_copy(ref, ref, window_sems.at[kind]).wait()


FIRST_IN_ATTEND = (1, 3, 6, 9, 11, 13, 15)
FIRST_IN_PROJECT = (1, 4, 8, 12)
SECOND_IN_PROJECT = (0, 2, 5, 9, 13)


def backward_kernel(
    orders, fields, slots, width,
    counts, starts, qkv, probs, mix, att, x_in, sums_a, w_qkv, gain_attn, shift_attn,
    d_in, packed, out_a, out_b,
    mask_v, gb_qkv, total_a, total_b, load_sem, store_sems,
    sent_a, got_a, summed_a, send_a, recv_a, sent_b, got_b, summed_b, send_b, recv_b,
):
    first = Reducer(orders, total_a.shape[0], total_a, sent_a, got_a, summed_a, send_a, recv_a)
    second = Reducer(orders, total_b.shape[0], total_b, sent_b, got_b, summed_b, send_b, recv_b)
    load = pltpu.make_async_copy(sums_a, total_a, load_sem)
    load.start()
    first.greet()
    fill_mask(mask_v)
    total_b[...] = jnp.zeros_like(total_b)
    gb_qkv[...] = jnp.zeros_like(gb_qkv)
    load.wait()
    steps = fields // UNROLL
    rows = UNROLL * slots

    def at_step(step, reducer, ahead, begin):
        for k, when in enumerate(ahead):

            @pl.when(step == when)
            def _(k=k):
                reducer.advance(begin + k)

    def attend(qkv_b, probs_b, mix_b, x_b, packed_b):
        step = pl.program_id(0)
        at_step(step, first, FIRST_IN_ATTEND, 0)
        grads = []
        for u in range(UNROLL):
            f = step * UNROLL + u
            head = lax.rem(starts[f], TILE)
            slot_row = lax.broadcasted_iota(jnp.int32, (slots, width), 0)
            live = (slot_row >= head) & (slot_row < head + counts[f])
            grads.append(block_heads(mix_b[u] * live.astype(f32).astype(bf16), mask_v))
        d_probs = [heads_dot(qkv_b[u, :, 2 * width :], grads[u]) for u in range(UNROLL)]
        for u in range(UNROLL):
            packed_b[u, :, 2 * width :] = heads_out(probs_b[u], grads[u]).astype(bf16)
        d_scores = []
        for u in range(UNROLL):
            weights = probs_b[u].astype(f32)
            weighted = weights * d_probs[u]
            inner = jnp.sum(weighted, axis=0, keepdims=True)
            d_scores.append((weighted - weights * inner).astype(bf16))
        for u in range(UNROLL):
            query = block_heads(qkv_b[u, :, :width], mask_v)
            packed_b[u, :, width : 2 * width] = heads_out(d_scores[u], query).astype(bf16)
        turned = [pairs_t(d_score) for d_score in d_scores]
        for u in range(UNROLL):
            d_query = heads_out_t(turned[u], qkv_b[u, :, width : 2 * width])
            packed_b[u, :, :width] = (d_query * HEAD**-0.5).astype(bf16)
        unit, _ = row_norm(x_b[...].reshape(rows, width).astype(f32))
        grad = packed_b[...].reshape(rows, 3 * width)
        add_blocks(total_b, 0, mm_tn(unit.astype(bf16), grad))
        gb_qkv[...] += fold(grad.astype(f32))

    def block(*shape):
        return pl.BlockSpec((UNROLL,) + shape, lambda i: (i, 0, 0))

    pltpu.emit_pipeline(
        attend,
        grid=(steps,),
        in_specs=[block(slots, 3 * width), block(slots, width), block(slots, width), block(slots, width)],
        out_specs=[block(slots, 3 * width)],
    )(qkv, probs, mix, x_in, packed)

    at = 3 * width * width // LANES
    add_vector(total_b, at, gb_qkv[...])
    grad_sum = jnp.sum(gb_qkv[...], axis=0, keepdims=True)
    gain = jnp.broadcast_to(row(gain_attn), (LANES, width)).T
    shift = jnp.broadcast_to(row(shift_attn), (LANES, width)).T
    gain_sum = jnp.zeros((width, LANES), f32)
    shift_sum = jnp.zeros((width, LANES), f32)
    for k in range(3 * width // LANES):
        here = pl.ds(k * width, width)
        cols = slice(k * LANES, (k + 1) * LANES)
        weight = w_qkv[:, cols].astype(f32)
        part = total_b[here, :]
        column = jnp.broadcast_to(grad_sum[:, cols], (width, LANES))
        gain_sum += weight * part
        shift_sum += weight * column
        total_b[here, :] = gain * part + shift * column
    at += 3 * width // LANES
    at = add_vector(total_b, at, gain_sum.T)
    add_vector(total_b, at, shift_sum.T)

    def project(packed_b, x_b, att_b, d_in_b):
        step = pl.program_id(0)
        at_step(step, second, SECOND_IN_PROJECT, 0)
        at_step(step, first, FIRST_IN_PROJECT, len(FIRST_IN_ATTEND))
        unit, rstd = row_norm(x_b[...].reshape(rows, width).astype(f32))
        d_normed = mm_nt(packed_b[...].reshape(rows, 3 * width), w_qkv[...])
        d_x = norm_back(d_normed * row(gain_attn), unit, rstd)
        d_x = att_b[...].reshape(rows, width).astype(f32) + d_x
        d_in_b[...] = d_x.astype(bf16).reshape(UNROLL, slots, width)

    pltpu.emit_pipeline(
        project,
        grid=(steps,),
        in_specs=[block(slots, 3 * width), block(slots, width), block(slots, width)],
        out_specs=[block(slots, width)],
    )(packed, x_in, att, d_in)

    for k in range(len(FIRST_IN_ATTEND) + len(FIRST_IN_PROJECT), first.steps):
        first.advance(k)
    store_a = pltpu.make_async_copy(summed_a, out_a, store_sems.at[0])
    store_a.start()
    for k in range(len(SECOND_IN_PROJECT), second.steps):
        second.advance(k)
    store_b = pltpu.make_async_copy(summed_b, out_b, store_sems.at[1])
    store_b.start()
    store_a.wait()
    store_b.wait()


def unblock(src, at, dst):
    rows, columns = dst.shape
    for k in range(columns // LANES):
        dst[:, k * LANES : (k + 1) * LANES] = src[pl.ds(at + k * rows, rows), :].astype(f32)


def unblock_t(src, at, dst):
    rows, columns = dst.shape
    for k in range(rows // LANES):
        part = src[pl.ds(at + k * columns, columns), :].astype(f32)
        dst[k * LANES : (k + 1) * LANES, :] = part.T


def unblock_vector(src, at, dst):
    (columns,) = dst.shape
    for k in range(columns // LANES):
        dst[k * LANES : (k + 1) * LANES] = src[pl.ds(at + k, 1), :].astype(f32).reshape(LANES)


def unpack_kernel(
    fields, slots, width, hidden,
    counts, starts, visible, d_in, enc, sums_a, sums_b,
    encoded, input_grad, w_qkv, b_query, b_value, w_out, b_out, w_up, b_up, w_down, b_down,
    gain_attn, shift_attn, gain_mlp, shift_mlp,
    qkv_v, up_v, down_v, sems,
):
    up_at, down_at, out_at, at = sum_rows(width, hidden)
    unblock(sums_a, up_at, up_v)
    copies = [pltpu.make_async_copy(up_v, w_up, sems.at[0])]
    copies[0].start()
    unblock_t(sums_a, down_at, down_v)
    copies.append(pltpu.make_async_copy(down_v, w_down, sems.at[1]))
    copies[1].start()
    unblock(sums_b, 0, qkv_v)
    copies.append(pltpu.make_async_copy(qkv_v, w_qkv, sems.at[2]))
    copies[2].start()
    unblock(sums_a, out_at, w_out)
    for ref in (b_up, b_down, b_out, gain_mlp, shift_mlp):
        unblock_vector(sums_a, at, ref)
        at += ref.shape[0] // LANES
    at = 3 * width * width // LANES
    for ref, rows in ((b_query, 2), (b_value, 1), (gain_attn, 1), (shift_attn, 1)):
        unblock_vector(sums_b, at, ref)
        at += rows * width // LANES

    def unpack(vis_blk, d_in_b, enc_b, enc_blk, grad_blk):
        step = pl.program_id(0)
        patch_row = lax.broadcasted_iota(jnp.int32, (grad_blk.shape[1], slots), 0)
        rows = lax.broadcasted_iota(jnp.int32, (slots, slots), 0)
        cols = lax.broadcasted_iota(jnp.int32, (slots, slots), 1)
        puts, shifts = [], []
        for u in range(GROUP):
            f = step * GROUP + u
            head, count = lax.rem(starts[f], TILE), counts[f]
            picks = shifted_picks(vis_blk[pl.ds(u, 1), :], head, count)
            puts.append((patch_row == picks).astype(f32).astype(bf16))
            shifts.append(((cols - rows == head) & (rows < count)).astype(f32).astype(bf16))
        for u in range(GROUP):
            grad_blk[u] = mm(puts[u], d_in_b[u]).astype(bf16)
            enc_blk[u] = mm(shifts[u], enc_b[u]).astype(bf16)

    def block(*shape):
        return pl.BlockSpec((GROUP,) + shape, lambda i: (i, 0, 0))

    pltpu.emit_pipeline(
        unpack,
        grid=(fields // GROUP,),
        in_specs=[
            pl.BlockSpec((GROUP, visible.shape[1]), lambda i: (i, 0)),
            block(slots, width),
            block(slots, width),
        ],
        out_specs=[block(*encoded.shape[1:]), block(*input_grad.shape[1:])],
    )(visible, d_in, enc, encoded, input_grad)
    for copy in copies:
        copy.wait()


def forward(sizes, args):
    (
        patches, visible, counts, upstream, w_qkv, b_query, b_value, w_out, b_out,
        w_up, b_up, w_down, b_down, gain_attn, shift_attn, gain_mlp, shift_mlp,
    ) = args
    fields, _, width = patches.shape
    slots, hidden = visible.shape[1], w_up.shape[1]
    cap = (fields * slots + ROWS - 1) // ROWS * ROWS
    tall = cap + ROWS
    vectors = (hidden + 4 * width) // LANES
    rows_a = padded_rows(sum_rows(width, hidden)[3] + vectors, sizes)
    shape = jax.ShapeDtypeStruct
    hbm = pl.BlockSpec(memory_space=pl.ANY)
    vmem = pl.BlockSpec(memory_space=pltpu.VMEM)
    smem = pl.BlockSpec(memory_space=pltpu.SMEM)
    windows = shape((fields, slots, width), bf16)
    return pl.pallas_call(
        functools.partial(forward_kernel, fields, slots, width, hidden),
        out_shape=[
            shape((fields,), jnp.int32),
            windows,
            shape((fields, slots, 3 * width), bf16),
            windows,
            windows,
            windows,
            windows,
            shape((rows_a, LANES), f32),
        ],
        in_specs=[smem, hbm, hbm, hbm] + [vmem] * 13,
        out_specs=[smem] + [hbm] * 6 + [vmem],
        scratch_shapes=[
            pltpu.VMEM((tall, width), bf16),
            pltpu.VMEM((tall, width), bf16),
            pltpu.VMEM((cap, 3 * width), bf16),
            pltpu.VMEM((tall, width), bf16),
            pltpu.VMEM((2, UNROLL, slots, width), bf16),
            pltpu.VMEM((ROWS, hidden), bf16),
            pltpu.VMEM((ROWS, hidden), bf16),
            pltpu.VMEM((4 * HEAD, 4 * HEAD), bf16),
            pltpu.VMEM((8, hidden), f32),
            pltpu.VMEM((8, width), f32),
            pltpu.VMEM((8, width), f32),
            pltpu.VMEM((8, width), f32),
            pltpu.VMEM((8, width), f32),
            pltpu.SemaphoreType.DMA((4,)),
            pltpu.SemaphoreType.DMA((2,)),
        ],
        compiler_params=pltpu.CompilerParams(vmem_limit_bytes=VMEM_BYTES),
        name="forward_rows",
    )(
        counts, patches, visible, upstream, w_qkv, b_query, b_value, w_out, b_out,
        w_up, b_up, w_down, b_down, gain_attn, shift_attn, gain_mlp, shift_mlp,
    )


def backward(sizes, counts, starts, qkv, probs, mix, att, x_rows, sums_a, w_qkv, gain, shift):
    fields, slots, width = mix.shape
    rows_b = padded_rows((3 * width * width + 5 * width) // LANES, sizes)
    shape = jax.ShapeDtypeStruct
    hbm = pl.BlockSpec(memory_space=pl.ANY)
    vmem = pl.BlockSpec(memory_space=pltpu.VMEM)
    smem = pl.BlockSpec(memory_space=pltpu.SMEM)
    return pl.pallas_call(
        functools.partial(backward_kernel, exchange_orders(sizes), fields, slots, width),
        out_shape=[
            shape(mix.shape, bf16),
            shape(qkv.shape, bf16),
            shape(sums_a.shape, bf16),
            shape((rows_b, LANES), bf16),
        ],
        in_specs=[smem, smem] + [hbm] * 6 + [vmem] * 3,
        out_specs=[hbm] * 4,
        scratch_shapes=[
            pltpu.VMEM((4 * HEAD, 4 * HEAD), bf16),
            pltpu.VMEM((8, 3 * width), f32),
            pltpu.VMEM(sums_a.shape, f32),
            pltpu.VMEM((rows_b, LANES), f32),
            pltpu.SemaphoreType.DMA,
            pltpu.SemaphoreType.DMA((2,)),
        ]
        + reducer_scratch(sums_a.shape[0], sizes)
        + reducer_scratch(rows_b, sizes),
        compiler_params=pltpu.CompilerParams(
            collective_id=0, has_side_effects=True, vmem_limit_bytes=VMEM_BYTES
        ),
        name="backward_rows",
    )(counts, starts, qkv, probs, mix, att, x_rows, sums_a, w_qkv, gain, shift)


def unpack_all(counts, starts, visible, d_in, enc, sums_a, sums_b, patch_rows, hidden):
    fields, slots, width = d_in.shape
    shape = jax.ShapeDtypeStruct
    hbm = pl.BlockSpec(memory_space=pl.ANY)
    vmem = pl.BlockSpec(memory_space=pltpu.VMEM)
    smem = pl.BlockSpec(memory_space=pltpu.SMEM)
    vector = shape((width,), f32)
    return pl.pallas_call(
        functools.partial(unpack_kernel, fields, slots, width, hidden),
        out_shape=[
            shape((fields, slots, width), bf16),
            shape((fields, patch_rows, width), bf16),
            shape((width, 3 * width), f32), vector, vector,
            shape((width, width), f32), vector,
            shape((width, hidden), f32), shape((hidden,), f32),
            shape((hidden, width), f32), vector,
            vector, vector, vector, vector,
        ],
        in_specs=[smem, smem] + [hbm] * 3 + [vmem] * 2,
        out_specs=[hbm] * 3 + [vmem] * 4 + [hbm, vmem, hbm] + [vmem] * 5,
        scratch_shapes=[
            pltpu.VMEM((width, 3 * width), f32),
            pltpu.VMEM((width, hidden), f32),
            pltpu.VMEM((hidden, width), f32),
            pltpu.SemaphoreType.DMA((3,)),
        ],
        compiler_params=pltpu.CompilerParams(vmem_limit_bytes=VMEM_BYTES),
        name="unpack_rows",
    )(counts, starts, visible, d_in, enc, sums_a, sums_b)


def per_device(sizes, *args):
    patches, visible, counts = args[:3]
    w_qkv, w_up, gain_attn, shift_attn = args[4], args[9], args[13], args[14]
    starts, x_rows, qkv, probs, att, mix, enc, sums_a = forward(sizes, args)
    d_in, _, total_a, total_b = backward(
        sizes, counts, starts, qkv, probs, mix, att, x_rows, sums_a, w_qkv, gain_attn, shift_attn
    )
    return tuple(
        unpack_all(
            counts, starts, visible, d_in, enc, total_a, total_b, patches.shape[1], w_up.shape[1]
        )
    )


def solution(mesh):
    rows = P(("wide", "narrow"))
    return jax.shard_map(
        functools.partial(per_device, dict(mesh.shape)),
        mesh=mesh,
        in_specs=(rows,) * 4 + (P(),) * 13,
        out_specs=(rows,) * 2 + (P(),) * 13,
        check_vma=False,
    )
```

```python
import functools

import jax
import jax.numpy as jnp
from jax import lax
from jax.experimental import pallas as pl
from jax.experimental.pallas import tpu as pltpu
from jax.sharding import PartitionSpec as P

HEAD = 64
EPS = 1e-06
FILL = -1e30
ROWS = 512
TILE = 16
UNROLL = 8
AHEAD = 16
GROUP = 8
BATCH = 16
PART = 256
SPLIT = 2
CHUNK = 256
VMEM_BYTES = 60 * 1024 * 1024
f32 = jnp.float32
bf16 = jnp.bfloat16


LANES = 128


def mm(left, right):
    return lax.dot_general(left, right, (((1,), (0,)), ((), ())), preferred_element_type=f32)


def mm_nt(left, right):
    return lax.dot_general(left, right, (((1,), (1,)), ((), ())), preferred_element_type=f32)


def mm_tn(left, right):
    return lax.dot_general(left, right, (((0,), (0,)), ((), ())), preferred_element_type=f32)


def row_norm(values):
    width = values.shape[-1]
    mean = jnp.sum(values, axis=-1, keepdims=True) * (1.0 / width)
    centered = values - mean
    variance = jnp.sum(centered * centered, axis=-1, keepdims=True) * (1.0 / width)
    rstd = lax.rsqrt(variance + EPS)
    return centered * rstd, rstd


def norm_back(grad, unit, rstd):
    width = grad.shape[-1]
    first = jnp.sum(grad, axis=-1, keepdims=True) * (1.0 / width)
    second = jnp.sum(grad * unit, axis=-1, keepdims=True) * (1.0 / width)
    return (grad - first - unit * second) * rstd


def fold(values):
    rows, width = values.shape
    return jnp.sum(values.reshape(rows // 8, 8, width), axis=0)


def fill_mask(mask):
    row = lax.broadcasted_iota(jnp.int32, mask.shape, 0) // HEAD
    col = lax.broadcasted_iota(jnp.int32, mask.shape, 1) // HEAD
    mask[...] = (row == col).astype(f32).astype(bf16)


def head_parts(width):
    parts, at = [], 0
    while at < width:
        size = min(4 * HEAD, width - at)
        parts.append((at, size))
        at += size
    return parts


def block_heads(values, mask):
    blocks = []
    for at, size in head_parts(values.shape[1]):
        tiled = jnp.concatenate([values[:, at : at + size]] * (size // HEAD), axis=0)
        blocks.append(tiled * mask[:size, :size])
    return blocks


def heads_dot(left, stacked):
    parts = [
        mm_nt(left[:, at : at + size], block)
        for (at, size), block in zip(head_parts(left.shape[1]), stacked)
    ]
    return jnp.concatenate(parts, axis=1)


def heads_out(left, stacked):
    parts = [
        mm(left[:, at : at + size], block)
        for (at, size), block in zip(head_parts(left.shape[1]), stacked)
    ]
    return jnp.concatenate(parts, axis=1)


def heads_out_t(weights, values):
    window = weights[0].shape[0] // 2
    parts = []
    for k, at in enumerate(range(0, values.shape[1], 2 * HEAD)):
        pair = mm(weights[k], values[:, at : at + 2 * HEAD])
        lane = lax.broadcasted_iota(jnp.int32, (window, 2 * HEAD), 1)
        parts.append(jnp.where(lane < HEAD, pair[:window], pair[window:]))
    return jnp.concatenate(parts, axis=1)


def pairs_t(values):
    return [values[:, at : at + 2 * HEAD].T for at in range(0, values.shape[1], 2 * HEAD)]


def add_blocks(sums, at, values):
    rows = values.shape[0]
    for k in range(values.shape[1] // LANES):
        block = pl.ds(at + k * rows, rows)
        sums[block, :] += values[:, k * LANES : (k + 1) * LANES]


def add_vector(sums, at, partial):
    vector = jnp.sum(partial, axis=0, keepdims=True)
    for k in range(vector.shape[1] // LANES):
        sums[pl.ds(at + k, 1), :] = vector[:, k * LANES : (k + 1) * LANES]
    return at + vector.shape[1] // LANES


def row(ref, cols=slice(None)):
    return ref[cols].reshape(1, -1)


def shifted_picks(vis, head, count):
    slots = vis.shape[1]
    lane = lax.broadcasted_iota(jnp.int32, vis.shape, 1)
    live = jnp.where(lane < count, vis, -1)
    wide = jnp.concatenate([live, jnp.full((1, LANES - slots), -1, jnp.int32)], axis=1)
    return pltpu.roll(wide, head, axis=1)[:, :slots]


def merge_store(ref, base, head, window):
    old = ref[pl.ds(base, TILE), :]
    row = lax.broadcasted_iota(jnp.int32, (TILE, window.shape[1]), 0)
    ref[pl.ds(base, TILE), :] = jnp.where(row >= head, window[:TILE], old)
    rest = window.shape[0] - TILE
    ref[pl.ds(base + TILE, rest), :] = window[TILE:]


def mesh_bits(sizes):
    wide = [("wide", 1 << k) for k in range(sizes["wide"].bit_length() - 1)]
    narrow = [("narrow", 1 << k) for k in range(sizes["narrow"].bit_length() - 1)]
    return wide, narrow


def exchange_orders(sizes):
    wide, narrow = mesh_bits(sizes)
    first, last = narrow[:1], wide[-1:]
    middle = wide[:1] + narrow[1:] + wide[1:-1]
    return [first + middle[k:] + middle[:k] + last for k in range(min(3, len(middle)))]


def partner(axis, distance):
    mine = lax.axis_index(axis)
    side = lax.rem(mine // distance, 2)
    return side, {axis: mine + distance * (1 - 2 * side)}


def rows_of_parts(rows, orders):
    unit = TILE << len(orders[0])
    units, parts, at = rows // unit, [], 0
    for k in range(len(orders)):
        share = (units + len(orders) - 1 - k) // len(orders) * unit
        if share:
            parts.append((at, share))
        at += share
    return parts


class Reducer:
    def __init__(self, orders, rows, total, sent, got, summed, send_sems, recv_sems):
        self.orders, self.total, self.sent, self.got, self.summed = orders, total, sent, got, summed
        self.send_sems, self.recv_sems = send_sems, recv_sems
        self.stages = len(orders[0])
        self.parts = rows_of_parts(rows, orders)
        self.partners = {pair: partner(*pair) for pair in orders[0]}
        self.bases = []
        for order, (base, share) in zip(orders, self.parts):
            bases = [base]
            for k, pair in enumerate(order):
                bases.append(bases[-1] + self.partners[pair][0] * (share >> (k + 1)))
            self.bases.append(bases)

    def greet(self):
        barrier = pltpu.get_barrier_semaphore()
        for axis, distance in self.orders[0]:
            _, other = self.partners[axis, distance]
            pl.semaphore_signal(barrier, inc=1, device_id=other, device_id_type=pl.DeviceIdType.MESH)
        pl.semaphore_wait(barrier, self.stages)

    def segment(self, part, stage):
        return self.bases[part][stage], self.parts[part][1] >> stage

    def copy(self, part, stage, src, dst):
        axis, distance = self.orders[part][stage if stage < self.stages else 2 * self.stages - 1 - stage]
        _, other = self.partners[axis, distance]
        return pltpu.make_async_remote_copy(
            src_ref=src, dst_ref=dst,
            send_sem=self.send_sems.at[part, stage], recv_sem=self.recv_sems.at[part, stage],
            device_id=other, device_id_type=pl.DeviceIdType.MESH,
        )

    def slot(self, part, stage):
        base, share = self.parts[part]
        return pl.ds(base + share - (share >> stage), share >> (stage + 1))

    def flight(self, part, stage):
        if stage < self.stages:
            slot = self.slot(part, stage)
            return self.copy(part, stage, self.sent.at[slot], self.got.at[slot])
        level = 2 * self.stages - stage
        base, size = self.segment(part, level)
        here = pl.ds(pl.multiple_of(base, TILE), size)
        return self.copy(part, stage, self.summed.at[here], self.summed.at[here])

    def leave(self, part, stage):
        if stage < self.stages:
            base, size = self.segment(part, stage)
            side, _ = self.partners[self.orders[part][stage]]
            half = size // 2
            away = pl.ds(pl.multiple_of(base + (1 - side) * half, TILE), half)
            self.sent[self.slot(part, stage), :] = self.total[away, :].astype(bf16)
        self.flight(part, stage).start()

    def arrive(self, part, stage):
        self.flight(part, stage).wait()
        if stage < self.stages:
            base, size = self.segment(part, stage + 1)
            here = pl.ds(pl.multiple_of(base, TILE), size)
            value = self.total[here, :] + self.got[self.slot(part, stage), :].astype(f32)
            if stage + 1 < self.stages:
                self.total[here, :] = value
            else:
                self.summed[here, :] = value.astype(bf16)

    def advance(self, stage):
        for part in range(len(self.parts)):
            if stage:
                self.arrive(part, stage - 1)
            if stage < 2 * self.stages:
                self.leave(part, stage)

    @property
    def steps(self):
        return 2 * self.stages + 1


def padded_rows(rows, sizes):
    unit = TILE * sizes["wide"] * sizes["narrow"]
    return (rows + unit - 1) // unit * unit


def reducer_scratch(rows, sizes):
    orders = exchange_orders(sizes)
    flights = (len(orders), 2 * len(orders[0]))
    return [
        pltpu.VMEM((rows, LANES), bf16),
        pltpu.VMEM((rows, LANES), bf16),
        pltpu.VMEM((rows, LANES), bf16),
        pltpu.SemaphoreType.DMA(flights),
        pltpu.SemaphoreType.DMA(flights),
    ]


def sum_rows(width, hidden):
    up, out = width * hidden // LANES, width * width // LANES
    return 0, up, 2 * up, 2 * up + out


def forward_kernel(
    fields, slots, width, hidden,
    counts, patches, visible, upstream,
    w_qkv, b_query, b_value, w_out, b_out, w_up, b_up, w_down, b_down,
    gain_attn, shift_attn, gain_mlp, shift_mlp,
    starts, x_out, unit_out, qkv_out, probs_out, att_out, mix_out, base_out, act_out, sums,
    x_v, g_v, qkv_v, mix_v, probs_v, act_v, dup_v, mask_v,
    gb_up, gb_down, gb_out, gg_mlp, gs_mlp, window_sems, probs_sems, land_sems,
    act_sems, base_sems,
):
    up_at, down_at, out_at, vector_at = sum_rows(width, hidden)
    patch_rows = patches.shape[0] // fields
    steps = fields // BATCH
    landing = qkv_v.shape[0] // (BATCH * patch_rows)
    cut = [slice(k * width, (k + 1) * width) for k in range(3)]

    def arrivals(third, step):
        size = BATCH * patch_rows
        src = pl.ds(pl.multiple_of(step * size, size), size)
        dst = pl.ds(pl.multiple_of((step - third * landing) * size, size), size)
        size = BATCH * slots
        up = pl.ds(pl.multiple_of(step * size, size), size)
        return (
            pltpu.make_async_copy(patches.at[src], qkv_v.at[dst, cut[third]], land_sems.at[0, step]),
            pltpu.make_async_copy(upstream.at[up], qkv_v.at[up, cut[2]], land_sems.at[1, step]),
        )

    def start_arrivals(third, step, carry):
        for copy in arrivals(third, step):
            copy.start()
        return carry

    for third in range(steps // landing):
        lax.fori_loop(
            third * landing, (third + 1) * landing, functools.partial(start_arrivals, third), 0
        )

    def place(f, at):
        count = counts[f]
        head = lax.rem(at, TILE)
        at = jnp.where(head + count > slots, at + TILE - head, at)
        starts[f] = at
        return at + count

    lax.fori_loop(0, fields, place, 0)
    last = starts[fields - 1]
    tail = pl.multiple_of(last - lax.rem(last, TILE) + slots, TILE)
    blocks = (tail + ROWS - 1) // ROWS
    for ref in (sums, gb_up, gb_down, gb_out, gg_mlp, gs_mlp):
        ref[...] = jnp.zeros_like(ref)
    fill_mask(mask_v)

    def where_is(f):
        start = starts[f]
        head = lax.rem(start, TILE)
        return pl.multiple_of(start - head, TILE), head, counts[f]

    def pack(third, step, carry):
        for copy in arrivals(third, step):
            copy.wait()
        patch_row = lax.broadcasted_iota(jnp.int32, (patch_rows, slots), 0)
        rows = lax.broadcasted_iota(jnp.int32, (slots, slots), 0)
        cols = lax.broadcasted_iota(jnp.int32, (slots, slots), 1)
        places = [where_is(step * BATCH + u) for u in range(BATCH)]
        takes, shifts = [], []
        for u, (base, head, count) in enumerate(places):
            picks = shifted_picks(visible[pl.ds(step * BATCH + u, 1), :], head, count)
            takes.append((patch_row == picks).astype(f32).astype(bf16))
            shifts.append(((rows - cols == head) & (cols < count)).astype(f32).astype(bf16))
        takes = [take.T for take in takes]
        x_wins, g_wins = [], []
        for u in range(BATCH):
            at = (step - third * landing) * BATCH + u
            field = qkv_v[pl.ds(pl.multiple_of(at * patch_rows, patch_rows), patch_rows), cut[third]]
            x_wins.append(mm(takes[u], field).astype(bf16))
        for u in range(BATCH):
            at = step * BATCH + u
            field = qkv_v[pl.ds(pl.multiple_of(at * slots, slots), slots), cut[2]]
            g_wins.append(mm(shifts[u], field).astype(bf16))
        for (base, head, _), x_win, g_win in zip(places, x_wins, g_wins):
            merge_store(x_v, base, head, x_win)
            merge_store(g_v, base, head, g_win)
        return carry

    for third in range(steps // landing):
        lax.fori_loop(third * landing, (third + 1) * landing, functools.partial(pack, third), 0)
    x_v[pl.ds(tail, ROWS), :] = jnp.zeros((ROWS, width), bf16)
    g_v[pl.ds(tail, ROWS), :] = jnp.zeros((ROWS, width), bf16)

    def window_copy(f, src, dst, kind):
        base, _, _ = where_is(f)
        return pltpu.make_async_copy(src.at[pl.ds(base, slots)], dst.at[f], window_sems.at[kind])

    def finished(i, f):
        base, _, _ = where_is(jnp.minimum(f, fields - 1))
        return (f < fields) & (base + slots <= (i + 1) * ROWS)

    def project(i, sent):
        rows = pl.ds(pl.multiple_of(i * ROWS, ROWS), ROWS)
        unit, _ = row_norm(x_v[rows, :].astype(f32))
        mix_v[rows, :] = unit.astype(bf16)
        normed = (unit * row(gain_attn) + row(shift_attn)).astype(bf16)
        query = mm(normed, w_qkv[:, cut[0]]) + row(b_query)
        qkv_v[rows, cut[0]] = (query * HEAD**-0.5).astype(bf16)
        qkv_v[rows, cut[1]] = mm(normed, w_qkv[:, cut[1]]).astype(bf16)
        qkv_v[rows, cut[2]] = (mm(normed, w_qkv[:, cut[2]]) + row(b_value)).astype(bf16)

        def send(f):
            window_copy(f, mix_v, unit_out, 4).start()
            window_copy(f, x_v, x_out, 5).start()
            return f + 1

        return lax.while_loop(functools.partial(finished, i), send, sent)

    lax.fori_loop(0, blocks, project, 0)
    pltpu.make_async_copy(unit_out, unit_out, window_sems.at[4]).wait()

    def probs_copy(i):
        slot = lax.rem(i, 2)
        return pltpu.make_async_copy(
            probs_v.at[slot], probs_out.at[pl.ds(i * AHEAD, AHEAD)], probs_sems.at[slot]
        )

    def attend(i, carry):
        slot = lax.rem(i, 2)

        @pl.when(i >= 2)
        def _():
            probs_copy(i - 2).wait()

        for u in range(AHEAD):
            window_copy(i * AHEAD + u, qkv_v, qkv_out, 0).start()
        places = [where_is(i * AHEAD + u) for u in range(AHEAD)]
        windows = [pl.ds(base, slots) for base, _, _ in places]
        scores = []
        for window in windows:
            stacked = block_heads(qkv_v[window, 0:width], mask_v)
            scores.append(heads_dot(qkv_v[window, width : 2 * width], stacked))
        weights = []
        for (_, head, count), score in zip(places, scores):
            slot_row = lax.broadcasted_iota(jnp.int32, score.shape, 0)
            live = (slot_row >= head) & (slot_row < head + count)
            score = jnp.where(live, score, FILL)
            expo = jnp.exp(score - jnp.max(score, axis=0, keepdims=True))
            total_row = jnp.sum(expo, axis=0, keepdims=True)
            weights.append((expo * (1.0 / total_row)).astype(bf16))
        for u, weight in enumerate(weights):
            probs_v[slot, u] = weight
        turned = [pairs_t(weight) for weight in weights]
        mixed = [
            heads_out_t(weight, qkv_v[window, 2 * width : 3 * width]).astype(bf16)
            for weight, window in zip(turned, windows)
        ]
        for (base, head, _), out in zip(places, mixed):
            merge_store(mix_v, base, head, out)
        probs_copy(i).start()
        return carry

    steps = fields // AHEAD
    lax.fori_loop(0, steps, attend, 0)
    probs_copy(steps - 2).wait()
    probs_copy(steps - 1).wait()
    mix_v[pl.ds(tail, ROWS), :] = jnp.zeros((ROWS, width), bf16)

    def act_copy(i):
        rows = pl.ds(pl.multiple_of(i * ROWS, ROWS), ROWS)
        slot = lax.rem(i, 2)
        return pltpu.make_async_copy(act_v.at[slot], act_out.at[rows], act_sems.at[slot])

    def base_copy(i):
        rows = pl.ds(pl.multiple_of(i * ROWS, ROWS), ROWS)
        return pltpu.make_async_copy(x_v.at[rows], base_out.at[rows], base_sems.at[i])

    def feed(i, sent):
        rows = pl.ds(pl.multiple_of(i * ROWS, ROWS), ROWS)
        slot = lax.rem(i, 2)

        @pl.when(i >= 2)
        def _():
            act_copy(i - 2).wait()

        mixed = mix_v[rows, :]
        grad_b = g_v[rows, :]
        grad = grad_b.astype(f32)
        residual = x_v[rows, :].astype(f32) + (mm(mixed, w_out[...]) + row(b_out))
        unit, rstd = row_norm(residual)
        normed = (unit * row(gain_mlp) + row(shift_mlp)).astype(bf16)
        normed_t = normed.T
        grad_t = grad_b.T
        for at in range(0, hidden, CHUNK):
            cols = slice(at, at + CHUNK)
            up = mm(normed, w_up[:, cols]) + row(b_up, cols)
            d_act = mm_nt(grad_b, w_down[cols, :])
            cdf = 0.5 + 0.5 * lax.erf(up * 0.7071067811865476)
            pdf = 0.3989422804014327 * jnp.exp(-0.5 * up * up)
            act_v[slot, :, cols] = (up * cdf).astype(bf16)
            d_up = d_act * (cdf + up * pdf)
            dup_v[:, cols] = d_up.astype(bf16)
            gb_up[:, cols] += fold(d_up)
        act_copy(i).start()
        d_normed = mm_nt(dup_v[...], w_up[...])
        add_blocks(sums, up_at, mm(normed_t, dup_v[...]))
        add_blocks(sums, down_at, mm(grad_t, act_v[slot]))
        x_v[rows, :] = (residual + row(b_down)).astype(bf16)
        base_copy(i).start()
        gb_down[...] += fold(grad)
        gg_mlp[...] += fold(d_normed * unit)
        gs_mlp[...] += fold(d_normed)
        d_residual = grad + norm_back(d_normed * row(gain_mlp), unit, rstd)
        d_att = d_residual.astype(bf16)
        gb_out[...] += fold(d_residual)
        add_blocks(sums, out_at, mm_tn(mixed, d_att))
        g_v[rows, :] = d_att
        mix_v[rows, :] = mm_nt(d_att, w_out[...]).astype(bf16)

        def send(f):
            window_copy(f, g_v, att_out, 1).start()
            window_copy(f, mix_v, mix_out, 2).start()
            return f + 1

        return lax.while_loop(functools.partial(finished, i), send, sent)

    pltpu.make_async_copy(x_out, x_out, window_sems.at[5]).wait()
    lax.fori_loop(0, blocks, feed, 0)
    at = vector_at
    for partial in (gb_up, gb_down, gb_out, gg_mlp, gs_mlp):
        at = add_vector(sums, at, partial[...])

    lax.fori_loop(jnp.maximum(blocks - 2, 0), blocks, lambda i, c: act_copy(i).wait(), None)
    lax.fori_loop(0, blocks, lambda i, c: base_copy(i).wait(), None)
    for kind, ref in enumerate((qkv_out, att_out, mix_out)):
        pltpu.make_async_copy(ref, ref, window_sems.at[kind]).wait()


FIRST_IN_ATTEND = (1, 3, 6, 9, 11, 13, 15)
FIRST_IN_PROJECT = (2, 6, 10, 14)
SECOND_IN_PROJECT = (0, 2, 4, 6, 8, 10, 12, 14)


def backward_kernel(
    orders, fields, slots, width,
    counts, starts, qkv, probs, mix, unit, att, x_in, base, act, sums_a,
    w_qkv, gain_attn, shift_attn, w_down,
    d_in, enc, out_a, out_b,
    packed_v, mask_v, gb_qkv, total_a, total_b, load_sem, store_sems,
    sent_a, got_a, summed_a, send_a, recv_a, sent_b, got_b, summed_b, send_b, recv_b,
):
    first = Reducer(orders, total_a.shape[0], total_a, sent_a, got_a, summed_a, send_a, recv_a)
    second = Reducer(orders, total_b.shape[0], total_b, sent_b, got_b, summed_b, send_b, recv_b)
    load = pltpu.make_async_copy(sums_a, total_a, load_sem)
    load.start()
    steps = fields // UNROLL
    rows = UNROLL * slots

    first.greet()
    fill_mask(mask_v)
    total_b[...] = jnp.zeros_like(total_b)
    gb_qkv[...] = jnp.zeros_like(gb_qkv)

    def at_step(step, reducer, ahead, begin):
        for k, when in enumerate(ahead):

            @pl.when(step == when)
            def _(k=k):
                reducer.advance(begin + k)

    def field_rows(step, u):
        return pl.ds(pl.multiple_of((step * UNROLL + u) * slots, slots), slots)

    def here(step):
        return pl.ds(pl.multiple_of(step * rows, rows), rows)

    def attend(qkv_b, probs_b, mix_b, unit_b):
        step = pl.program_id(0)

        @pl.when(step == FIRST_IN_ATTEND[0])
        def _():
            load.wait()

        at_step(step, first, FIRST_IN_ATTEND, 0)
        grads = []
        for u in range(UNROLL):
            f = step * UNROLL + u
            head = lax.rem(starts[f], TILE)
            slot_row = lax.broadcasted_iota(jnp.int32, (slots, width), 0)
            live = (slot_row >= head) & (slot_row < head + counts[f])
            grads.append(block_heads(mix_b[u] * live.astype(f32).astype(bf16), mask_v))
        d_probs = [heads_dot(qkv_b[u, :, 2 * width :], grads[u]) for u in range(UNROLL)]
        for u in range(UNROLL):
            packed_v[field_rows(step, u), 2 * width :] = heads_out(probs_b[u], grads[u]).astype(bf16)
        d_scores = []
        for u in range(UNROLL):
            weights = probs_b[u].astype(f32)
            weighted = weights * d_probs[u]
            inner = jnp.sum(weighted, axis=0, keepdims=True)
            d_scores.append((weighted - weights * inner).astype(bf16))
        for u in range(UNROLL):
            query = block_heads(qkv_b[u, :, :width], mask_v)
            packed_v[field_rows(step, u), width : 2 * width] = heads_out(d_scores[u], query).astype(bf16)
        turned = [pairs_t(d_score) for d_score in d_scores]
        for u in range(UNROLL):
            d_query = heads_out_t(turned[u], qkv_b[u, :, width : 2 * width])
            packed_v[field_rows(step, u), :width] = (d_query * HEAD**-0.5).astype(bf16)
        grad = packed_v[here(step), :]
        add_blocks(total_b, 0, mm_tn(unit_b[...].reshape(rows, width), grad))
        gb_qkv[...] += fold(grad.astype(f32))

    def block(*shape):
        return pl.BlockSpec((UNROLL,) + shape, lambda i: (i, 0, 0))

    pltpu.emit_pipeline(
        attend,
        grid=(steps,),
        in_specs=[block(slots, 3 * width)] + [block(slots, width)] * 3,
    )(qkv, probs, mix, unit)

    at = 3 * width * width // LANES
    add_vector(total_b, at, gb_qkv[...])
    grad_sum = jnp.sum(gb_qkv[...], axis=0, keepdims=True)
    gain = jnp.broadcast_to(row(gain_attn), (LANES, width)).T
    shift = jnp.broadcast_to(row(shift_attn), (LANES, width)).T
    gain_sum = jnp.zeros((width, LANES), f32)
    shift_sum = jnp.zeros((width, LANES), f32)
    for k in range(3 * width // LANES):
        at_rows = pl.ds(k * width, width)
        cols = slice(k * LANES, (k + 1) * LANES)
        weight = w_qkv[:, cols].astype(f32)
        part = total_b[at_rows, :]
        column = jnp.broadcast_to(grad_sum[:, cols], (width, LANES))
        gain_sum += weight * part
        shift_sum += weight * column
        total_b[at_rows, :] = gain * part + shift * column
    at += 3 * width // LANES
    at = add_vector(total_b, at, gain_sum.T)
    add_vector(total_b, at, shift_sum.T)

    less = PART // SPLIT

    def project(x_b, att_b, act_b, base_b, d_in_b, enc_b):
        step = pl.program_id(0)
        at_step(step, second, SECOND_IN_PROJECT, 0)
        at_step(step, first, FIRST_IN_PROJECT, len(FIRST_IN_ATTEND))
        grads, downs = {}, {}
        for k in range(rows // PART + 1):
            if k < rows // PART:
                at = pl.multiple_of(step * rows + k * PART, PART)
                grads[k] = mm_nt(packed_v[pl.ds(at, PART), :], w_qkv[...])
                downs[k] = mm(act_b[k * less : (k + 1) * less, :], w_down[...])
            if k:
                part = pl.ds((k - 1) * PART, PART)
                unit, rstd = row_norm(x_b[part, :].astype(f32))
                d_x = norm_back(grads.pop(k - 1) * row(gain_attn), unit, rstd)
                d_in_b[part, :] = (att_b[part, :].astype(f32) + d_x).astype(bf16)
                part = pl.ds((k - 1) * less, less)
                enc_b[part, :] = (base_b[part, :].astype(f32) + downs.pop(k - 1)).astype(bf16)

    narrow = pl.BlockSpec((rows, width), lambda i: (i, 0))
    short = pl.BlockSpec((rows // SPLIT, width), lambda i: (i, 0))
    pltpu.emit_pipeline(
        project,
        grid=(steps,),
        in_specs=[
            narrow, narrow, pl.BlockSpec((rows // SPLIT, act.shape[1]), lambda i: (i, 0)), short,
        ],
        out_specs=[narrow, short],
    )(x_in, att, act, base, d_in, enc)

    for k in range(len(FIRST_IN_ATTEND) + len(FIRST_IN_PROJECT), first.steps):
        first.advance(k)
    store_a = pltpu.make_async_copy(summed_a, out_a, store_sems.at[0])
    store_a.start()
    for k in range(len(SECOND_IN_PROJECT), second.steps):
        second.advance(k)
    store_b = pltpu.make_async_copy(summed_b, out_b, store_sems.at[1])
    store_b.start()
    store_a.wait()
    store_b.wait()


def unblock(src, at, dst):
    rows, columns = dst.shape
    for k in range(columns // LANES):
        dst[:, k * LANES : (k + 1) * LANES] = src[pl.ds(at + k * rows, rows), :].astype(f32)


def unblock_t(src, at, dst):
    rows, columns = dst.shape
    for k in range(rows // LANES):
        part = src[pl.ds(at + k * columns, columns), :].astype(f32)
        dst[k * LANES : (k + 1) * LANES, :] = part.T


def unblock_vector(src, at, dst):
    (columns,) = dst.shape
    for k in range(columns // LANES):
        dst[k * LANES : (k + 1) * LANES] = src[pl.ds(at + k, 1), :].astype(f32).reshape(LANES)


def unpack_kernel(
    fields, slots, width, hidden,
    counts, starts, visible, d_in, enc, base, act, w_down_in, sums_a, sums_b,
    encoded, input_grad, w_qkv, b_query, b_value, w_out, b_out, w_up, b_up, w_down, b_down,
    gain_attn, shift_attn, gain_mlp, shift_mlp,
    d_in_v, enc_v, out_v, grad_v, act_v, qkv_v, up_v, down_v, sems, weight_sems,
):
    up_at, down_at, out_at, at = sum_rows(width, hidden)
    steps = fields // GROUP

    def group(step):
        return pl.ds(step * GROUP, GROUP)

    def enc_load(src, step):
        rows = pl.ds(pl.multiple_of(step * GROUP * slots, GROUP * slots), GROUP * slots)
        return pltpu.make_async_copy(src.at[rows], enc_v.at[rows], sems.at[1, step])

    early = enc.shape[0] // (GROUP * slots)

    def act_load(step):
        size = GROUP * slots
        src = pl.ds(pl.multiple_of(step * size, size), size)
        dst = pl.ds(pl.multiple_of((step - early) * size, size), size)
        return pltpu.make_async_copy(act.at[src], act_v.at[dst], sems.at[2, step])

    def used(step):
        return step * GROUP * slots < starts[fields - 1] + slots

    def loads(step):
        rows = pl.ds(pl.multiple_of(step * GROUP * slots, GROUP * slots), GROUP * slots)
        return (
            pltpu.make_async_copy(d_in.at[rows], d_in_v.at[rows], sems.at[0, step]),
        )

    def stores(step):
        return (
            pltpu.make_async_copy(out_v.at[group(step)], encoded.at[group(step)], sems.at[1, step]),
            pltpu.make_async_copy(grad_v.at[group(step)], input_grad.at[group(step)], sems.at[0, step]),
        )

    def start_loads(step, carry):
        for copy in loads(step):
            copy.start()

        @pl.when(step < early)
        def _():
            enc_load(enc, step).start()

        @pl.when((step >= early) & used(step))
        def _():
            enc_load(base, step).start()
            act_load(step).start()

        return carry

    def wait_stores(step, carry):
        for copy in stores(step):
            copy.wait()
        return carry

    def unpack(step, carry):
        for copy in loads(step):
            copy.wait()

        @pl.when(step < early)
        def _():
            enc_load(enc, step).wait()

        @pl.when((step >= early) & used(step))
        def _():
            enc_load(base, step).wait()
            act_load(step).wait()
            size = GROUP * slots
            here = pl.ds(pl.multiple_of(step * size, size), size)
            late = pl.ds(pl.multiple_of((step - early) * size, size), size)
            last = enc_v[here, :].astype(f32) + mm(act_v[late, :], w_down_in[...])
            enc_v[here, :] = last.astype(bf16)

        patch_row = lax.broadcasted_iota(jnp.int32, (input_grad.shape[1], slots), 0)
        rows = lax.broadcasted_iota(jnp.int32, (slots, slots), 0)
        cols = lax.broadcasted_iota(jnp.int32, (slots, slots), 1)
        puts, shifts = [], []
        for u in range(GROUP):
            f = step * GROUP + u
            head, count = lax.rem(starts[f], TILE), counts[f]
            picks = shifted_picks(visible[pl.ds(f, 1), :], head, count)
            puts.append((patch_row == picks).astype(f32).astype(bf16))
            shifts.append(((cols - rows == head) & (rows < count)).astype(f32).astype(bf16))
        for u in range(GROUP):
            f = step * GROUP + u
            window = pl.ds(pl.multiple_of(f * slots, slots), slots)
            grad_v[f] = mm(puts[u], d_in_v[window, :]).astype(bf16)
            at = pl.multiple_of(starts[f] - lax.rem(starts[f], TILE), TILE)
            out_v[f] = mm(shifts[u], enc_v[pl.ds(at, slots), :]).astype(bf16)
        for copy in stores(step):
            copy.start()
        return carry

    lax.fori_loop(0, steps, start_loads, 0)
    lax.fori_loop(0, steps, unpack, 0)
    copies = []
    unblock(sums_a, up_at, up_v)
    copies.append(pltpu.make_async_copy(up_v, w_up, weight_sems.at[0]))
    copies[0].start()
    unblock_t(sums_a, down_at, down_v)
    copies.append(pltpu.make_async_copy(down_v, w_down, weight_sems.at[1]))
    copies[1].start()
    unblock(sums_b, 0, qkv_v)
    copies.append(pltpu.make_async_copy(qkv_v, w_qkv, weight_sems.at[2]))
    copies[2].start()
    unblock(sums_a, out_at, w_out)
    for ref in (b_up, b_down, b_out, gain_mlp, shift_mlp):
        unblock_vector(sums_a, at, ref)
        at += ref.shape[0] // LANES
    at = 3 * width * width // LANES
    for ref, rows in ((b_query, 2), (b_value, 1), (gain_attn, 1), (shift_attn, 1)):
        unblock_vector(sums_b, at, ref)
        at += rows * width // LANES
    lax.fori_loop(0, steps, wait_stores, 0)
    for copy in copies:
        copy.wait()


def forward(sizes, args):
    (
        patches, visible, counts, upstream, w_qkv, b_query, b_value, w_out, b_out,
        w_up, b_up, w_down, b_down, gain_attn, shift_attn, gain_mlp, shift_mlp,
    ) = args
    fields, _, width = patches.shape
    slots, hidden = visible.shape[1], w_up.shape[1]
    cap = (fields * slots + ROWS - 1) // ROWS * ROWS
    tall = cap + ROWS
    vectors = (hidden + 4 * width) // LANES
    rows_a = padded_rows(sum_rows(width, hidden)[3] + vectors, sizes)
    shape = jax.ShapeDtypeStruct
    hbm = pl.BlockSpec(memory_space=pl.ANY)
    vmem = pl.BlockSpec(memory_space=pltpu.VMEM)
    smem = pl.BlockSpec(memory_space=pltpu.SMEM)
    windows = shape((fields, slots, width), bf16)
    return pl.pallas_call(
        functools.partial(forward_kernel, fields, slots, width, hidden),
        out_shape=[
            shape((fields,), jnp.int32),
            windows,
            windows,
            shape((fields, slots, 3 * width), bf16),
            windows,
            windows,
            windows,
            shape((cap, width), bf16),
            shape((cap, hidden), bf16),
            shape((rows_a, LANES), f32),
        ],
        in_specs=[smem, hbm, vmem, hbm] + [vmem] * 13,
        out_specs=[smem] + [hbm] * 8 + [vmem],
        scratch_shapes=[
            pltpu.VMEM((tall, width), bf16),
            pltpu.VMEM((tall, width), bf16),
            pltpu.VMEM((cap, 3 * width), bf16),
            pltpu.VMEM((tall, width), bf16),
            pltpu.VMEM((2, AHEAD, slots, width), bf16),
            pltpu.VMEM((2, ROWS, hidden), bf16),
            pltpu.VMEM((ROWS, hidden), bf16),
            pltpu.VMEM((4 * HEAD, 4 * HEAD), bf16),
            pltpu.VMEM((8, hidden), f32),
            pltpu.VMEM((8, width), f32),
            pltpu.VMEM((8, width), f32),
            pltpu.VMEM((8, width), f32),
            pltpu.VMEM((8, width), f32),
            pltpu.SemaphoreType.DMA((6,)),
            pltpu.SemaphoreType.DMA((2,)),
            pltpu.SemaphoreType.DMA((2, fields // BATCH)),
            pltpu.SemaphoreType.DMA((2,)),
            pltpu.SemaphoreType.DMA((cap // ROWS,)),
        ],
        compiler_params=pltpu.CompilerParams(vmem_limit_bytes=VMEM_BYTES),
        name="forward_rows",
    )(
        counts, patches.reshape(-1, width), visible, upstream.reshape(-1, width),
        w_qkv, b_query, b_value, w_out, b_out, w_up, b_up, w_down, b_down, gain_attn, shift_attn, gain_mlp, shift_mlp,
    )


def backward(
    sizes, counts, starts, qkv, probs, mix, unit, att, x_rows, base, act, sums_a,
    w_qkv, gain, shift, w_down,
):
    fields, slots, width = mix.shape
    rows_b = padded_rows((3 * width * width + 5 * width) // LANES, sizes)
    shape = jax.ShapeDtypeStruct
    hbm = pl.BlockSpec(memory_space=pl.ANY)
    vmem = pl.BlockSpec(memory_space=pltpu.VMEM)
    smem = pl.BlockSpec(memory_space=pltpu.SMEM)
    return pl.pallas_call(
        functools.partial(backward_kernel, exchange_orders(sizes), fields, slots, width),
        out_shape=[
            shape((fields * slots, width), bf16),
            shape((act.shape[0] // SPLIT, width), bf16),
            shape(sums_a.shape, bf16),
            shape((rows_b, LANES), bf16),
        ],
        in_specs=[smem, smem] + [hbm] * 9 + [vmem] * 4,
        out_specs=[hbm] * 4,
        scratch_shapes=[
            pltpu.VMEM((fields * slots, 3 * width), bf16),
            pltpu.VMEM((4 * HEAD, 4 * HEAD), bf16),
            pltpu.VMEM((8, 3 * width), f32),
            pltpu.VMEM(sums_a.shape, f32),
            pltpu.VMEM((rows_b, LANES), f32),
            pltpu.SemaphoreType.DMA,
            pltpu.SemaphoreType.DMA((2,)),
        ]
        + reducer_scratch(sums_a.shape[0], sizes)
        + reducer_scratch(rows_b, sizes),
        compiler_params=pltpu.CompilerParams(
            collective_id=0, has_side_effects=True, vmem_limit_bytes=VMEM_BYTES
        ),
        name="backward_rows",
    )(
        counts, starts, qkv, probs, mix, unit, att.reshape(-1, width), x_rows.reshape(-1, width),
        base, act, sums_a, w_qkv, gain, shift, w_down,
    )


def unpack_all(
    counts, starts, visible, d_in, enc, base, act, w_down, sums_a, sums_b, patch_rows, hidden
):
    (fields, slots), width = visible.shape, d_in.shape[1]
    shape = jax.ShapeDtypeStruct
    hbm = pl.BlockSpec(memory_space=pl.ANY)
    vmem = pl.BlockSpec(memory_space=pltpu.VMEM)
    smem = pl.BlockSpec(memory_space=pltpu.SMEM)
    vector = shape((width,), f32)
    return pl.pallas_call(
        functools.partial(unpack_kernel, fields, slots, width, hidden),
        out_shape=[
            shape((fields, slots, width), bf16),
            shape((fields, patch_rows, width), bf16),
            shape((width, 3 * width), f32), vector, vector,
            shape((width, width), f32), vector,
            shape((width, hidden), f32), shape((hidden,), f32),
            shape((hidden, width), f32), vector,
            vector, vector, vector, vector,
        ],
        in_specs=[smem, smem, vmem] + [hbm] * 4 + [vmem] * 3,
        out_specs=[hbm] * 3 + [vmem] * 4 + [hbm, vmem, hbm] + [vmem] * 5,
        scratch_shapes=[
            pltpu.VMEM(d_in.shape, bf16),
            pltpu.VMEM(base.shape, bf16),
            pltpu.VMEM((fields, slots, width), bf16),
            pltpu.VMEM((fields, patch_rows, width), bf16),
            pltpu.VMEM((base.shape[0] - enc.shape[0], hidden), bf16),
            pltpu.VMEM((width, 3 * width), f32),
            pltpu.VMEM((width, hidden), f32),
            pltpu.VMEM((hidden, width), f32),
            pltpu.SemaphoreType.DMA((3, fields // GROUP)),
            pltpu.SemaphoreType.DMA((3,)),
        ],
        compiler_params=pltpu.CompilerParams(vmem_limit_bytes=VMEM_BYTES),
        name="unpack_rows",
    )(counts, starts, visible, d_in, enc, base, act, w_down, sums_a, sums_b)


def per_device(sizes, *args):
    patches, visible, counts = args[:3]
    w_qkv, w_up, gain_attn, shift_attn = args[4], args[9], args[13], args[14]
    starts, x_rows, unit, qkv, probs, att, mix, base, act, sums_a = forward(sizes, args)
    d_in, enc, total_a, total_b = backward(
        sizes, counts, starts, qkv, probs, mix, unit, att, x_rows, base, act, sums_a,
        w_qkv, gain_attn, shift_attn, args[11],
    )
    return tuple(
        unpack_all(
            counts, starts, visible, d_in, enc, base, act, args[11], total_a, total_b, patches.shape[1], w_up.shape[1]
        )
    )


def solution(mesh):
    rows = P(("wide", "narrow"))
    return jax.shard_map(
        functools.partial(per_device, dict(mesh.shape)),
        mesh=mesh,
        in_specs=(rows,) * 4 + (P(),) * 13,
        out_specs=(rows,) * 2 + (P(),) * 13,
        check_vma=False,
    )
```

```python
import functools

import jax
import jax.numpy as jnp
from jax import lax
from jax.experimental import pallas as pl
from jax.experimental.pallas import tpu as pltpu
from jax.sharding import PartitionSpec as P

HEAD = 64
EPS = 1e-06
FILL = -1e30
ROWS = 512
TILE = 16
UNROLL = 16
AHEAD = 16
GROUP = 8
BATCH = 16
PART = 256
SPLIT = 2
CHUNK = 256
VMEM_BYTES = 60 * 1024 * 1024
f32 = jnp.float32
bf16 = jnp.bfloat16


LANES = 128


def mm(left, right):
    return lax.dot_general(left, right, (((1,), (0,)), ((), ())), preferred_element_type=f32)


def mm_nt(left, right):
    return lax.dot_general(left, right, (((1,), (1,)), ((), ())), preferred_element_type=f32)


def mm_tn(left, right):
    return lax.dot_general(left, right, (((0,), (0,)), ((), ())), preferred_element_type=f32)


def row_norm(values):
    width = values.shape[-1]
    mean = jnp.sum(values, axis=-1, keepdims=True) * (1.0 / width)
    centered = values - mean
    variance = jnp.sum(centered * centered, axis=-1, keepdims=True) * (1.0 / width)
    rstd = lax.rsqrt(variance + EPS)
    return centered * rstd, rstd


def norm_back(grad, unit, rstd):
    width = grad.shape[-1]
    first = jnp.sum(grad, axis=-1, keepdims=True) * (1.0 / width)
    second = jnp.sum(grad * unit, axis=-1, keepdims=True) * (1.0 / width)
    return (grad - first - unit * second) * rstd


def fold(values):
    rows, width = values.shape
    return jnp.sum(values.reshape(rows // 8, 8, width), axis=0)


def fill_mask(mask):
    row = lax.broadcasted_iota(jnp.int32, mask.shape, 0) // HEAD
    col = lax.broadcasted_iota(jnp.int32, mask.shape, 1) // HEAD
    mask[...] = (row == col).astype(f32).astype(bf16)


def head_parts(width):
    parts, at = [], 0
    while at < width:
        size = min(4 * HEAD, width - at)
        parts.append((at, size))
        at += size
    return parts


def block_heads(values, mask):
    blocks = []
    for at, size in head_parts(values.shape[1]):
        tiled = jnp.concatenate([values[:, at : at + size]] * (size // HEAD), axis=0)
        blocks.append(tiled * mask[:size, :size])
    return blocks


def heads_dot(left, stacked):
    parts = [
        mm_nt(left[:, at : at + size], block)
        for (at, size), block in zip(head_parts(left.shape[1]), stacked)
    ]
    return jnp.concatenate(parts, axis=1)


def heads_out(left, stacked):
    parts = [
        mm(left[:, at : at + size], block)
        for (at, size), block in zip(head_parts(left.shape[1]), stacked)
    ]
    return jnp.concatenate(parts, axis=1)


def heads_out_t(weights, values):
    window = weights[0].shape[0] // 2
    parts = []
    for k, at in enumerate(range(0, values.shape[1], 2 * HEAD)):
        pair = mm(weights[k], values[:, at : at + 2 * HEAD])
        lane = lax.broadcasted_iota(jnp.int32, (window, 2 * HEAD), 1)
        parts.append(jnp.where(lane < HEAD, pair[:window], pair[window:]))
    return jnp.concatenate(parts, axis=1)


def pairs_t(values):
    return [values[:, at : at + 2 * HEAD].T for at in range(0, values.shape[1], 2 * HEAD)]


def add_blocks(sums, at, values):
    rows = values.shape[0]
    for k in range(values.shape[1] // LANES):
        block = pl.ds(at + k * rows, rows)
        sums[block, :] += values[:, k * LANES : (k + 1) * LANES]


def add_vector(sums, at, partial):
    vector = jnp.sum(partial, axis=0, keepdims=True)
    for k in range(vector.shape[1] // LANES):
        sums[pl.ds(at + k, 1), :] = vector[:, k * LANES : (k + 1) * LANES]
    return at + vector.shape[1] // LANES


def row(ref, cols=slice(None)):
    return ref[cols].reshape(1, -1)


def shifted_picks(vis, head, count):
    slots = vis.shape[1]
    lane = lax.broadcasted_iota(jnp.int32, vis.shape, 1)
    live = jnp.where(lane < count, vis, -1)
    wide = jnp.concatenate([live, jnp.full((1, LANES - slots), -1, jnp.int32)], axis=1)
    return pltpu.roll(wide, head, axis=1)[:, :slots]


def merge_store(ref, base, head, window):
    old = ref[pl.ds(base, TILE), :]
    row = lax.broadcasted_iota(jnp.int32, (TILE, window.shape[1]), 0)
    ref[pl.ds(base, TILE), :] = jnp.where(row >= head, window[:TILE], old)
    rest = window.shape[0] - TILE
    ref[pl.ds(base + TILE, rest), :] = window[TILE:]


def mesh_bits(sizes):
    wide = [("wide", 1 << k) for k in range(sizes["wide"].bit_length() - 1)]
    narrow = [("narrow", 1 << k) for k in range(sizes["narrow"].bit_length() - 1)]
    return wide, narrow


def exchange_orders(sizes):
    wide, narrow = mesh_bits(sizes)
    first, last = narrow[:1], wide[-1:]
    middle = wide[:1] + narrow[1:] + wide[1:-1]
    orders = [first + middle[k:] + middle[:k] + last for k in range(min(3, len(middle)))]
    return [[(pair,) for pair in order] for order in orders]


def direct_orders(sizes):
    wide, narrow = mesh_bits(sizes)
    plane, line = tuple(wide[:1] + narrow[1:]), tuple(wide[1:])
    return [[tuple(narrow[:1]), plane, line], [tuple(narrow[:1]), line, plane]]


def members(group):
    return [
        tuple(pair for k, pair in enumerate(group) if mask >> k & 1)
        for mask in range(1, 1 << len(group))
    ]


def rows_of_parts(rows, orders):
    unit = TILE << sum(len(group) for group in orders[0])
    units, parts, at = rows // unit, [], 0
    for k in range(len(orders)):
        share = (units + len(orders) - 1 - k) // len(orders) * unit
        if share:
            parts.append((at, share))
        at += share
    return parts


class Reducer:
    def __init__(self, orders, rows, total, sent, got, summed, send_sems, recv_sems):
        self.orders, self.total, self.sent, self.got, self.summed = orders, total, sent, got, summed
        self.send_sems, self.recv_sems = send_sems, recv_sems
        self.stages = len(orders[0])
        self.parts = rows_of_parts(rows, orders)
        self.sides = {}
        for group in orders[0]:
            for axis, distance in group:
                self.sides[axis, distance] = lax.rem(lax.axis_index(axis) // distance, 2)
        self.bases, self.sizes = [], []
        for order, (base, size) in zip(orders, self.parts):
            bases, sizes = [base], [size]
            for group in order:
                sizes.append(sizes[-1] >> len(group))
                bases.append(bases[-1] + self.place(group) * sizes[-1])
            self.bases.append(bases)
            self.sizes.append(sizes)

    def place(self, group, flipped=()):
        place = 0
        for k, pair in enumerate(group):
            side = self.sides[pair]
            place = place + (1 << k) * (1 - side if pair in flipped else side)
        return place

    def device(self, flipped):
        other = {}
        for axis, distance in flipped:
            mine = other.get(axis, lax.axis_index(axis))
            other[axis] = mine + distance * (1 - 2 * self.sides[axis, distance])
        return other

    def partners(self):
        return {flipped for order in self.orders for group in order for flipped in members(group)}

    def greet(self, partners):
        barrier = pltpu.get_barrier_semaphore()
        for flipped in sorted(partners):
            pl.semaphore_signal(
                barrier, inc=1, device_id=self.device(flipped), device_id_type=pl.DeviceIdType.MESH
            )
        pl.semaphore_wait(barrier, len(partners))

    def flights(self, part, stage):
        summing = stage < self.stages
        level = stage if summing else 2 * self.stages - 1 - stage
        group = self.orders[part][level]
        size = self.sizes[part][level + 1]
        base, share = self.parts[part]
        for k, flipped in enumerate(members(group)):
            if summing:
                slot = pl.ds(base + share - self.sizes[part][level] + k * size, size)
                src, dst = self.sent.at[slot], self.got.at[slot]
            else:
                slot = pl.ds(pl.multiple_of(self.bases[part][level + 1], TILE), size)
                src = dst = self.summed.at[slot]
            copy = pltpu.make_async_remote_copy(
                src_ref=src, dst_ref=dst,
                send_sem=self.send_sems.at[part, stage, k], recv_sem=self.recv_sems.at[part, stage, k],
                device_id=self.device(flipped), device_id_type=pl.DeviceIdType.MESH,
            )
            yield copy, flipped, slot

    def leave(self, part, stage):
        for copy, flipped, slot in self.flights(part, stage):
            if stage < self.stages:
                size = self.sizes[part][stage + 1]
                at = self.bases[part][stage] + self.place(self.orders[part][stage], flipped) * size
                self.sent[slot, :] = self.total[pl.ds(pl.multiple_of(at, TILE), size), :].astype(bf16)
            copy.start()

    def arrive(self, part, stage):
        flights = list(self.flights(part, stage))
        for copy, _, _ in flights:
            copy.wait()
        if stage < self.stages:
            here = pl.ds(pl.multiple_of(self.bases[part][stage + 1], TILE), self.sizes[part][stage + 1])
            value = self.total[here, :]
            for _, _, slot in flights:
                value = value + self.got[slot, :].astype(f32)
            if stage + 1 < self.stages:
                self.total[here, :] = value
            else:
                self.summed[here, :] = value.astype(bf16)

    def advance(self, stage):
        for part in range(len(self.parts)):
            if stage:
                self.arrive(part, stage - 1)
            if stage < 2 * self.stages:
                self.leave(part, stage)

    @property
    def steps(self):
        return 2 * self.stages + 1


def padded_rows(rows, sizes):
    unit = TILE * sizes["wide"] * sizes["narrow"]
    return (rows + unit - 1) // unit * unit


def reducer_scratch(rows, orders):
    most = max(len(members(group)) for group in orders[0])
    flights = (len(orders), 2 * len(orders[0]), most)
    return [
        pltpu.VMEM((rows, LANES), bf16),
        pltpu.VMEM((rows, LANES), bf16),
        pltpu.VMEM((rows, LANES), bf16),
        pltpu.SemaphoreType.DMA(flights),
        pltpu.SemaphoreType.DMA(flights),
    ]


def sum_rows(width, hidden):
    up, out = width * hidden // LANES, width * width // LANES
    return 0, up, 2 * up, 2 * up + out


def forward_kernel(
    fields, slots, width, hidden,
    counts, patches, visible, upstream,
    w_qkv, b_query, b_value, w_out, b_out, w_up, b_up, w_down, b_down,
    gain_attn, shift_attn, gain_mlp, shift_mlp,
    starts, x_out, unit_out, qkv_out, probs_out, att_out, mix_out, base_out, act_out, sums,
    x_v, g_v, qkv_v, mix_v, probs_v, act_v, dup_v, mask_v, picks_v,
    gb_up, gb_down, gb_out, gg_mlp, gs_mlp, window_sems, probs_sems, land_sems,
    act_sems, base_sems,
):
    up_at, down_at, out_at, vector_at = sum_rows(width, hidden)
    patch_rows = patches.shape[0] // fields
    steps = fields // BATCH
    landing = qkv_v.shape[0] // (BATCH * patch_rows)
    cut = [slice(k * width, (k + 1) * width) for k in range(3)]

    def arrivals(third, step):
        size = BATCH * patch_rows
        src = pl.ds(pl.multiple_of(step * size, size), size)
        dst = pl.ds(pl.multiple_of((step - third * landing) * size, size), size)
        size = BATCH * slots
        up = pl.ds(pl.multiple_of(step * size, size), size)
        return (
            pltpu.make_async_copy(patches.at[src], qkv_v.at[dst, cut[third]], land_sems.at[0, step]),
            pltpu.make_async_copy(upstream.at[up], qkv_v.at[up, cut[2]], land_sems.at[1, step]),
        )

    def start_arrivals(third, step, carry):
        for copy in arrivals(third, step):
            copy.start()
        return carry

    for third in range(steps // landing):
        lax.fori_loop(
            third * landing, (third + 1) * landing, functools.partial(start_arrivals, third), 0
        )

    def place(f, at):
        count = counts[f]
        head = lax.rem(at, TILE)
        at = jnp.where(head + count > slots, at + TILE - head, at)
        starts[f] = at
        return at + count

    lax.fori_loop(0, fields, place, 0)
    last = starts[fields - 1]
    tail = pl.multiple_of(last - lax.rem(last, TILE) + slots, TILE)
    blocks = (tail + ROWS - 1) // ROWS
    for ref in (sums, gb_up, gb_down, gb_out, gg_mlp, gs_mlp):
        ref[...] = jnp.zeros_like(ref)
    fill_mask(mask_v)
    picks_v[...] = visible[...].T

    def where_is(f):
        start = starts[f]
        head = lax.rem(start, TILE)
        return pl.multiple_of(start - head, TILE), head, counts[f]

    def pack(third, step, carry):
        for copy in arrivals(third, step):
            copy.wait()
        patch_row = lax.broadcasted_iota(jnp.int32, (patch_rows, slots), 0)
        rows = lax.broadcasted_iota(jnp.int32, (slots, slots), 0)
        cols = lax.broadcasted_iota(jnp.int32, (slots, slots), 1)
        places = [where_is(step * BATCH + u) for u in range(BATCH)]
        takes, shifts = [], []
        for u, (base, head, count) in enumerate(places):
            picks = shifted_picks(picks_v[pl.ds(step * BATCH + u, 1), :], head, count)
            takes.append((patch_row == picks).astype(f32).astype(bf16))
            shifts.append(((rows - cols == head) & (cols < count)).astype(f32).astype(bf16))
        takes = [take.T for take in takes]
        x_wins, g_wins = [], []
        for u in range(BATCH):
            at = (step - third * landing) * BATCH + u
            field = qkv_v[pl.ds(pl.multiple_of(at * patch_rows, patch_rows), patch_rows), cut[third]]
            x_wins.append(mm(takes[u], field).astype(bf16))
        for u in range(BATCH):
            at = step * BATCH + u
            field = qkv_v[pl.ds(pl.multiple_of(at * slots, slots), slots), cut[2]]
            g_wins.append(mm(shifts[u], field).astype(bf16))
        for (base, head, _), x_win, g_win in zip(places, x_wins, g_wins):
            merge_store(x_v, base, head, x_win)
            merge_store(g_v, base, head, g_win)
        return carry

    for third in range(steps // landing):
        lax.fori_loop(third * landing, (third + 1) * landing, functools.partial(pack, third), 0)
    x_v[pl.ds(tail, ROWS), :] = jnp.zeros((ROWS, width), bf16)
    g_v[pl.ds(tail, ROWS), :] = jnp.zeros((ROWS, width), bf16)

    def window_copy(f, src, dst, kind):
        base, _, _ = where_is(f)
        return pltpu.make_async_copy(src.at[pl.ds(base, slots)], dst.at[f], window_sems.at[kind])

    def finished(i, f):
        base, _, _ = where_is(jnp.minimum(f, fields - 1))
        return (f < fields) & (base + slots <= (i + 1) * ROWS)

    def project(i, sent):
        rows = pl.ds(pl.multiple_of(i * ROWS, ROWS), ROWS)
        unit, _ = row_norm(x_v[rows, :].astype(f32))
        mix_v[rows, :] = unit.astype(bf16)
        normed = (unit * row(gain_attn) + row(shift_attn)).astype(bf16)
        query = mm(normed, w_qkv[:, cut[0]]) + row(b_query)
        qkv_v[rows, cut[0]] = (query * HEAD**-0.5).astype(bf16)
        qkv_v[rows, cut[1]] = mm(normed, w_qkv[:, cut[1]]).astype(bf16)
        qkv_v[rows, cut[2]] = (mm(normed, w_qkv[:, cut[2]]) + row(b_value)).astype(bf16)

        def send(f):
            window_copy(f, mix_v, unit_out, 4).start()
            window_copy(f, x_v, x_out, 5).start()
            return f + 1

        return lax.while_loop(functools.partial(finished, i), send, sent)

    lax.fori_loop(0, blocks, project, 0)
    pltpu.make_async_copy(unit_out, unit_out, window_sems.at[4]).wait()

    def probs_copy(i):
        slot = lax.rem(i, 2)
        return pltpu.make_async_copy(
            probs_v.at[slot], probs_out.at[pl.ds(i * AHEAD, AHEAD)], probs_sems.at[slot]
        )

    def attend(i, carry):
        slot = lax.rem(i, 2)

        @pl.when(i >= 2)
        def _():
            probs_copy(i - 2).wait()

        for u in range(AHEAD):
            window_copy(i * AHEAD + u, qkv_v, qkv_out, 0).start()
        places = [where_is(i * AHEAD + u) for u in range(AHEAD)]
        windows = [pl.ds(base, slots) for base, _, _ in places]
        scores = []
        for window in windows:
            stacked = block_heads(qkv_v[window, 0:width], mask_v)
            scores.append(heads_dot(qkv_v[window, width : 2 * width], stacked))
        weights = []
        for (_, head, count), score in zip(places, scores):
            slot_row = lax.broadcasted_iota(jnp.int32, score.shape, 0)
            live = (slot_row >= head) & (slot_row < head + count)
            score = jnp.where(live, score, FILL)
            expo = jnp.exp(score - jnp.max(score, axis=0, keepdims=True))
            total_row = jnp.sum(expo, axis=0, keepdims=True)
            weights.append((expo * (1.0 / total_row)).astype(bf16))
        for u, weight in enumerate(weights):
            probs_v[slot, u] = weight
        turned = [pairs_t(weight) for weight in weights]
        mixed = [
            heads_out_t(weight, qkv_v[window, 2 * width : 3 * width]).astype(bf16)
            for weight, window in zip(turned, windows)
        ]
        for (base, head, _), out in zip(places, mixed):
            merge_store(mix_v, base, head, out)
        probs_copy(i).start()
        return carry

    steps = fields // AHEAD
    lax.fori_loop(0, steps, attend, 0)
    probs_copy(steps - 2).wait()
    probs_copy(steps - 1).wait()
    mix_v[pl.ds(tail, ROWS), :] = jnp.zeros((ROWS, width), bf16)

    def act_copy(i):
        rows = pl.ds(pl.multiple_of(i * ROWS, ROWS), ROWS)
        slot = lax.rem(i, 2)
        return pltpu.make_async_copy(act_v.at[slot], act_out.at[rows], act_sems.at[slot])

    def base_copy(i):
        rows = pl.ds(pl.multiple_of(i * ROWS, ROWS), ROWS)
        return pltpu.make_async_copy(x_v.at[rows], base_out.at[rows], base_sems.at[i])

    def feed(i, sent):
        rows = pl.ds(pl.multiple_of(i * ROWS, ROWS), ROWS)
        slot = lax.rem(i, 2)

        @pl.when(i >= 2)
        def _():
            act_copy(i - 2).wait()

        mixed = mix_v[rows, :]
        grad_b = g_v[rows, :]
        grad = grad_b.astype(f32)
        residual = x_v[rows, :].astype(f32) + (mm(mixed, w_out[...]) + row(b_out))
        unit, rstd = row_norm(residual)
        normed = (unit * row(gain_mlp) + row(shift_mlp)).astype(bf16)
        normed_t = normed.T
        grad_t = grad_b.T
        for at in range(0, hidden, CHUNK):
            cols = slice(at, at + CHUNK)
            up = mm(normed, w_up[:, cols]) + row(b_up, cols)
            d_act = mm_nt(grad_b, w_down[cols, :])
            cdf = 0.5 + 0.5 * lax.erf(up * 0.7071067811865476)
            pdf = 0.3989422804014327 * jnp.exp(-0.5 * up * up)
            act_v[slot, :, cols] = (up * cdf).astype(bf16)
            d_up = d_act * (cdf + up * pdf)
            dup_v[:, cols] = d_up.astype(bf16)
            gb_up[:, cols] += fold(d_up)
        act_copy(i).start()
        d_normed = mm_nt(dup_v[...], w_up[...])
        add_blocks(sums, up_at, mm(normed_t, dup_v[...]))
        add_blocks(sums, down_at, mm(grad_t, act_v[slot]))
        x_v[rows, :] = (residual + row(b_down)).astype(bf16)
        base_copy(i).start()
        gb_down[...] += fold(grad)
        gg_mlp[...] += fold(d_normed * unit)
        gs_mlp[...] += fold(d_normed)
        d_residual = grad + norm_back(d_normed * row(gain_mlp), unit, rstd)
        d_att = d_residual.astype(bf16)
        gb_out[...] += fold(d_residual)
        add_blocks(sums, out_at, mm_tn(mixed, d_att))
        g_v[rows, :] = d_att
        mix_v[rows, :] = mm_nt(d_att, w_out[...]).astype(bf16)

        def send(f):
            window_copy(f, g_v, att_out, 1).start()
            window_copy(f, mix_v, mix_out, 2).start()
            return f + 1

        return lax.while_loop(functools.partial(finished, i), send, sent)

    pltpu.make_async_copy(x_out, x_out, window_sems.at[5]).wait()
    lax.fori_loop(0, blocks, feed, 0)
    at = vector_at
    for partial in (gb_up, gb_down, gb_out, gg_mlp, gs_mlp):
        at = add_vector(sums, at, partial[...])

    lax.fori_loop(jnp.maximum(blocks - 2, 0), blocks, lambda i, c: act_copy(i).wait(), None)
    lax.fori_loop(0, blocks, lambda i, c: base_copy(i).wait(), None)
    for kind, ref in enumerate((qkv_out, att_out, mix_out)):
        pltpu.make_async_copy(ref, ref, window_sems.at[kind]).wait()


FIRST_IN_ATTEND = (1, 2, 4, 5, 6, 7)
FIRST_IN_PROJECT = (1, 2, 4, 6)
SECOND_IN_PROJECT = (0, 1, 3, 5, 7)


def backward_kernel(
    orders_a, orders_b, fields, slots, width,
    counts, starts, qkv, probs, mix, unit, att, x_in, base, act, sums_a,
    w_qkv, gain_attn, shift_attn, w_down,
    d_in, enc, out_a, out_b,
    packed_v, mask_v, gb_qkv, total_a, total_b, load_sem, store_sems,
    sent_a, got_a, summed_a, send_a, recv_a, sent_b, got_b, summed_b, send_b, recv_b,
):
    first = Reducer(orders_a, total_a.shape[0], total_a, sent_a, got_a, summed_a, send_a, recv_a)
    second = Reducer(orders_b, total_b.shape[0], total_b, sent_b, got_b, summed_b, send_b, recv_b)
    load = pltpu.make_async_copy(sums_a, total_a, load_sem)
    load.start()
    steps = fields // UNROLL
    rows = UNROLL * slots

    first.greet(first.partners() | second.partners())
    fill_mask(mask_v)
    total_b[...] = jnp.zeros_like(total_b)
    gb_qkv[...] = jnp.zeros_like(gb_qkv)

    def at_step(step, reducer, ahead, begin):
        for k, when in enumerate(ahead):

            @pl.when(step == when)
            def _(k=k):
                reducer.advance(begin + k)

    def field_rows(step, u):
        return pl.ds(pl.multiple_of((step * UNROLL + u) * slots, slots), slots)

    def here(step):
        return pl.ds(pl.multiple_of(step * rows, rows), rows)

    def attend(qkv_b, probs_b, mix_b, unit_b):
        step = pl.program_id(0)

        @pl.when(step == FIRST_IN_ATTEND[0])
        def _():
            load.wait()

        at_step(step, first, FIRST_IN_ATTEND, 0)
        grads = []
        for u in range(UNROLL):
            f = step * UNROLL + u
            head = lax.rem(starts[f], TILE)
            slot_row = lax.broadcasted_iota(jnp.int32, (slots, width), 0)
            live = (slot_row >= head) & (slot_row < head + counts[f])
            grads.append(block_heads(mix_b[u] * live.astype(f32).astype(bf16), mask_v))
        d_probs = [heads_dot(qkv_b[u, :, 2 * width :], grads[u]) for u in range(UNROLL)]
        for u in range(UNROLL):
            packed_v[field_rows(step, u), 2 * width :] = heads_out(probs_b[u], grads[u]).astype(bf16)
        d_scores = []
        for u in range(UNROLL):
            weights = probs_b[u].astype(f32)
            weighted = weights * d_probs[u]
            inner = jnp.sum(weighted, axis=0, keepdims=True)
            d_scores.append((weighted - weights * inner).astype(bf16))
        for u in range(UNROLL):
            query = block_heads(qkv_b[u, :, :width], mask_v)
            packed_v[field_rows(step, u), width : 2 * width] = heads_out(d_scores[u], query).astype(bf16)
        turned = [pairs_t(d_score) for d_score in d_scores]
        for u in range(UNROLL):
            d_query = heads_out_t(turned[u], qkv_b[u, :, width : 2 * width])
            packed_v[field_rows(step, u), :width] = (d_query * HEAD**-0.5).astype(bf16)
        grad = packed_v[here(step), :]
        add_blocks(total_b, 0, mm_tn(unit_b[...].reshape(rows, width), grad))
        gb_qkv[...] += fold(grad.astype(f32))

    def block(*shape):
        return pl.BlockSpec((UNROLL,) + shape, lambda i: (i, 0, 0))

    pltpu.emit_pipeline(
        attend,
        grid=(steps,),
        in_specs=[block(slots, 3 * width)] + [block(slots, width)] * 3,
    )(qkv, probs, mix, unit)

    at = 3 * width * width // LANES
    add_vector(total_b, at, gb_qkv[...])
    grad_sum = jnp.sum(gb_qkv[...], axis=0, keepdims=True)
    gain = jnp.broadcast_to(row(gain_attn), (LANES, width)).T
    shift = jnp.broadcast_to(row(shift_attn), (LANES, width)).T
    gain_sum = jnp.zeros((width, LANES), f32)
    shift_sum = jnp.zeros((width, LANES), f32)
    for k in range(3 * width // LANES):
        at_rows = pl.ds(k * width, width)
        cols = slice(k * LANES, (k + 1) * LANES)
        weight = w_qkv[:, cols].astype(f32)
        part = total_b[at_rows, :]
        column = jnp.broadcast_to(grad_sum[:, cols], (width, LANES))
        gain_sum += weight * part
        shift_sum += weight * column
        total_b[at_rows, :] = gain * part + shift * column
    at += 3 * width // LANES
    at = add_vector(total_b, at, gain_sum.T)
    add_vector(total_b, at, shift_sum.T)

    less = PART // SPLIT

    def project(x_b, att_b, act_b, base_b, d_in_b, enc_b):
        step = pl.program_id(0)
        at_step(step, second, SECOND_IN_PROJECT, 0)
        at_step(step, first, FIRST_IN_PROJECT, len(FIRST_IN_ATTEND))
        grads, downs = {}, {}
        for k in range(rows // PART + 1):
            if k < rows // PART:
                at = pl.multiple_of(step * rows + k * PART, PART)
                grads[k] = mm_nt(packed_v[pl.ds(at, PART), :], w_qkv[...])
                downs[k] = mm(act_b[k * less : (k + 1) * less, :], w_down[...])
            if k:
                part = pl.ds((k - 1) * PART, PART)
                unit, rstd = row_norm(x_b[part, :].astype(f32))
                d_x = norm_back(grads.pop(k - 1) * row(gain_attn), unit, rstd)
                d_in_b[part, :] = (att_b[part, :].astype(f32) + d_x).astype(bf16)
                part = pl.ds((k - 1) * less, less)
                enc_b[part, :] = (base_b[part, :].astype(f32) + downs.pop(k - 1)).astype(bf16)

    narrow = pl.BlockSpec((rows, width), lambda i: (i, 0))
    short = pl.BlockSpec((rows // SPLIT, width), lambda i: (i, 0))
    pltpu.emit_pipeline(
        project,
        grid=(steps,),
        in_specs=[
            narrow, narrow, pl.BlockSpec((rows // SPLIT, act.shape[1]), lambda i: (i, 0)), short,
        ],
        out_specs=[narrow, short],
    )(x_in, att, act, base, d_in, enc)

    for k in range(len(FIRST_IN_ATTEND) + len(FIRST_IN_PROJECT), first.steps):
        first.advance(k)
    store_a = pltpu.make_async_copy(summed_a, out_a, store_sems.at[0])
    store_a.start()
    for k in range(len(SECOND_IN_PROJECT), second.steps):
        second.advance(k)
    store_b = pltpu.make_async_copy(summed_b, out_b, store_sems.at[1])
    store_b.start()
    store_a.wait()
    store_b.wait()


def unblock(src, at, dst):
    rows, columns = dst.shape
    for k in range(columns // LANES):
        dst[:, k * LANES : (k + 1) * LANES] = src[pl.ds(at + k * rows, rows), :].astype(f32)


def unblock_t(src, at, dst):
    rows, columns = dst.shape
    for k in range(rows // LANES):
        part = src[pl.ds(at + k * columns, columns), :].astype(f32)
        dst[k * LANES : (k + 1) * LANES, :] = part.T


def unblock_vector(src, at, dst):
    (columns,) = dst.shape
    for k in range(columns // LANES):
        dst[k * LANES : (k + 1) * LANES] = src[pl.ds(at + k, 1), :].astype(f32).reshape(LANES)


def unpack_kernel(
    fields, slots, width, hidden,
    counts, starts, visible, d_in, enc, base, act, w_down_in, sums_a, sums_b,
    encoded, input_grad, w_qkv, b_query, b_value, w_out, b_out, w_up, b_up, w_down, b_down,
    gain_attn, shift_attn, gain_mlp, shift_mlp,
    picks_v, d_in_v, enc_v, out_v, grad_v, act_v, qkv_v, up_v, down_v, sems, weight_sems,
):
    up_at, down_at, out_at, at = sum_rows(width, hidden)
    steps = fields // GROUP

    def group(step):
        return pl.ds(step * GROUP, GROUP)

    def enc_load(src, step):
        rows = pl.ds(pl.multiple_of(step * GROUP * slots, GROUP * slots), GROUP * slots)
        return pltpu.make_async_copy(src.at[rows], enc_v.at[rows], sems.at[1, step])

    early = enc.shape[0] // (GROUP * slots)

    def act_load(step):
        size = GROUP * slots
        src = pl.ds(pl.multiple_of(step * size, size), size)
        dst = pl.ds(pl.multiple_of((step - early) * size, size), size)
        return pltpu.make_async_copy(act.at[src], act_v.at[dst], sems.at[2, step])

    def used(step):
        return step * GROUP * slots < starts[fields - 1] + slots

    def loads(step):
        rows = pl.ds(pl.multiple_of(step * GROUP * slots, GROUP * slots), GROUP * slots)
        return (
            pltpu.make_async_copy(d_in.at[rows], d_in_v.at[rows], sems.at[0, step]),
        )

    def stores(step):
        return (
            pltpu.make_async_copy(out_v.at[group(step)], encoded.at[group(step)], sems.at[1, step]),
            pltpu.make_async_copy(grad_v.at[group(step)], input_grad.at[group(step)], sems.at[0, step]),
        )

    def start_loads(step, carry):
        for copy in loads(step):
            copy.start()

        @pl.when(step < early)
        def _():
            enc_load(enc, step).start()

        @pl.when((step >= early) & used(step))
        def _():
            enc_load(base, step).start()
            act_load(step).start()

        return carry

    def wait_stores(step, carry):
        for copy in stores(step):
            copy.wait()
        return carry

    def unpack(step, carry):
        for copy in loads(step):
            copy.wait()

        @pl.when(step < early)
        def _():
            enc_load(enc, step).wait()

        @pl.when((step >= early) & used(step))
        def _():
            enc_load(base, step).wait()
            act_load(step).wait()
            size = GROUP * slots
            here = pl.ds(pl.multiple_of(step * size, size), size)
            late = pl.ds(pl.multiple_of((step - early) * size, size), size)
            last = enc_v[here, :].astype(f32) + mm(act_v[late, :], w_down_in[...])
            enc_v[here, :] = last.astype(bf16)

        patch_row = lax.broadcasted_iota(jnp.int32, (input_grad.shape[1], slots), 0)
        rows = lax.broadcasted_iota(jnp.int32, (slots, slots), 0)
        cols = lax.broadcasted_iota(jnp.int32, (slots, slots), 1)
        puts, shifts = [], []
        for u in range(GROUP):
            f = step * GROUP + u
            head, count = lax.rem(starts[f], TILE), counts[f]
            picks = shifted_picks(picks_v[pl.ds(f, 1), :], head, count)
            puts.append((patch_row == picks).astype(f32).astype(bf16))
            shifts.append(((cols - rows == head) & (rows < count)).astype(f32).astype(bf16))
        for u in range(GROUP):
            f = step * GROUP + u
            window = pl.ds(pl.multiple_of(f * slots, slots), slots)
            grad_v[f] = mm(puts[u], d_in_v[window, :]).astype(bf16)
            at = pl.multiple_of(starts[f] - lax.rem(starts[f], TILE), TILE)
            out_v[f] = mm(shifts[u], enc_v[pl.ds(at, slots), :]).astype(bf16)
        for copy in stores(step):
            copy.start()
        return carry

    lax.fori_loop(0, steps, start_loads, 0)
    picks_v[...] = visible[...].T
    copies = []
    unblock(sums_a, up_at, up_v)
    copies.append(pltpu.make_async_copy(up_v, w_up, weight_sems.at[0]))
    copies[0].start()
    unblock_t(sums_a, down_at, down_v)
    copies.append(pltpu.make_async_copy(down_v, w_down, weight_sems.at[1]))
    copies[1].start()
    unblock(sums_b, 0, qkv_v)
    copies.append(pltpu.make_async_copy(qkv_v, w_qkv, weight_sems.at[2]))
    copies[2].start()
    unblock(sums_a, out_at, w_out)
    for ref in (b_up, b_down, b_out, gain_mlp, shift_mlp):
        unblock_vector(sums_a, at, ref)
        at += ref.shape[0] // LANES
    at = 3 * width * width // LANES
    for ref, rows in ((b_query, 2), (b_value, 1), (gain_attn, 1), (shift_attn, 1)):
        unblock_vector(sums_b, at, ref)
        at += rows * width // LANES
    lax.fori_loop(0, steps, unpack, 0)
    lax.fori_loop(0, steps, wait_stores, 0)
    for copy in copies:
        copy.wait()


def forward(sizes, args):
    (
        patches, visible, counts, upstream, w_qkv, b_query, b_value, w_out, b_out,
        w_up, b_up, w_down, b_down, gain_attn, shift_attn, gain_mlp, shift_mlp,
    ) = args
    fields, _, width = patches.shape
    slots, hidden = visible.shape[1], w_up.shape[1]
    cap = (fields * slots + ROWS - 1) // ROWS * ROWS
    tall = cap + ROWS
    vectors = (hidden + 4 * width) // LANES
    rows_a = padded_rows(sum_rows(width, hidden)[3] + vectors, sizes)
    shape = jax.ShapeDtypeStruct
    hbm = pl.BlockSpec(memory_space=pl.ANY)
    vmem = pl.BlockSpec(memory_space=pltpu.VMEM)
    smem = pl.BlockSpec(memory_space=pltpu.SMEM)
    windows = shape((fields, slots, width), bf16)
    return pl.pallas_call(
        functools.partial(forward_kernel, fields, slots, width, hidden),
        out_shape=[
            shape((fields,), jnp.int32),
            windows,
            windows,
            shape((fields, slots, 3 * width), bf16),
            windows,
            windows,
            windows,
            shape((cap, width), bf16),
            shape((cap, hidden), bf16),
            shape((rows_a, LANES), f32),
        ],
        in_specs=[smem, hbm, vmem, hbm] + [vmem] * 13,
        out_specs=[smem] + [hbm] * 8 + [vmem],
        scratch_shapes=[
            pltpu.VMEM((tall, width), bf16),
            pltpu.VMEM((tall, width), bf16),
            pltpu.VMEM((cap, 3 * width), bf16),
            pltpu.VMEM((tall, width), bf16),
            pltpu.VMEM((2, AHEAD, slots, width), bf16),
            pltpu.VMEM((2, ROWS, hidden), bf16),
            pltpu.VMEM((ROWS, hidden), bf16),
            pltpu.VMEM((4 * HEAD, 4 * HEAD), bf16),
            pltpu.VMEM((fields, slots), jnp.int32),
            pltpu.VMEM((8, hidden), f32),
            pltpu.VMEM((8, width), f32),
            pltpu.VMEM((8, width), f32),
            pltpu.VMEM((8, width), f32),
            pltpu.VMEM((8, width), f32),
            pltpu.SemaphoreType.DMA((6,)),
            pltpu.SemaphoreType.DMA((2,)),
            pltpu.SemaphoreType.DMA((2, fields // BATCH)),
            pltpu.SemaphoreType.DMA((2,)),
            pltpu.SemaphoreType.DMA((cap // ROWS,)),
        ],
        compiler_params=pltpu.CompilerParams(vmem_limit_bytes=VMEM_BYTES),
        name="forward_rows",
    )(
        counts, patches.reshape(-1, width), visible.T, upstream.reshape(-1, width),
        w_qkv, b_query, b_value, w_out, b_out, w_up, b_up, w_down, b_down, gain_attn, shift_attn, gain_mlp, shift_mlp,
    )


def backward(
    sizes, counts, starts, qkv, probs, mix, unit, att, x_rows, base, act, sums_a,
    w_qkv, gain, shift, w_down,
):
    fields, slots, width = mix.shape
    orders_a, orders_b = exchange_orders(sizes), direct_orders(sizes)
    rows_b = padded_rows((3 * width * width + 5 * width) // LANES, sizes)
    shape = jax.ShapeDtypeStruct
    hbm = pl.BlockSpec(memory_space=pl.ANY)
    vmem = pl.BlockSpec(memory_space=pltpu.VMEM)
    smem = pl.BlockSpec(memory_space=pltpu.SMEM)
    return pl.pallas_call(
        functools.partial(backward_kernel, orders_a, orders_b, fields, slots, width),
        out_shape=[
            shape((fields * slots, width), bf16),
            shape((act.shape[0] // SPLIT, width), bf16),
            shape(sums_a.shape, bf16),
            shape((rows_b, LANES), bf16),
        ],
        in_specs=[smem, smem] + [hbm] * 9 + [vmem] * 4,
        out_specs=[hbm] * 4,
        scratch_shapes=[
            pltpu.VMEM((fields * slots, 3 * width), bf16),
            pltpu.VMEM((4 * HEAD, 4 * HEAD), bf16),
            pltpu.VMEM((8, 3 * width), f32),
            pltpu.VMEM(sums_a.shape, f32),
            pltpu.VMEM((rows_b, LANES), f32),
            pltpu.SemaphoreType.DMA,
            pltpu.SemaphoreType.DMA((2,)),
        ]
        + reducer_scratch(sums_a.shape[0], orders_a)
        + reducer_scratch(rows_b, orders_b),
        compiler_params=pltpu.CompilerParams(
            collective_id=0, has_side_effects=True, vmem_limit_bytes=VMEM_BYTES
        ),
        name="backward_rows",
    )(
        counts, starts, qkv, probs, mix, unit, att.reshape(-1, width), x_rows.reshape(-1, width),
        base, act, sums_a, w_qkv, gain, shift, w_down,
    )


def unpack_all(
    counts, starts, visible, d_in, enc, base, act, w_down, sums_a, sums_b, patch_rows, hidden
):
    (slots, fields), width = visible.shape, d_in.shape[1]
    shape = jax.ShapeDtypeStruct
    hbm = pl.BlockSpec(memory_space=pl.ANY)
    vmem = pl.BlockSpec(memory_space=pltpu.VMEM)
    smem = pl.BlockSpec(memory_space=pltpu.SMEM)
    vector = shape((width,), f32)
    return pl.pallas_call(
        functools.partial(unpack_kernel, fields, slots, width, hidden),
        out_shape=[
            shape((fields, slots, width), bf16),
            shape((fields, patch_rows, width), bf16),
            shape((width, 3 * width), f32), vector, vector,
            shape((width, width), f32), vector,
            shape((width, hidden), f32), shape((hidden,), f32),
            shape((hidden, width), f32), vector,
            vector, vector, vector, vector,
        ],
        in_specs=[smem, smem, vmem] + [hbm] * 4 + [vmem] * 3,
        out_specs=[hbm] * 3 + [vmem] * 4 + [hbm, vmem, hbm] + [vmem] * 5,
        scratch_shapes=[
            pltpu.VMEM((fields, slots), jnp.int32),
            pltpu.VMEM(d_in.shape, bf16),
            pltpu.VMEM(base.shape, bf16),
            pltpu.VMEM((fields, slots, width), bf16),
            pltpu.VMEM((fields, patch_rows, width), bf16),
            pltpu.VMEM((base.shape[0] - enc.shape[0], hidden), bf16),
            pltpu.VMEM((width, 3 * width), f32),
            pltpu.VMEM((width, hidden), f32),
            pltpu.VMEM((hidden, width), f32),
            pltpu.SemaphoreType.DMA((3, fields // GROUP)),
            pltpu.SemaphoreType.DMA((3,)),
        ],
        compiler_params=pltpu.CompilerParams(vmem_limit_bytes=VMEM_BYTES),
        name="unpack_rows",
    )(counts, starts, visible, d_in, enc, base, act, w_down, sums_a, sums_b)


def per_device(sizes, *args):
    patches, visible, counts = args[:3]
    w_qkv, w_up, gain_attn, shift_attn = args[4], args[9], args[13], args[14]
    starts, x_rows, unit, qkv, probs, att, mix, base, act, sums_a = forward(sizes, args)
    d_in, enc, total_a, total_b = backward(
        sizes, counts, starts, qkv, probs, mix, unit, att, x_rows, base, act, sums_a,
        w_qkv, gain_attn, shift_attn, args[11],
    )
    return tuple(
        unpack_all(
            counts, starts, visible.T, d_in, enc, base, act, args[11], total_a, total_b, patches.shape[1], w_up.shape[1]
        )
    )


def solution(mesh):
    rows = P(("wide", "narrow"))
    return jax.shard_map(
        functools.partial(per_device, dict(mesh.shape)),
        mesh=mesh,
        in_specs=(rows,) * 4 + (P(),) * 13,
        out_specs=(rows,) * 2 + (P(),) * 13,
        check_vma=False,
    )
```

```python
import functools

import jax
import jax.numpy as jnp
from jax import lax
from jax.experimental import pallas as pl
from jax.experimental.pallas import tpu as pltpu
from jax.sharding import PartitionSpec as P

HEAD = 64
EPS = 1e-06
FILL = -1e30
ROWS = 512
TILE = 16
UNROLL = 16
AHEAD = 16
GROUP = 8
BATCH = 16
PIECES = 4
PART = 256
SPLIT = 2
CHUNK = 256
VMEM_BYTES = 60 * 1024 * 1024
f32 = jnp.float32
bf16 = jnp.bfloat16


LANES = 128


def mm(left, right):
    return lax.dot_general(left, right, (((1,), (0,)), ((), ())), preferred_element_type=f32)


def mm_nt(left, right):
    return lax.dot_general(left, right, (((1,), (1,)), ((), ())), preferred_element_type=f32)


def mm_tn(left, right):
    return lax.dot_general(left, right, (((0,), (0,)), ((), ())), preferred_element_type=f32)


def row_norm(values):
    width = values.shape[-1]
    mean = jnp.sum(values, axis=-1, keepdims=True) * (1.0 / width)
    centered = values - mean
    variance = jnp.sum(centered * centered, axis=-1, keepdims=True) * (1.0 / width)
    rstd = lax.rsqrt(variance + EPS)
    return centered * rstd, rstd


def norm_back(grad, unit, rstd):
    width = grad.shape[-1]
    first = jnp.sum(grad, axis=-1, keepdims=True) * (1.0 / width)
    second = jnp.sum(grad * unit, axis=-1, keepdims=True) * (1.0 / width)
    return (grad - first - unit * second) * rstd


def fold(values):
    rows, width = values.shape
    return jnp.sum(values.reshape(rows // 8, 8, width), axis=0)


def fill_mask(mask):
    row = lax.broadcasted_iota(jnp.int32, mask.shape, 0) // HEAD
    col = lax.broadcasted_iota(jnp.int32, mask.shape, 1) // HEAD
    mask[...] = (row == col).astype(f32).astype(bf16)


def head_parts(width):
    parts, at = [], 0
    while at < width:
        size = min(4 * HEAD, width - at)
        parts.append((at, size))
        at += size
    return parts


def block_heads(values, mask):
    blocks = []
    for at, size in head_parts(values.shape[1]):
        tiled = jnp.concatenate([values[:, at : at + size]] * (size // HEAD), axis=0)
        blocks.append(tiled * mask[:size, :size])
    return blocks


def heads_dot(left, stacked):
    parts = [
        mm_nt(left[:, at : at + size], block)
        for (at, size), block in zip(head_parts(left.shape[1]), stacked)
    ]
    return jnp.concatenate(parts, axis=1)


def heads_out(left, stacked):
    parts = [
        mm(left[:, at : at + size], block)
        for (at, size), block in zip(head_parts(left.shape[1]), stacked)
    ]
    return jnp.concatenate(parts, axis=1)


def heads_out_t(weights, values):
    window = weights[0].shape[0] // 2
    parts = []
    for k, at in enumerate(range(0, values.shape[1], 2 * HEAD)):
        pair = mm(weights[k], values[:, at : at + 2 * HEAD])
        lane = lax.broadcasted_iota(jnp.int32, (window, 2 * HEAD), 1)
        parts.append(jnp.where(lane < HEAD, pair[:window], pair[window:]))
    return jnp.concatenate(parts, axis=1)


def pairs_t(values):
    return [values[:, at : at + 2 * HEAD].T for at in range(0, values.shape[1], 2 * HEAD)]


def start_all(pairs, sems):
    copies = [
        pltpu.make_async_copy(src, dst, sems.at[k]) for k, (src, dst) in enumerate(pairs)
    ]
    for copy in copies:
        copy.start()
    return copies


def add_blocks(sums, at, values):
    rows = values.shape[0]
    for k in range(values.shape[1] // LANES):
        block = pl.ds(at + k * rows, rows)
        sums[block, :] += values[:, k * LANES : (k + 1) * LANES]


def add_vector(sums, at, partial):
    vector = jnp.sum(partial, axis=0, keepdims=True)
    for k in range(vector.shape[1] // LANES):
        sums[pl.ds(at + k, 1), :] = vector[:, k * LANES : (k + 1) * LANES]
    return at + vector.shape[1] // LANES


def row(ref, cols=slice(None)):
    return ref[cols].reshape(1, -1)


def shifted_picks(vis, head, count):
    slots = vis.shape[1]
    lane = lax.broadcasted_iota(jnp.int32, vis.shape, 1)
    live = jnp.where(lane < count, vis, -1)
    wide = jnp.concatenate([live, jnp.full((1, LANES - slots), -1, jnp.int32)], axis=1)
    return pltpu.roll(wide, head, axis=1)[:, :slots]


def merge_store(ref, base, head, window):
    old = ref[pl.ds(base, TILE), :]
    row = lax.broadcasted_iota(jnp.int32, (TILE, window.shape[1]), 0)
    ref[pl.ds(base, TILE), :] = jnp.where(row >= head, window[:TILE], old)
    rest = window.shape[0] - TILE
    ref[pl.ds(base + TILE, rest), :] = window[TILE:]


def mesh_bits(sizes):
    wide = [("wide", 1 << k) for k in range(sizes["wide"].bit_length() - 1)]
    narrow = [("narrow", 1 << k) for k in range(sizes["narrow"].bit_length() - 1)]
    return wide, narrow


def exchange_orders(sizes):
    wide, narrow = mesh_bits(sizes)
    first, last = narrow[:1], wide[-1:]
    middle = wide[:1] + narrow[1:] + wide[1:-1]
    orders = [first + middle[k:] + middle[:k] + last for k in range(min(3, len(middle)))]
    return [[(pair,) for pair in order] for order in orders]


def direct_orders(sizes):
    wide, narrow = mesh_bits(sizes)
    plane, line = tuple(wide[:1] + narrow[1:]), tuple(wide[1:])
    return [[tuple(narrow[:1]), plane, line], [tuple(narrow[:1]), line, plane]]


def members(group):
    return [
        tuple(pair for k, pair in enumerate(group) if mask >> k & 1)
        for mask in range(1, 1 << len(group))
    ]


def rows_of_parts(rows, orders):
    unit = TILE << sum(len(group) for group in orders[0])
    units, parts, at = rows // unit, [], 0
    for k in range(len(orders)):
        share = (units + len(orders) - 1 - k) // len(orders) * unit
        if share:
            parts.append((at, share))
        at += share
    return parts


class Reducer:
    def __init__(self, orders, rows, total, sent, got, summed, send_sems, recv_sems):
        self.orders, self.total, self.sent, self.got, self.summed = orders, total, sent, got, summed
        self.send_sems, self.recv_sems = send_sems, recv_sems
        self.stages = len(orders[0])
        self.parts = rows_of_parts(rows, orders)
        self.sides = {}
        for group in orders[0]:
            for axis, distance in group:
                self.sides[axis, distance] = lax.rem(lax.axis_index(axis) // distance, 2)
        self.bases, self.sizes = [], []
        for order, (base, size) in zip(orders, self.parts):
            bases, sizes = [base], [size]
            for group in order:
                sizes.append(sizes[-1] >> len(group))
                bases.append(bases[-1] + self.place(group) * sizes[-1])
            self.bases.append(bases)
            self.sizes.append(sizes)

    def place(self, group, flipped=()):
        place = 0
        for k, pair in enumerate(group):
            side = self.sides[pair]
            place = place + (1 << k) * (1 - side if pair in flipped else side)
        return place

    def device(self, flipped):
        other = {}
        for axis, distance in flipped:
            mine = other.get(axis, lax.axis_index(axis))
            other[axis] = mine + distance * (1 - 2 * self.sides[axis, distance])
        return other

    def partners(self):
        return {flipped for order in self.orders for group in order for flipped in members(group)}

    def greet(self, partners):
        barrier = pltpu.get_barrier_semaphore()
        for flipped in sorted(partners):
            pl.semaphore_signal(
                barrier, inc=1, device_id=self.device(flipped), device_id_type=pl.DeviceIdType.MESH
            )
        pl.semaphore_wait(barrier, len(partners))

    def flights(self, part, stage):
        summing = stage < self.stages
        level = stage if summing else 2 * self.stages - 1 - stage
        group = self.orders[part][level]
        size = self.sizes[part][level + 1]
        base, share = self.parts[part]
        for k, flipped in enumerate(members(group)):
            if summing:
                slot = pl.ds(base + share - self.sizes[part][level] + k * size, size)
                src, dst = self.sent.at[slot], self.got.at[slot]
            else:
                slot = pl.ds(pl.multiple_of(self.bases[part][level + 1], TILE), size)
                src = dst = self.summed.at[slot]
            copy = pltpu.make_async_remote_copy(
                src_ref=src, dst_ref=dst,
                send_sem=self.send_sems.at[part, stage, k], recv_sem=self.recv_sems.at[part, stage, k],
                device_id=self.device(flipped), device_id_type=pl.DeviceIdType.MESH,
            )
            yield copy, flipped, slot

    def leave(self, part, stage):
        for copy, flipped, slot in self.flights(part, stage):
            if stage < self.stages:
                size = self.sizes[part][stage + 1]
                at = self.bases[part][stage] + self.place(self.orders[part][stage], flipped) * size
                self.sent[slot, :] = self.total[pl.ds(pl.multiple_of(at, TILE), size), :].astype(bf16)
            copy.start()

    def arrive(self, part, stage):
        flights = list(self.flights(part, stage))
        for copy, _, _ in flights:
            copy.wait()
        if stage < self.stages:
            here = pl.ds(pl.multiple_of(self.bases[part][stage + 1], TILE), self.sizes[part][stage + 1])
            value = self.total[here, :]
            for _, _, slot in flights:
                value = value + self.got[slot, :].astype(f32)
            if stage + 1 < self.stages:
                self.total[here, :] = value
            else:
                self.summed[here, :] = value.astype(bf16)

    def advance(self, stage):
        for part in range(len(self.parts)):
            if stage:
                self.arrive(part, stage - 1)
            if stage < 2 * self.stages:
                self.leave(part, stage)

    @property
    def steps(self):
        return 2 * self.stages + 1


def padded_rows(rows, sizes):
    unit = TILE * sizes["wide"] * sizes["narrow"]
    return (rows + unit - 1) // unit * unit


def reducer_scratch(rows, orders):
    most = max(len(members(group)) for group in orders[0])
    flights = (len(orders), 2 * len(orders[0]), most)
    return [
        pltpu.VMEM((rows, LANES), bf16),
        pltpu.VMEM((rows, LANES), bf16),
        pltpu.VMEM((rows, LANES), bf16),
        pltpu.SemaphoreType.DMA(flights),
        pltpu.SemaphoreType.DMA(flights),
    ]


def sum_rows(width, hidden):
    up, out = width * hidden // LANES, width * width // LANES
    return 0, up, 2 * up, 2 * up + out


def forward_kernel(
    fields, slots, width, hidden,
    counts, patches, visible, upstream,
    w_qkv_hbm, b_query, b_value, w_out_hbm, b_out, w_up_hbm, b_up, w_down_hbm, b_down,
    gain_attn, shift_attn, gain_mlp, shift_mlp,
    starts, x_out, unit_out, qkv_out, probs_out, att_out, mix_out, base_out, act_out, sums,
    x_v, g_v, qkv_v, mix_v, probs_v, act_v, dup_v, mask_v, picks_v,
    gb_up, gb_down, gb_out, gg_mlp, gs_mlp, window_sems, probs_sems, land_sems,
    act_sems, base_sems, w_qkv, w_out, w_up, w_down, weight_sems,
):
    up_at, down_at, out_at, vector_at = sum_rows(width, hidden)
    patch_rows = patches.shape[0] // fields
    steps = fields // BATCH
    landing = qkv_v.shape[0] // (BATCH * patch_rows)
    cut = [slice(k * width, (k + 1) * width) for k in range(3)]

    def arrivals(third, step):
        size = BATCH * patch_rows
        src = pl.ds(pl.multiple_of(step * size, size), size)
        dst = pl.ds(pl.multiple_of((step - third * landing) * size, size), size)
        size = BATCH * slots
        up = pl.ds(pl.multiple_of(step * size, size), size)
        return (
            pltpu.make_async_copy(patches.at[src], qkv_v.at[dst, cut[third]], land_sems.at[0, step]),
            pltpu.make_async_copy(upstream.at[up], qkv_v.at[up, cut[2]], land_sems.at[1, step]),
        )

    def start_arrivals(third, step, carry):
        for copy in arrivals(third, step):
            copy.start()
        return carry

    for third in range(steps // landing):
        lax.fori_loop(
            third * landing, (third + 1) * landing, functools.partial(start_arrivals, third), 0
        )

    weights = start_all(
        ((w_qkv_hbm, w_qkv), (w_out_hbm, w_out), (w_up_hbm, w_up), (w_down_hbm, w_down)), weight_sems
    )

    def place(f, at):
        count = counts[f]
        head = lax.rem(at, TILE)
        at = jnp.where(head + count > slots, at + TILE - head, at)
        starts[f] = at
        return at + count

    lax.fori_loop(0, fields, place, 0)
    last = starts[fields - 1]
    tail = pl.multiple_of(last - lax.rem(last, TILE) + slots, TILE)
    blocks = (tail + ROWS - 1) // ROWS
    for ref in (sums, gb_up, gb_down, gb_out, gg_mlp, gs_mlp):
        ref[...] = jnp.zeros_like(ref)
    fill_mask(mask_v)
    picks_v[...] = visible[...].T

    def where_is(f):
        start = starts[f]
        head = lax.rem(start, TILE)
        return pl.multiple_of(start - head, TILE), head, counts[f]

    def pack(third, step, carry):
        for copy in arrivals(third, step):
            copy.wait()
        patch_row = lax.broadcasted_iota(jnp.int32, (patch_rows, slots), 0)
        rows = lax.broadcasted_iota(jnp.int32, (slots, slots), 0)
        cols = lax.broadcasted_iota(jnp.int32, (slots, slots), 1)
        places = [where_is(step * BATCH + u) for u in range(BATCH)]
        takes, shifts = [], []
        for u, (base, head, count) in enumerate(places):
            picks = shifted_picks(picks_v[pl.ds(step * BATCH + u, 1), :], head, count)
            takes.append((patch_row == picks).astype(f32).astype(bf16))
            shifts.append(((rows - cols == head) & (cols < count)).astype(f32).astype(bf16))
        takes = [take.T for take in takes]
        x_wins, g_wins = [], []
        for u in range(BATCH):
            at = (step - third * landing) * BATCH + u
            field = qkv_v[pl.ds(pl.multiple_of(at * patch_rows, patch_rows), patch_rows), cut[third]]
            x_wins.append(mm(takes[u], field).astype(bf16))
        for u in range(BATCH):
            at = step * BATCH + u
            field = qkv_v[pl.ds(pl.multiple_of(at * slots, slots), slots), cut[2]]
            g_wins.append(mm(shifts[u], field).astype(bf16))
        for (base, head, _), x_win, g_win in zip(places, x_wins, g_wins):
            merge_store(x_v, base, head, x_win)
            merge_store(g_v, base, head, g_win)
        return carry

    for third in range(steps // landing):
        lax.fori_loop(third * landing, (third + 1) * landing, functools.partial(pack, third), 0)
    x_v[pl.ds(tail, ROWS), :] = jnp.zeros((ROWS, width), bf16)
    g_v[pl.ds(tail, ROWS), :] = jnp.zeros((ROWS, width), bf16)

    def window_copy(f, src, dst, kind):
        base, _, _ = where_is(f)
        return pltpu.make_async_copy(src.at[pl.ds(base, slots)], dst.at[f], window_sems.at[kind])

    def finished(i, f):
        base, _, _ = where_is(jnp.minimum(f, fields - 1))
        return (f < fields) & (base + slots <= (i + 1) * ROWS)

    def norm(i, piece):
        size = ROWS // PIECES
        rows = pl.ds(pl.multiple_of(i * ROWS + piece * size, size), size)
        unit, _ = row_norm(x_v[rows, :].astype(f32))
        mix_v[rows, :] = unit.astype(bf16)
        normed = (unit * row(gain_attn) + row(shift_attn)).astype(bf16)
        act_v[lax.rem(i, 2), piece * size : (piece + 1) * size, 0:width] = normed

    def project(i, sent):
        rows = pl.ds(pl.multiple_of(i * ROWS, ROWS), ROWS)
        normed = act_v[lax.rem(i, 2), :, 0:width]
        query = mm(normed, w_qkv[:, cut[0]]) + row(b_query)
        qkv_v[rows, cut[0]] = (query * HEAD**-0.5).astype(bf16)
        norm(i + 1, 0)
        norm(i + 1, 1)
        qkv_v[rows, cut[1]] = mm(normed, w_qkv[:, cut[1]]).astype(bf16)
        norm(i + 1, 2)
        norm(i + 1, 3)
        qkv_v[rows, cut[2]] = (mm(normed, w_qkv[:, cut[2]]) + row(b_value)).astype(bf16)

        def send(f):
            window_copy(f, mix_v, unit_out, 4).start()
            window_copy(f, x_v, x_out, 5).start()
            return f + 1

        return lax.while_loop(functools.partial(finished, i), send, sent)

    for copy in weights:
        copy.wait()
    for piece in range(PIECES):
        norm(0, piece)
    lax.fori_loop(0, blocks, project, 0)
    pltpu.make_async_copy(unit_out, unit_out, window_sems.at[4]).wait()

    def probs_copy(i):
        slot = lax.rem(i, 2)
        return pltpu.make_async_copy(
            probs_v.at[slot], probs_out.at[pl.ds(i * AHEAD, AHEAD)], probs_sems.at[slot]
        )

    def attend(i, carry):
        slot = lax.rem(i, 2)

        @pl.when(i >= 2)
        def _():
            probs_copy(i - 2).wait()

        for u in range(AHEAD):
            window_copy(i * AHEAD + u, qkv_v, qkv_out, 0).start()
        places = [where_is(i * AHEAD + u) for u in range(AHEAD)]
        windows = [pl.ds(base, slots) for base, _, _ in places]
        scores = []
        for window in windows:
            stacked = block_heads(qkv_v[window, 0:width], mask_v)
            scores.append(heads_dot(qkv_v[window, width : 2 * width], stacked))
        weights = []
        for (_, head, count), score in zip(places, scores):
            slot_row = lax.broadcasted_iota(jnp.int32, score.shape, 0)
            live = (slot_row >= head) & (slot_row < head + count)
            score = jnp.where(live, score, FILL)
            expo = jnp.exp(score - jnp.max(score, axis=0, keepdims=True))
            total_row = jnp.sum(expo, axis=0, keepdims=True)
            weights.append((expo * (1.0 / total_row)).astype(bf16))
        for u, weight in enumerate(weights):
            probs_v[slot, u] = weight
        turned = [pairs_t(weight) for weight in weights]
        mixed = [
            heads_out_t(weight, qkv_v[window, 2 * width : 3 * width]).astype(bf16)
            for weight, window in zip(turned, windows)
        ]
        for (base, head, _), out in zip(places, mixed):
            merge_store(mix_v, base, head, out)
        probs_copy(i).start()
        return carry

    steps = fields // AHEAD
    lax.fori_loop(0, steps, attend, 0)
    probs_copy(steps - 2).wait()
    probs_copy(steps - 1).wait()
    mix_v[pl.ds(tail, ROWS), :] = jnp.zeros((ROWS, width), bf16)

    def act_copy(i):
        rows = pl.ds(pl.multiple_of(i * ROWS, ROWS), ROWS)
        slot = lax.rem(i, 2)
        return pltpu.make_async_copy(act_v.at[slot], act_out.at[rows], act_sems.at[slot])

    def base_copy(i):
        rows = pl.ds(pl.multiple_of(i * ROWS, ROWS), ROWS)
        return pltpu.make_async_copy(x_v.at[rows], base_out.at[rows], base_sems.at[i])

    def feed(i, sent):
        rows = pl.ds(pl.multiple_of(i * ROWS, ROWS), ROWS)
        slot = lax.rem(i, 2)

        @pl.when(i >= 2)
        def _():
            act_copy(i - 2).wait()

        mixed = mix_v[rows, :]
        grad_b = g_v[rows, :]
        grad = grad_b.astype(f32)
        residual = x_v[rows, :].astype(f32) + (mm(mixed, w_out[...]) + row(b_out))
        unit, rstd = row_norm(residual)
        normed = (unit * row(gain_mlp) + row(shift_mlp)).astype(bf16)
        normed_t = normed.T
        grad_t = grad_b.T
        for at in range(0, hidden, CHUNK):
            cols = slice(at, at + CHUNK)
            up = mm(normed, w_up[:, cols]) + row(b_up, cols)
            d_act = mm_nt(grad_b, w_down[cols, :])
            cdf = 0.5 + 0.5 * lax.erf(up * 0.7071067811865476)
            pdf = 0.3989422804014327 * jnp.exp(-0.5 * up * up)
            act_v[slot, :, cols] = (up * cdf).astype(bf16)
            d_up = d_act * (cdf + up * pdf)
            dup_v[:, cols] = d_up.astype(bf16)
            gb_up[:, cols] += fold(d_up)
        act_copy(i).start()
        d_normed = mm_nt(dup_v[...], w_up[...])
        add_blocks(sums, up_at, mm(normed_t, dup_v[...]))
        add_blocks(sums, down_at, mm(grad_t, act_v[slot]))
        x_v[rows, :] = (residual + row(b_down)).astype(bf16)
        base_copy(i).start()
        gb_down[...] += fold(grad)
        gg_mlp[...] += fold(d_normed * unit)
        gs_mlp[...] += fold(d_normed)
        d_residual = grad + norm_back(d_normed * row(gain_mlp), unit, rstd)
        d_att = d_residual.astype(bf16)
        gb_out[...] += fold(d_residual)
        add_blocks(sums, out_at, mm_tn(mixed, d_att))
        g_v[rows, :] = d_att
        mix_v[rows, :] = mm_nt(d_att, w_out[...]).astype(bf16)

        def send(f):
            window_copy(f, g_v, att_out, 1).start()
            window_copy(f, mix_v, mix_out, 2).start()
            return f + 1

        return lax.while_loop(functools.partial(finished, i), send, sent)

    pltpu.make_async_copy(x_out, x_out, window_sems.at[5]).wait()
    lax.fori_loop(0, blocks, feed, 0)
    at = vector_at
    for partial in (gb_up, gb_down, gb_out, gg_mlp, gs_mlp):
        at = add_vector(sums, at, partial[...])

    lax.fori_loop(jnp.maximum(blocks - 2, 0), blocks, lambda i, c: act_copy(i).wait(), None)
    lax.fori_loop(0, blocks, lambda i, c: base_copy(i).wait(), None)
    for kind, ref in enumerate((qkv_out, att_out, mix_out)):
        pltpu.make_async_copy(ref, ref, window_sems.at[kind]).wait()


FIRST_IN_ATTEND = (1, 2, 4, 5, 6, 7)
FIRST_IN_PROJECT = (1, 2, 4, 6)
SECOND_IN_PROJECT = (0, 1, 3, 5, 7)


def backward_kernel(
    orders_a, orders_b, fields, slots, width,
    counts, starts, qkv, probs, mix, unit, att, x_in, base, act, sums_a,
    w_qkv_hbm, gain_attn, shift_attn, w_down_hbm,
    d_in, enc, out_a, out_b,
    packed_v, mask_v, gb_qkv, total_a, total_b, w_qkv, w_down, load_sem, store_sems, weight_sems,
    sent_a, got_a, summed_a, send_a, recv_a, sent_b, got_b, summed_b, send_b, recv_b,
):
    first = Reducer(orders_a, total_a.shape[0], total_a, sent_a, got_a, summed_a, send_a, recv_a)
    second = Reducer(orders_b, total_b.shape[0], total_b, sent_b, got_b, summed_b, send_b, recv_b)
    load = pltpu.make_async_copy(sums_a, total_a, load_sem)
    load.start()
    weight_loads = start_all(((w_qkv_hbm, w_qkv), (w_down_hbm, w_down)), weight_sems)
    steps = fields // UNROLL
    rows = UNROLL * slots

    first.greet(first.partners() | second.partners())
    fill_mask(mask_v)
    total_b[...] = jnp.zeros_like(total_b)
    gb_qkv[...] = jnp.zeros_like(gb_qkv)

    def at_step(step, reducer, ahead, begin):
        for k, when in enumerate(ahead):

            @pl.when(step == when)
            def _(k=k):
                reducer.advance(begin + k)

    def field_rows(step, u):
        return pl.ds(pl.multiple_of((step * UNROLL + u) * slots, slots), slots)

    def here(step):
        return pl.ds(pl.multiple_of(step * rows, rows), rows)

    def attend(qkv_b, probs_b, mix_b, unit_b):
        step = pl.program_id(0)

        @pl.when(step == FIRST_IN_ATTEND[0])
        def _():
            load.wait()

        at_step(step, first, FIRST_IN_ATTEND, 0)
        grads = []
        for u in range(UNROLL):
            f = step * UNROLL + u
            head = lax.rem(starts[f], TILE)
            slot_row = lax.broadcasted_iota(jnp.int32, (slots, width), 0)
            live = (slot_row >= head) & (slot_row < head + counts[f])
            grads.append(block_heads(mix_b[u] * live.astype(f32).astype(bf16), mask_v))
        d_probs = [heads_dot(qkv_b[u, :, 2 * width :], grads[u]) for u in range(UNROLL)]
        for u in range(UNROLL):
            packed_v[field_rows(step, u), 2 * width :] = heads_out(probs_b[u], grads[u]).astype(bf16)
        d_scores = []
        for u in range(UNROLL):
            weights = probs_b[u].astype(f32)
            weighted = weights * d_probs[u]
            inner = jnp.sum(weighted, axis=0, keepdims=True)
            d_scores.append((weighted - weights * inner).astype(bf16))
        for u in range(UNROLL):
            query = block_heads(qkv_b[u, :, :width], mask_v)
            packed_v[field_rows(step, u), width : 2 * width] = heads_out(d_scores[u], query).astype(bf16)
        turned = [pairs_t(d_score) for d_score in d_scores]
        for u in range(UNROLL):
            d_query = heads_out_t(turned[u], qkv_b[u, :, width : 2 * width])
            packed_v[field_rows(step, u), :width] = (d_query * HEAD**-0.5).astype(bf16)
        grad = packed_v[here(step), :]
        add_blocks(total_b, 0, mm_tn(unit_b[...].reshape(rows, width), grad))
        gb_qkv[...] += fold(grad.astype(f32))

    def block(*shape):
        return pl.BlockSpec((UNROLL,) + shape, lambda i: (i, 0, 0))

    pltpu.emit_pipeline(
        attend,
        grid=(steps,),
        in_specs=[block(slots, 3 * width)] + [block(slots, width)] * 3,
    )(qkv, probs, mix, unit)

    for copy in weight_loads:
        copy.wait()
    at = 3 * width * width // LANES
    add_vector(total_b, at, gb_qkv[...])
    grad_sum = jnp.sum(gb_qkv[...], axis=0, keepdims=True)
    gain = jnp.broadcast_to(row(gain_attn), (LANES, width)).T
    shift = jnp.broadcast_to(row(shift_attn), (LANES, width)).T
    gain_sum = jnp.zeros((width, LANES), f32)
    shift_sum = jnp.zeros((width, LANES), f32)
    for k in range(3 * width // LANES):
        at_rows = pl.ds(k * width, width)
        cols = slice(k * LANES, (k + 1) * LANES)
        weight = w_qkv[:, cols].astype(f32)
        part = total_b[at_rows, :]
        column = jnp.broadcast_to(grad_sum[:, cols], (width, LANES))
        gain_sum += weight * part
        shift_sum += weight * column
        total_b[at_rows, :] = gain * part + shift * column
    at += 3 * width // LANES
    at = add_vector(total_b, at, gain_sum.T)
    add_vector(total_b, at, shift_sum.T)

    less = PART // SPLIT

    def project(x_b, att_b, act_b, base_b, d_in_b, enc_b):
        step = pl.program_id(0)
        at_step(step, second, SECOND_IN_PROJECT, 0)
        at_step(step, first, FIRST_IN_PROJECT, len(FIRST_IN_ATTEND))
        grads, downs = {}, {}
        for k in range(rows // PART + 1):
            if k < rows // PART:
                at = pl.multiple_of(step * rows + k * PART, PART)
                grads[k] = mm_nt(packed_v[pl.ds(at, PART), :], w_qkv[...])
                downs[k] = mm(act_b[k * less : (k + 1) * less, :], w_down[...])
            if k:
                part = pl.ds((k - 1) * PART, PART)
                unit, rstd = row_norm(x_b[part, :].astype(f32))
                d_x = norm_back(grads.pop(k - 1) * row(gain_attn), unit, rstd)
                d_in_b[part, :] = (att_b[part, :].astype(f32) + d_x).astype(bf16)
                part = pl.ds((k - 1) * less, less)
                enc_b[part, :] = (base_b[part, :].astype(f32) + downs.pop(k - 1)).astype(bf16)

    narrow = pl.BlockSpec((rows, width), lambda i: (i, 0))
    short = pl.BlockSpec((rows // SPLIT, width), lambda i: (i, 0))
    pltpu.emit_pipeline(
        project,
        grid=(steps,),
        in_specs=[
            narrow, narrow, pl.BlockSpec((rows // SPLIT, act.shape[1]), lambda i: (i, 0)), short,
        ],
        out_specs=[narrow, short],
    )(x_in, att, act, base, d_in, enc)

    for k in range(len(FIRST_IN_ATTEND) + len(FIRST_IN_PROJECT), first.steps):
        first.advance(k)
    store_a = pltpu.make_async_copy(summed_a, out_a, store_sems.at[0])
    store_a.start()
    for k in range(len(SECOND_IN_PROJECT), second.steps):
        second.advance(k)
    store_b = pltpu.make_async_copy(summed_b, out_b, store_sems.at[1])
    store_b.start()
    store_a.wait()
    store_b.wait()


def unblock(src, at, dst):
    rows, columns = dst.shape
    for k in range(columns // LANES):
        dst[:, k * LANES : (k + 1) * LANES] = src[pl.ds(at + k * rows, rows), :].astype(f32)


def unblock_t(src, at, dst):
    rows, columns = dst.shape
    for k in range(rows // LANES):
        part = src[pl.ds(at + k * columns, columns), :].astype(f32)
        dst[k * LANES : (k + 1) * LANES, :] = part.T


def unblock_vector(src, at, dst):
    (columns,) = dst.shape
    for k in range(columns // LANES):
        dst[k * LANES : (k + 1) * LANES] = src[pl.ds(at + k, 1), :].astype(f32).reshape(LANES)


def unpack_kernel(
    fields, slots, width, hidden,
    counts, starts, visible, d_in, enc, base, act, w_down_hbm, sums_a_hbm, sums_b_hbm,
    encoded, input_grad, w_qkv, b_query, b_value, w_out, b_out, w_up, b_up, w_down, b_down,
    gain_attn, shift_attn, gain_mlp, shift_mlp,
    picks_v, d_in_v, enc_v, out_v, grad_v, act_v, qkv_v, up_v, down_v,
    sums_a, sums_b, w_down_in, sems, weight_sems,
):
    up_at, down_at, out_at, at = sum_rows(width, hidden)
    steps = fields // GROUP

    def group(step):
        return pl.ds(step * GROUP, GROUP)

    def enc_load(src, step):
        rows = pl.ds(pl.multiple_of(step * GROUP * slots, GROUP * slots), GROUP * slots)
        return pltpu.make_async_copy(src.at[rows], enc_v.at[rows], sems.at[1, step])

    early = enc.shape[0] // (GROUP * slots)

    def act_load(step):
        size = GROUP * slots
        src = pl.ds(pl.multiple_of(step * size, size), size)
        dst = pl.ds(pl.multiple_of((step - early) * size, size), size)
        return pltpu.make_async_copy(act.at[src], act_v.at[dst], sems.at[2, step])

    def used(step):
        return step * GROUP * slots < starts[fields - 1] + slots

    def loads(step):
        rows = pl.ds(pl.multiple_of(step * GROUP * slots, GROUP * slots), GROUP * slots)
        return (
            pltpu.make_async_copy(d_in.at[rows], d_in_v.at[rows], sems.at[0, step]),
        )

    def stores(step):
        return (
            pltpu.make_async_copy(out_v.at[group(step)], encoded.at[group(step)], sems.at[1, step]),
            pltpu.make_async_copy(grad_v.at[group(step)], input_grad.at[group(step)], sems.at[0, step]),
        )

    def start_loads(step, carry):
        for copy in loads(step):
            copy.start()

        @pl.when(step < early)
        def _():
            enc_load(enc, step).start()

        @pl.when((step >= early) & used(step))
        def _():
            enc_load(base, step).start()
            act_load(step).start()

        return carry

    def wait_stores(step, carry):
        for copy in stores(step):
            copy.wait()
        return carry

    def unpack(step, carry):
        for copy in loads(step):
            copy.wait()

        @pl.when(step < early)
        def _():
            enc_load(enc, step).wait()

        @pl.when((step >= early) & used(step))
        def _():
            enc_load(base, step).wait()
            act_load(step).wait()
            size = GROUP * slots
            here = pl.ds(pl.multiple_of(step * size, size), size)
            late = pl.ds(pl.multiple_of((step - early) * size, size), size)
            last = enc_v[here, :].astype(f32) + mm(act_v[late, :], w_down_in[...])
            enc_v[here, :] = last.astype(bf16)

        patch_row = lax.broadcasted_iota(jnp.int32, (input_grad.shape[1], slots), 0)
        rows = lax.broadcasted_iota(jnp.int32, (slots, slots), 0)
        cols = lax.broadcasted_iota(jnp.int32, (slots, slots), 1)
        puts, shifts = [], []
        for u in range(GROUP):
            f = step * GROUP + u
            head, count = lax.rem(starts[f], TILE), counts[f]
            picks = shifted_picks(picks_v[pl.ds(f, 1), :], head, count)
            puts.append((patch_row == picks).astype(f32).astype(bf16))
            shifts.append(((cols - rows == head) & (rows < count)).astype(f32).astype(bf16))
        for u in range(GROUP):
            f = step * GROUP + u
            window = pl.ds(pl.multiple_of(f * slots, slots), slots)
            grad_v[f] = mm(puts[u], d_in_v[window, :]).astype(bf16)
            at = pl.multiple_of(starts[f] - lax.rem(starts[f], TILE), TILE)
            out_v[f] = mm(shifts[u], enc_v[pl.ds(at, slots), :]).astype(bf16)
        for copy in stores(step):
            copy.start()
        return carry

    ahead = [
        pltpu.make_async_copy(src, dst, weight_sems.at[3 + k])
        for k, (src, dst) in enumerate(
            ((sums_a_hbm, sums_a), (sums_b_hbm, sums_b), (w_down_hbm, w_down_in))
        )
    ]
    for copy in ahead:
        copy.start()
    lax.fori_loop(0, steps, start_loads, 0)
    picks_v[...] = visible[...].T
    for copy in ahead:
        copy.wait()
    copies = []
    unblock(sums_a, up_at, up_v)
    copies.append(pltpu.make_async_copy(up_v, w_up, weight_sems.at[0]))
    copies[0].start()
    unblock_t(sums_a, down_at, down_v)
    copies.append(pltpu.make_async_copy(down_v, w_down, weight_sems.at[1]))
    copies[1].start()
    unblock(sums_b, 0, qkv_v)
    copies.append(pltpu.make_async_copy(qkv_v, w_qkv, weight_sems.at[2]))
    copies[2].start()
    unblock(sums_a, out_at, w_out)
    for ref in (b_up, b_down, b_out, gain_mlp, shift_mlp):
        unblock_vector(sums_a, at, ref)
        at += ref.shape[0] // LANES
    at = 3 * width * width // LANES
    for ref, rows in ((b_query, 2), (b_value, 1), (gain_attn, 1), (shift_attn, 1)):
        unblock_vector(sums_b, at, ref)
        at += rows * width // LANES
    lax.fori_loop(0, steps, unpack, 0)
    lax.fori_loop(0, steps, wait_stores, 0)
    for copy in copies:
        copy.wait()


def forward(sizes, args):
    (
        patches, visible, counts, upstream, w_qkv, b_query, b_value, w_out, b_out,
        w_up, b_up, w_down, b_down, gain_attn, shift_attn, gain_mlp, shift_mlp,
    ) = args
    fields, _, width = patches.shape
    slots, hidden = visible.shape[1], w_up.shape[1]
    cap = (fields * slots + ROWS - 1) // ROWS * ROWS
    tall = cap + ROWS
    vectors = (hidden + 4 * width) // LANES
    rows_a = padded_rows(sum_rows(width, hidden)[3] + vectors, sizes)
    shape = jax.ShapeDtypeStruct
    hbm = pl.BlockSpec(memory_space=pl.ANY)
    vmem = pl.BlockSpec(memory_space=pltpu.VMEM)
    smem = pl.BlockSpec(memory_space=pltpu.SMEM)
    windows = shape((fields, slots, width), bf16)
    return pl.pallas_call(
        functools.partial(forward_kernel, fields, slots, width, hidden),
        out_shape=[
            shape((fields,), jnp.int32),
            windows,
            windows,
            shape((fields, slots, 3 * width), bf16),
            windows,
            windows,
            windows,
            shape((cap, width), bf16),
            shape((cap, hidden), bf16),
            shape((rows_a, LANES), f32),
        ],
        in_specs=[smem, hbm, vmem, hbm, hbm, vmem, vmem, hbm, vmem, hbm, vmem, hbm] + [vmem] * 5,
        out_specs=[smem] + [hbm] * 8 + [vmem],
        scratch_shapes=[
            pltpu.VMEM((tall, width), bf16),
            pltpu.VMEM((tall, width), bf16),
            pltpu.VMEM((cap, 3 * width), bf16),
            pltpu.VMEM((tall, width), bf16),
            pltpu.VMEM((2, AHEAD, slots, width), bf16),
            pltpu.VMEM((2, ROWS, hidden), bf16),
            pltpu.VMEM((ROWS, hidden), bf16),
            pltpu.VMEM((4 * HEAD, 4 * HEAD), bf16),
            pltpu.VMEM((fields, slots), jnp.int32),
            pltpu.VMEM((8, hidden), f32),
            pltpu.VMEM((8, width), f32),
            pltpu.VMEM((8, width), f32),
            pltpu.VMEM((8, width), f32),
            pltpu.VMEM((8, width), f32),
            pltpu.SemaphoreType.DMA((6,)),
            pltpu.SemaphoreType.DMA((2,)),
            pltpu.SemaphoreType.DMA((2, fields // BATCH)),
            pltpu.SemaphoreType.DMA((2,)),
            pltpu.SemaphoreType.DMA((cap // ROWS,)),
            pltpu.VMEM(w_qkv.shape, bf16),
            pltpu.VMEM(w_out.shape, bf16),
            pltpu.VMEM(w_up.shape, bf16),
            pltpu.VMEM(w_down.shape, bf16),
            pltpu.SemaphoreType.DMA((4,)),
        ],
        compiler_params=pltpu.CompilerParams(vmem_limit_bytes=VMEM_BYTES),
        name="forward_rows",
    )(
        counts, patches.reshape(-1, width), visible.T, upstream.reshape(-1, width),
        w_qkv, b_query, b_value, w_out, b_out, w_up, b_up, w_down, b_down, gain_attn, shift_attn, gain_mlp, shift_mlp,
    )


def backward(
    sizes, counts, starts, qkv, probs, mix, unit, att, x_rows, base, act, sums_a,
    w_qkv, gain, shift, w_down,
):
    fields, slots, width = mix.shape
    orders_a, orders_b = exchange_orders(sizes), direct_orders(sizes)
    rows_b = padded_rows((3 * width * width + 5 * width) // LANES, sizes)
    shape = jax.ShapeDtypeStruct
    hbm = pl.BlockSpec(memory_space=pl.ANY)
    vmem = pl.BlockSpec(memory_space=pltpu.VMEM)
    smem = pl.BlockSpec(memory_space=pltpu.SMEM)
    return pl.pallas_call(
        functools.partial(backward_kernel, orders_a, orders_b, fields, slots, width),
        out_shape=[
            shape((fields * slots, width), bf16),
            shape((act.shape[0] // SPLIT, width), bf16),
            shape(sums_a.shape, bf16),
            shape((rows_b, LANES), bf16),
        ],
        in_specs=[smem, smem] + [hbm] * 10 + [vmem] * 2 + [hbm],
        out_specs=[hbm] * 4,
        scratch_shapes=[
            pltpu.VMEM((fields * slots, 3 * width), bf16),
            pltpu.VMEM((4 * HEAD, 4 * HEAD), bf16),
            pltpu.VMEM((8, 3 * width), f32),
            pltpu.VMEM(sums_a.shape, f32),
            pltpu.VMEM((rows_b, LANES), f32),
            pltpu.VMEM(w_qkv.shape, bf16),
            pltpu.VMEM(w_down.shape, bf16),
            pltpu.SemaphoreType.DMA,
            pltpu.SemaphoreType.DMA((2,)),
            pltpu.SemaphoreType.DMA((2,)),
        ]
        + reducer_scratch(sums_a.shape[0], orders_a)
        + reducer_scratch(rows_b, orders_b),
        compiler_params=pltpu.CompilerParams(
            collective_id=0, has_side_effects=True, vmem_limit_bytes=VMEM_BYTES
        ),
        name="backward_rows",
    )(
        counts, starts, qkv, probs, mix, unit, att.reshape(-1, width), x_rows.reshape(-1, width),
        base, act, sums_a, w_qkv, gain, shift, w_down,
    )


def unpack_all(
    counts, starts, visible, d_in, enc, base, act, w_down, sums_a, sums_b, patch_rows, hidden
):
    (slots, fields), width = visible.shape, d_in.shape[1]
    shape = jax.ShapeDtypeStruct
    hbm = pl.BlockSpec(memory_space=pl.ANY)
    vmem = pl.BlockSpec(memory_space=pltpu.VMEM)
    smem = pl.BlockSpec(memory_space=pltpu.SMEM)
    vector = shape((width,), f32)
    return pl.pallas_call(
        functools.partial(unpack_kernel, fields, slots, width, hidden),
        out_shape=[
            shape((fields, slots, width), bf16),
            shape((fields, patch_rows, width), bf16),
            shape((width, 3 * width), f32), vector, vector,
            shape((width, width), f32), vector,
            shape((width, hidden), f32), shape((hidden,), f32),
            shape((hidden, width), f32), vector,
            vector, vector, vector, vector,
        ],
        in_specs=[smem, smem, vmem] + [hbm] * 7,
        out_specs=[hbm] * 3 + [vmem] * 4 + [hbm, vmem, hbm] + [vmem] * 5,
        scratch_shapes=[
            pltpu.VMEM((fields, slots), jnp.int32),
            pltpu.VMEM(d_in.shape, bf16),
            pltpu.VMEM(base.shape, bf16),
            pltpu.VMEM((fields, slots, width), bf16),
            pltpu.VMEM((fields, patch_rows, width), bf16),
            pltpu.VMEM((base.shape[0] - enc.shape[0], hidden), bf16),
            pltpu.VMEM((width, 3 * width), f32),
            pltpu.VMEM((width, hidden), f32),
            pltpu.VMEM((hidden, width), f32),
            pltpu.VMEM(sums_a.shape, bf16),
            pltpu.VMEM(sums_b.shape, bf16),
            pltpu.VMEM(w_down.shape, bf16),
            pltpu.SemaphoreType.DMA((3, fields // GROUP)),
            pltpu.SemaphoreType.DMA((6,)),
        ],
        compiler_params=pltpu.CompilerParams(vmem_limit_bytes=VMEM_BYTES),
        name="unpack_rows",
    )(counts, starts, visible, d_in, enc, base, act, w_down, sums_a, sums_b)


def per_device(sizes, *args):
    patches, visible, counts = args[:3]
    w_qkv, w_up, gain_attn, shift_attn = args[4], args[9], args[13], args[14]
    starts, x_rows, unit, qkv, probs, att, mix, base, act, sums_a = forward(sizes, args)
    d_in, enc, total_a, total_b = backward(
        sizes, counts, starts, qkv, probs, mix, unit, att, x_rows, base, act, sums_a,
        w_qkv, gain_attn, shift_attn, args[11],
    )
    return tuple(
        unpack_all(
            counts, starts, visible.T, d_in, enc, base, act, args[11], total_a, total_b, patches.shape[1], w_up.shape[1]
        )
    )


def solution(mesh):
    rows = P(("wide", "narrow"))
    return jax.shard_map(
        functools.partial(per_device, dict(mesh.shape)),
        mesh=mesh,
        in_specs=(rows,) * 4 + (P(),) * 13,
        out_specs=(rows,) * 2 + (P(),) * 13,
        check_vma=False,
    )
```

```python
import functools

import jax
import jax.numpy as jnp
from jax import lax
from jax.experimental import pallas as pl
from jax.experimental.pallas import tpu as pltpu
from jax.sharding import PartitionSpec as P

HEAD = 64
EPS = 1e-06
FILL = -1e30
ROWS = 512
TILE = 16
UNROLL = 16
AHEAD = 16
GROUP = 8
BATCH = 16
PIECES = 4
PART = 256
SPLIT = 2
CHUNK = 256
VMEM_BYTES = 60 * 1024 * 1024
f32 = jnp.float32
bf16 = jnp.bfloat16


LANES = 128


def mm(left, right):
    return lax.dot_general(left, right, (((1,), (0,)), ((), ())), preferred_element_type=f32)


def mm_nt(left, right):
    return lax.dot_general(left, right, (((1,), (1,)), ((), ())), preferred_element_type=f32)


def mm_tn(left, right):
    return lax.dot_general(left, right, (((0,), (0,)), ((), ())), preferred_element_type=f32)


def row_norm(values):
    width = values.shape[-1]
    mean = jnp.sum(values, axis=-1, keepdims=True) * (1.0 / width)
    centered = values - mean
    variance = jnp.sum(centered * centered, axis=-1, keepdims=True) * (1.0 / width)
    rstd = lax.rsqrt(variance + EPS)
    return centered * rstd, rstd


def norm_back(grad, unit, rstd):
    width = grad.shape[-1]
    first = jnp.sum(grad, axis=-1, keepdims=True) * (1.0 / width)
    second = jnp.sum(grad * unit, axis=-1, keepdims=True) * (1.0 / width)
    return (grad - first - unit * second) * rstd


def fold(values):
    rows, width = values.shape
    return jnp.sum(values.reshape(rows // 8, 8, width), axis=0)


def fill_mask(mask):
    row = lax.broadcasted_iota(jnp.int32, mask.shape, 0) // HEAD
    col = lax.broadcasted_iota(jnp.int32, mask.shape, 1) // HEAD
    mask[...] = (row == col).astype(f32).astype(bf16)


def head_parts(width):
    parts, at = [], 0
    while at < width:
        size = min(4 * HEAD, width - at)
        parts.append((at, size))
        at += size
    return parts


def block_heads(values, mask):
    blocks = []
    for at, size in head_parts(values.shape[1]):
        tiled = jnp.concatenate([values[:, at : at + size]] * (size // HEAD), axis=0)
        blocks.append(tiled * mask[:size, :size])
    return blocks


def heads_dot(left, stacked):
    parts = [
        mm_nt(left[:, at : at + size], block)
        for (at, size), block in zip(head_parts(left.shape[1]), stacked)
    ]
    return jnp.concatenate(parts, axis=1)


def heads_out(left, stacked):
    parts = [
        mm(left[:, at : at + size], block)
        for (at, size), block in zip(head_parts(left.shape[1]), stacked)
    ]
    return jnp.concatenate(parts, axis=1)


def heads_out_t(weights, values):
    window = weights[0].shape[0] // 2
    parts = []
    for k, at in enumerate(range(0, values.shape[1], 2 * HEAD)):
        pair = mm(weights[k], values[:, at : at + 2 * HEAD])
        lane = lax.broadcasted_iota(jnp.int32, (window, 2 * HEAD), 1)
        parts.append(jnp.where(lane < HEAD, pair[:window], pair[window:]))
    return jnp.concatenate(parts, axis=1)


def pairs_t(values):
    return [values[:, at : at + 2 * HEAD].T for at in range(0, values.shape[1], 2 * HEAD)]


def start_all(pairs, sems):
    copies = [
        pltpu.make_async_copy(src, dst, sems.at[k]) for k, (src, dst) in enumerate(pairs)
    ]
    for copy in copies:
        copy.start()
    return copies


def add_blocks(sums, at, values):
    rows = values.shape[0]
    for k in range(values.shape[1] // LANES):
        block = pl.ds(at + k * rows, rows)
        sums[block, :] += values[:, k * LANES : (k + 1) * LANES]


def add_vector(sums, at, partial):
    vector = jnp.sum(partial, axis=0, keepdims=True)
    for k in range(vector.shape[1] // LANES):
        sums[pl.ds(at + k, 1), :] = vector[:, k * LANES : (k + 1) * LANES]
    return at + vector.shape[1] // LANES


def row(ref, cols=slice(None)):
    return ref[cols].reshape(1, -1)


def shifted_picks(vis, head, count):
    slots = vis.shape[1]
    lane = lax.broadcasted_iota(jnp.int32, vis.shape, 1)
    live = jnp.where(lane < count, vis, -1)
    wide = jnp.concatenate([live, jnp.full((1, LANES - slots), -1, jnp.int32)], axis=1)
    return pltpu.roll(wide, head, axis=1)[:, :slots]


def merge_store(ref, base, head, window):
    old = ref[pl.ds(base, TILE), :]
    row = lax.broadcasted_iota(jnp.int32, (TILE, window.shape[1]), 0)
    ref[pl.ds(base, TILE), :] = jnp.where(row >= head, window[:TILE], old)
    rest = window.shape[0] - TILE
    ref[pl.ds(base + TILE, rest), :] = window[TILE:]


def mesh_bits(sizes):
    wide = [("wide", 1 << k) for k in range(sizes["wide"].bit_length() - 1)]
    narrow = [("narrow", 1 << k) for k in range(sizes["narrow"].bit_length() - 1)]
    return wide, narrow


def exchange_orders(sizes):
    wide, narrow = mesh_bits(sizes)
    first, last = narrow[:1], wide[-1:]
    middle = wide[:1] + narrow[1:] + wide[1:-1]
    orders = [first + middle[k:] + middle[:k] + last for k in range(min(3, len(middle)))]
    return [[(pair,) for pair in order] for order in orders]


def direct_orders(sizes):
    wide, narrow = mesh_bits(sizes)
    plane, line = tuple(wide[:1] + narrow[1:]), tuple(wide[1:])
    return [[tuple(narrow[:1]), plane, line], [tuple(narrow[:1]), line, plane]]


def members(group):
    return [
        tuple(pair for k, pair in enumerate(group) if mask >> k & 1)
        for mask in range(1, 1 << len(group))
    ]


def rows_of_parts(rows, orders):
    unit = TILE << sum(len(group) for group in orders[0])
    units, parts, at = rows // unit, [], 0
    for k in range(len(orders)):
        share = (units + len(orders) - 1 - k) // len(orders) * unit
        if share:
            parts.append((at, share))
        at += share
    return parts


class Reducer:
    def __init__(self, orders, rows, total, sent, got, summed, send_sems, recv_sems):
        self.orders, self.total, self.sent, self.got, self.summed = orders, total, sent, got, summed
        self.send_sems, self.recv_sems = send_sems, recv_sems
        self.stages = len(orders[0])
        self.parts = rows_of_parts(rows, orders)
        self.sides = {}
        for group in orders[0]:
            for axis, distance in group:
                self.sides[axis, distance] = lax.rem(lax.axis_index(axis) // distance, 2)
        self.bases, self.sizes = [], []
        for order, (base, size) in zip(orders, self.parts):
            bases, sizes = [base], [size]
            for group in order:
                sizes.append(sizes[-1] >> len(group))
                bases.append(bases[-1] + self.place(group) * sizes[-1])
            self.bases.append(bases)
            self.sizes.append(sizes)

    def place(self, group, flipped=()):
        place = 0
        for k, pair in enumerate(group):
            side = self.sides[pair]
            place = place + (1 << k) * (1 - side if pair in flipped else side)
        return place

    def device(self, flipped):
        other = {}
        for axis, distance in flipped:
            mine = other.get(axis, lax.axis_index(axis))
            other[axis] = mine + distance * (1 - 2 * self.sides[axis, distance])
        return other

    def partners(self):
        return {flipped for order in self.orders for group in order for flipped in members(group)}

    def greet(self, partners):
        barrier = pltpu.get_barrier_semaphore()
        for flipped in sorted(partners):
            pl.semaphore_signal(
                barrier, inc=1, device_id=self.device(flipped), device_id_type=pl.DeviceIdType.MESH
            )
        pl.semaphore_wait(barrier, len(partners))

    def flights(self, part, stage):
        summing = stage < self.stages
        level = stage if summing else 2 * self.stages - 1 - stage
        group = self.orders[part][level]
        size = self.sizes[part][level + 1]
        base, share = self.parts[part]
        for k, flipped in enumerate(members(group)):
            if summing:
                slot = pl.ds(base + share - self.sizes[part][level] + k * size, size)
                src, dst = self.sent.at[slot], self.got.at[slot]
            else:
                slot = pl.ds(pl.multiple_of(self.bases[part][level + 1], TILE), size)
                src = dst = self.summed.at[slot]
            copy = pltpu.make_async_remote_copy(
                src_ref=src, dst_ref=dst,
                send_sem=self.send_sems.at[part, stage, k], recv_sem=self.recv_sems.at[part, stage, k],
                device_id=self.device(flipped), device_id_type=pl.DeviceIdType.MESH,
            )
            yield copy, flipped, slot

    def leave(self, part, stage):
        for copy, flipped, slot in self.flights(part, stage):
            if stage < self.stages:
                size = self.sizes[part][stage + 1]
                at = self.bases[part][stage] + self.place(self.orders[part][stage], flipped) * size
                self.sent[slot, :] = self.total[pl.ds(pl.multiple_of(at, TILE), size), :].astype(bf16)
            copy.start()

    def arrive(self, part, stage):
        flights = list(self.flights(part, stage))
        for copy, _, _ in flights:
            copy.wait()
        if stage < self.stages:
            here = pl.ds(pl.multiple_of(self.bases[part][stage + 1], TILE), self.sizes[part][stage + 1])
            value = self.total[here, :]
            for _, _, slot in flights:
                value = value + self.got[slot, :].astype(f32)
            if stage + 1 < self.stages:
                self.total[here, :] = value
            else:
                self.summed[here, :] = value.astype(bf16)

    def advance(self, stage):
        for part in range(len(self.parts)):
            if stage:
                self.arrive(part, stage - 1)
            if stage < 2 * self.stages:
                self.leave(part, stage)

    @property
    def steps(self):
        return 2 * self.stages + 1


def padded_rows(rows, sizes):
    unit = TILE * sizes["wide"] * sizes["narrow"]
    return (rows + unit - 1) // unit * unit


def reducer_scratch(rows, orders):
    most = max(len(members(group)) for group in orders[0])
    flights = (len(orders), 2 * len(orders[0]), most)
    return [
        pltpu.VMEM((rows, LANES), bf16),
        pltpu.VMEM((rows, LANES), bf16),
        pltpu.VMEM((rows, LANES), bf16),
        pltpu.SemaphoreType.DMA(flights),
        pltpu.SemaphoreType.DMA(flights),
    ]


def sum_rows(width, hidden):
    up, out = width * hidden // LANES, width * width // LANES
    return 0, up, 2 * up, 2 * up + out


def forward_kernel(
    fields, slots, width, hidden,
    counts, patches, visible, upstream,
    w_qkv_hbm, b_query, b_value, w_out_hbm, b_out, w_up_hbm, b_up, w_down_hbm, b_down,
    gain_attn, shift_attn, gain_mlp, shift_mlp,
    starts, x_out, unit_out, qkv_out, probs_out, att_out, mix_out, base_out, act_out, sums_out,
    x_v, g_v, qkv_v, mix_v, probs_v, act_v, dup_v, mask_v, picks_v,
    gb_up, gb_down, gb_out, gg_mlp, gs_mlp, window_sems, probs_sems, land_sems,
    act_sems, base_sems, w_qkv, w_out, w_up, w_down, weight_sems, sums, sums_sem,
):
    up_at, down_at, out_at, vector_at = sum_rows(width, hidden)
    patch_rows = patches.shape[0] // fields
    steps = fields // BATCH
    landing = qkv_v.shape[0] // (BATCH * patch_rows)
    cut = [slice(k * width, (k + 1) * width) for k in range(3)]

    def arrivals(third, step):
        size = BATCH * patch_rows
        src = pl.ds(pl.multiple_of(step * size, size), size)
        dst = pl.ds(pl.multiple_of((step - third * landing) * size, size), size)
        size = BATCH * slots
        up = pl.ds(pl.multiple_of(step * size, size), size)
        return (
            pltpu.make_async_copy(patches.at[src], qkv_v.at[dst, cut[third]], land_sems.at[0, step]),
            pltpu.make_async_copy(upstream.at[up], qkv_v.at[up, cut[2]], land_sems.at[1, step]),
        )

    def start_arrivals(third, step, carry):
        for copy in arrivals(third, step):
            copy.start()
        return carry

    for third in range(steps // landing):
        lax.fori_loop(
            third * landing, (third + 1) * landing, functools.partial(start_arrivals, third), 0
        )

    weights = start_all(
        ((w_qkv_hbm, w_qkv), (w_out_hbm, w_out), (w_up_hbm, w_up), (w_down_hbm, w_down)), weight_sems
    )

    def place(f, at):
        count = counts[f]
        head = lax.rem(at, TILE)
        at = jnp.where(head + count > slots, at + TILE - head, at)
        starts[f] = at
        return at + count

    lax.fori_loop(0, fields, place, 0)
    last = starts[fields - 1]
    tail = pl.multiple_of(last - lax.rem(last, TILE) + slots, TILE)
    blocks = (tail + ROWS - 1) // ROWS
    for ref in (sums, gb_up, gb_down, gb_out, gg_mlp, gs_mlp):
        ref[...] = jnp.zeros_like(ref)
    fill_mask(mask_v)
    picks_v[...] = visible[...].T

    def where_is(f):
        start = starts[f]
        head = lax.rem(start, TILE)
        return pl.multiple_of(start - head, TILE), head, counts[f]

    def pack(third, step, carry):
        for copy in arrivals(third, step):
            copy.wait()
        patch_row = lax.broadcasted_iota(jnp.int32, (patch_rows, slots), 0)
        rows = lax.broadcasted_iota(jnp.int32, (slots, slots), 0)
        cols = lax.broadcasted_iota(jnp.int32, (slots, slots), 1)
        places = [where_is(step * BATCH + u) for u in range(BATCH)]
        takes, shifts = [], []
        for u, (base, head, count) in enumerate(places):
            picks = shifted_picks(picks_v[pl.ds(step * BATCH + u, 1), :], head, count)
            takes.append((patch_row == picks).astype(f32).astype(bf16))
            shifts.append(((rows - cols == head) & (cols < count)).astype(f32).astype(bf16))
        takes = [take.T for take in takes]
        x_wins, g_wins = [], []
        for u in range(BATCH):
            at = (step - third * landing) * BATCH + u
            field = qkv_v[pl.ds(pl.multiple_of(at * patch_rows, patch_rows), patch_rows), cut[third]]
            x_wins.append(mm(takes[u], field).astype(bf16))
        for u in range(BATCH):
            at = step * BATCH + u
            field = qkv_v[pl.ds(pl.multiple_of(at * slots, slots), slots), cut[2]]
            g_wins.append(mm(shifts[u], field).astype(bf16))
        for (base, head, _), x_win, g_win in zip(places, x_wins, g_wins):
            merge_store(x_v, base, head, x_win)
            merge_store(g_v, base, head, g_win)
        return carry

    for third in range(steps // landing):
        lax.fori_loop(third * landing, (third + 1) * landing, functools.partial(pack, third), 0)
    x_v[pl.ds(tail, ROWS), :] = jnp.zeros((ROWS, width), bf16)
    g_v[pl.ds(tail, ROWS), :] = jnp.zeros((ROWS, width), bf16)

    def window_copy(f, src, dst, kind):
        base, _, _ = where_is(f)
        return pltpu.make_async_copy(src.at[pl.ds(base, slots)], dst.at[f], window_sems.at[kind])

    def finished(i, f):
        base, _, _ = where_is(jnp.minimum(f, fields - 1))
        return (f < fields) & (base + slots <= (i + 1) * ROWS)

    def norm(i, piece):
        size = ROWS // PIECES
        rows = pl.ds(pl.multiple_of(i * ROWS + piece * size, size), size)
        unit, _ = row_norm(x_v[rows, :].astype(f32))
        mix_v[rows, :] = unit.astype(bf16)
        normed = (unit * row(gain_attn) + row(shift_attn)).astype(bf16)
        act_v[lax.rem(i, 2), piece * size : (piece + 1) * size, 0:width] = normed

    def project(i, sent):
        rows = pl.ds(pl.multiple_of(i * ROWS, ROWS), ROWS)
        normed = act_v[lax.rem(i, 2), :, 0:width]
        query = mm(normed, w_qkv[:, cut[0]]) + row(b_query)
        qkv_v[rows, cut[0]] = (query * HEAD**-0.5).astype(bf16)
        norm(i + 1, 0)
        norm(i + 1, 1)
        qkv_v[rows, cut[1]] = mm(normed, w_qkv[:, cut[1]]).astype(bf16)
        norm(i + 1, 2)
        norm(i + 1, 3)
        qkv_v[rows, cut[2]] = (mm(normed, w_qkv[:, cut[2]]) + row(b_value)).astype(bf16)

        def send(f):
            window_copy(f, mix_v, unit_out, 4).start()
            window_copy(f, x_v, x_out, 5).start()
            return f + 1

        return lax.while_loop(functools.partial(finished, i), send, sent)

    for copy in weights:
        copy.wait()
    for piece in range(PIECES):
        norm(0, piece)
    lax.fori_loop(0, blocks, project, 0)
    pltpu.make_async_copy(unit_out, unit_out, window_sems.at[4]).wait()

    def probs_copy(i):
        slot = lax.rem(i, 2)
        return pltpu.make_async_copy(
            probs_v.at[slot], probs_out.at[pl.ds(i * AHEAD, AHEAD)], probs_sems.at[slot]
        )

    def attend(i, carry):
        slot = lax.rem(i, 2)

        @pl.when(i >= 2)
        def _():
            probs_copy(i - 2).wait()

        for u in range(AHEAD):
            window_copy(i * AHEAD + u, qkv_v, qkv_out, 0).start()
        places = [where_is(i * AHEAD + u) for u in range(AHEAD)]
        windows = [pl.ds(base, slots) for base, _, _ in places]
        scores = []
        for window in windows:
            stacked = block_heads(qkv_v[window, 0:width], mask_v)
            scores.append(heads_dot(qkv_v[window, width : 2 * width], stacked))
        weights = []
        for (_, head, count), score in zip(places, scores):
            slot_row = lax.broadcasted_iota(jnp.int32, score.shape, 0)
            live = (slot_row >= head) & (slot_row < head + count)
            score = jnp.where(live, score, FILL)
            expo = jnp.exp(score - jnp.max(score, axis=0, keepdims=True))
            total_row = jnp.sum(expo, axis=0, keepdims=True)
            weights.append((expo * (1.0 / total_row)).astype(bf16))
        for u, weight in enumerate(weights):
            probs_v[slot, u] = weight
        turned = [pairs_t(weight) for weight in weights]
        mixed = [
            heads_out_t(weight, qkv_v[window, 2 * width : 3 * width]).astype(bf16)
            for weight, window in zip(turned, windows)
        ]
        for (base, head, _), out in zip(places, mixed):
            merge_store(mix_v, base, head, out)
        probs_copy(i).start()
        return carry

    steps = fields // AHEAD
    lax.fori_loop(0, steps, attend, 0)
    probs_copy(steps - 2).wait()
    probs_copy(steps - 1).wait()
    mix_v[pl.ds(tail, ROWS), :] = jnp.zeros((ROWS, width), bf16)

    def act_copy(i):
        rows = pl.ds(pl.multiple_of(i * ROWS, ROWS), ROWS)
        slot = lax.rem(i, 2)
        return pltpu.make_async_copy(act_v.at[slot], act_out.at[rows], act_sems.at[slot])

    def base_copy(i):
        rows = pl.ds(pl.multiple_of(i * ROWS, ROWS), ROWS)
        return pltpu.make_async_copy(x_v.at[rows], base_out.at[rows], base_sems.at[i])

    def feed(i, sent):
        rows = pl.ds(pl.multiple_of(i * ROWS, ROWS), ROWS)
        slot = lax.rem(i, 2)

        @pl.when(i >= 2)
        def _():
            act_copy(i - 2).wait()

        mixed = mix_v[rows, :]
        grad_b = g_v[rows, :]
        grad = grad_b.astype(f32)
        residual = x_v[rows, :].astype(f32) + (mm(mixed, w_out[...]) + row(b_out))
        unit, rstd = row_norm(residual)
        normed = (unit * row(gain_mlp) + row(shift_mlp)).astype(bf16)
        normed_t = normed.T
        grad_t = grad_b.T
        for at in range(0, hidden, CHUNK):
            cols = slice(at, at + CHUNK)
            up = mm(normed, w_up[:, cols]) + row(b_up, cols)
            d_act = mm_nt(grad_b, w_down[cols, :])
            cdf = 0.5 + 0.5 * lax.erf(up * 0.7071067811865476)
            pdf = 0.3989422804014327 * jnp.exp(-0.5 * up * up)
            act_v[slot, :, cols] = (up * cdf).astype(bf16)
            d_up = d_act * (cdf + up * pdf)
            dup_v[:, cols] = d_up.astype(bf16)
            gb_up[:, cols] += fold(d_up)
        act_copy(i).start()
        d_normed = mm_nt(dup_v[...], w_up[...])
        add_blocks(sums, up_at, mm(normed_t, dup_v[...]))
        add_blocks(sums, down_at, mm(grad_t, act_v[slot]))
        x_v[rows, :] = (residual + row(b_down)).astype(bf16)
        base_copy(i).start()
        gb_down[...] += fold(grad)
        gg_mlp[...] += fold(d_normed * unit)
        gs_mlp[...] += fold(d_normed)
        d_residual = grad + norm_back(d_normed * row(gain_mlp), unit, rstd)
        d_att = d_residual.astype(bf16)
        gb_out[...] += fold(d_residual)
        add_blocks(sums, out_at, mm_tn(mixed, d_att))
        g_v[rows, :] = d_att
        mix_v[rows, :] = mm_nt(d_att, w_out[...]).astype(bf16)

        def send(f):
            window_copy(f, g_v, att_out, 1).start()
            window_copy(f, mix_v, mix_out, 2).start()
            return f + 1

        return lax.while_loop(functools.partial(finished, i), send, sent)

    pltpu.make_async_copy(x_out, x_out, window_sems.at[5]).wait()
    lax.fori_loop(0, blocks, feed, 0)
    at = vector_at
    for partial in (gb_up, gb_down, gb_out, gg_mlp, gs_mlp):
        at = add_vector(sums, at, partial[...])
    sums_copy = pltpu.make_async_copy(sums, sums_out, sums_sem)
    sums_copy.start()

    lax.fori_loop(jnp.maximum(blocks - 2, 0), blocks, lambda i, c: act_copy(i).wait(), None)
    lax.fori_loop(0, blocks, lambda i, c: base_copy(i).wait(), None)
    sums_copy.wait()
    for kind, ref in enumerate((qkv_out, att_out, mix_out)):
        pltpu.make_async_copy(ref, ref, window_sems.at[kind]).wait()


FIRST_IN_ATTEND = (1, 2, 4, 5, 6, 7)
FIRST_IN_PROJECT = (1, 2, 4, 6)
SECOND_IN_PROJECT = (0, 1, 3, 5, 7)


def backward_kernel(
    orders_a, orders_b, fields, slots, width,
    counts, starts, qkv, probs, mix, unit, att, x_in, base, act, sums_a,
    w_qkv_hbm, gain_attn, shift_attn, w_down_hbm,
    d_in, enc, out_a, out_b,
    packed_v, mask_v, gb_qkv, total_a, total_b, w_qkv, w_down, load_sem, store_sems, weight_sems,
    sent_a, got_a, summed_a, send_a, recv_a, sent_b, got_b, summed_b, send_b, recv_b,
):
    first = Reducer(orders_a, total_a.shape[0], total_a, sent_a, got_a, summed_a, send_a, recv_a)
    second = Reducer(orders_b, total_b.shape[0], total_b, sent_b, got_b, summed_b, send_b, recv_b)
    load = pltpu.make_async_copy(sums_a, total_a, load_sem)
    load.start()
    weight_loads = start_all(((w_qkv_hbm, w_qkv), (w_down_hbm, w_down)), weight_sems)
    steps = fields // UNROLL
    rows = UNROLL * slots

    first.greet(first.partners() | second.partners())
    fill_mask(mask_v)
    total_b[...] = jnp.zeros_like(total_b)
    gb_qkv[...] = jnp.zeros_like(gb_qkv)

    def at_step(step, reducer, ahead, begin):
        for k, when in enumerate(ahead):

            @pl.when(step == when)
            def _(k=k):
                reducer.advance(begin + k)

    def field_rows(step, u):
        return pl.ds(pl.multiple_of((step * UNROLL + u) * slots, slots), slots)

    def here(step):
        return pl.ds(pl.multiple_of(step * rows, rows), rows)

    def attend(qkv_b, probs_b, mix_b, unit_b):
        step = pl.program_id(0)

        @pl.when(step == FIRST_IN_ATTEND[0])
        def _():
            load.wait()

        at_step(step, first, FIRST_IN_ATTEND, 0)
        grads = []
        for u in range(UNROLL):
            f = step * UNROLL + u
            head = lax.rem(starts[f], TILE)
            slot_row = lax.broadcasted_iota(jnp.int32, (slots, width), 0)
            live = (slot_row >= head) & (slot_row < head + counts[f])
            grads.append(block_heads(mix_b[u] * live.astype(f32).astype(bf16), mask_v))
        d_probs = [heads_dot(qkv_b[u, :, 2 * width :], grads[u]) for u in range(UNROLL)]
        for u in range(UNROLL):
            packed_v[field_rows(step, u), 2 * width :] = heads_out(probs_b[u], grads[u]).astype(bf16)
        d_scores = []
        for u in range(UNROLL):
            weights = probs_b[u].astype(f32)
            weighted = weights * d_probs[u]
            inner = jnp.sum(weighted, axis=0, keepdims=True)
            d_scores.append((weighted - weights * inner).astype(bf16))
        for u in range(UNROLL):
            query = block_heads(qkv_b[u, :, :width], mask_v)
            packed_v[field_rows(step, u), width : 2 * width] = heads_out(d_scores[u], query).astype(bf16)
        turned = [pairs_t(d_score) for d_score in d_scores]
        for u in range(UNROLL):
            d_query = heads_out_t(turned[u], qkv_b[u, :, width : 2 * width])
            packed_v[field_rows(step, u), :width] = (d_query * HEAD**-0.5).astype(bf16)
        grad = packed_v[here(step), :]
        add_blocks(total_b, 0, mm_tn(unit_b[...].reshape(rows, width), grad))
        gb_qkv[...] += fold(grad.astype(f32))

    def block(*shape):
        return pl.BlockSpec((UNROLL,) + shape, lambda i: (i, 0, 0))

    pltpu.emit_pipeline(
        attend,
        grid=(steps,),
        in_specs=[block(slots, 3 * width)] + [block(slots, width)] * 3,
    )(qkv, probs, mix, unit)

    for copy in weight_loads:
        copy.wait()
    at = 3 * width * width // LANES
    add_vector(total_b, at, gb_qkv[...])
    grad_sum = jnp.sum(gb_qkv[...], axis=0, keepdims=True)
    gain = jnp.broadcast_to(row(gain_attn), (LANES, width)).T
    shift = jnp.broadcast_to(row(shift_attn), (LANES, width)).T
    gain_sum = jnp.zeros((width, LANES), f32)
    shift_sum = jnp.zeros((width, LANES), f32)
    for k in range(3 * width // LANES):
        at_rows = pl.ds(k * width, width)
        cols = slice(k * LANES, (k + 1) * LANES)
        weight = w_qkv[:, cols].astype(f32)
        part = total_b[at_rows, :]
        column = jnp.broadcast_to(grad_sum[:, cols], (width, LANES))
        gain_sum += weight * part
        shift_sum += weight * column
        total_b[at_rows, :] = gain * part + shift * column
    at += 3 * width // LANES
    at = add_vector(total_b, at, gain_sum.T)
    add_vector(total_b, at, shift_sum.T)

    less = PART // SPLIT

    def project(x_b, att_b, act_b, base_b, d_in_b, enc_b):
        step = pl.program_id(0)
        at_step(step, second, SECOND_IN_PROJECT, 0)
        at_step(step, first, FIRST_IN_PROJECT, len(FIRST_IN_ATTEND))
        grads, downs = {}, {}
        for k in range(rows // PART + 1):
            if k < rows // PART:
                at = pl.multiple_of(step * rows + k * PART, PART)
                grads[k] = mm_nt(packed_v[pl.ds(at, PART), :], w_qkv[...])
                downs[k] = mm(act_b[k * less : (k + 1) * less, :], w_down[...])
            if k:
                part = pl.ds((k - 1) * PART, PART)
                unit, rstd = row_norm(x_b[part, :].astype(f32))
                d_x = norm_back(grads.pop(k - 1) * row(gain_attn), unit, rstd)
                d_in_b[part, :] = (att_b[part, :].astype(f32) + d_x).astype(bf16)
                part = pl.ds((k - 1) * less, less)
                enc_b[part, :] = (base_b[part, :].astype(f32) + downs.pop(k - 1)).astype(bf16)

    narrow = pl.BlockSpec((rows, width), lambda i: (i, 0))
    short = pl.BlockSpec((rows // SPLIT, width), lambda i: (i, 0))
    pltpu.emit_pipeline(
        project,
        grid=(steps,),
        in_specs=[
            narrow, narrow, pl.BlockSpec((rows // SPLIT, act.shape[1]), lambda i: (i, 0)), short,
        ],
        out_specs=[narrow, short],
    )(x_in, att, act, base, d_in, enc)

    for k in range(len(FIRST_IN_ATTEND) + len(FIRST_IN_PROJECT), first.steps):
        first.advance(k)
    store_a = pltpu.make_async_copy(summed_a, out_a, store_sems.at[0])
    store_a.start()
    for k in range(len(SECOND_IN_PROJECT), second.steps):
        second.advance(k)
    store_b = pltpu.make_async_copy(summed_b, out_b, store_sems.at[1])
    store_b.start()
    store_a.wait()
    store_b.wait()


def unblock(src, at, dst):
    rows, columns = dst.shape
    for k in range(columns // LANES):
        dst[:, k * LANES : (k + 1) * LANES] = src[pl.ds(at + k * rows, rows), :].astype(f32)


def unblock_t(src, at, dst):
    rows, columns = dst.shape
    for k in range(rows // LANES):
        part = src[pl.ds(at + k * columns, columns), :].astype(f32)
        dst[k * LANES : (k + 1) * LANES, :] = part.T


def unblock_vector(rows, at, dst):
    (columns,) = dst.shape
    for k in range(columns // LANES):
        dst[k * LANES : (k + 1) * LANES] = rows[at + k : at + k + 1, :].reshape(LANES)


def unpack_kernel(
    fields, slots, width, hidden,
    counts, starts, visible, d_in, enc, base, act, w_down_hbm, sums_a_hbm, sums_b_hbm,
    encoded, input_grad, w_qkv, b_query, b_value, w_out, b_out, w_up, b_up, w_down, b_down,
    gain_attn, shift_attn, gain_mlp, shift_mlp,
    picks_v, d_in_v, enc_v, out_v, grad_v, act_v, qkv_v, up_v, down_v,
    sums_a, sums_b, w_down_in, sems, weight_sems,
):
    up_at, down_at, out_at, at = sum_rows(width, hidden)
    steps = fields // GROUP

    def group(step):
        return pl.ds(step * GROUP, GROUP)

    def enc_load(src, step):
        rows = pl.ds(pl.multiple_of(step * GROUP * slots, GROUP * slots), GROUP * slots)
        return pltpu.make_async_copy(src.at[rows], enc_v.at[rows], sems.at[1, step])

    early = enc.shape[0] // (GROUP * slots)

    def act_load(step):
        size = GROUP * slots
        src = pl.ds(pl.multiple_of(step * size, size), size)
        dst = pl.ds(pl.multiple_of((step - early) * size, size), size)
        return pltpu.make_async_copy(act.at[src], act_v.at[dst], sems.at[2, step])

    def used(step):
        return step * GROUP * slots < starts[fields - 1] + slots

    def loads(step):
        rows = pl.ds(pl.multiple_of(step * GROUP * slots, GROUP * slots), GROUP * slots)
        return (
            pltpu.make_async_copy(d_in.at[rows], d_in_v.at[rows], sems.at[0, step]),
        )

    def stores(step):
        return (
            pltpu.make_async_copy(out_v.at[group(step)], encoded.at[group(step)], sems.at[1, step]),
            pltpu.make_async_copy(grad_v.at[group(step)], input_grad.at[group(step)], sems.at[0, step]),
        )

    def start_loads(step, carry):
        for copy in loads(step):
            copy.start()

        @pl.when(step < early)
        def _():
            enc_load(enc, step).start()

        @pl.when((step >= early) & used(step))
        def _():
            enc_load(base, step).start()
            act_load(step).start()

        return carry

    def wait_stores(step, carry):
        for copy in stores(step):
            copy.wait()
        return carry

    def unpack(step, carry):
        for copy in loads(step):
            copy.wait()

        @pl.when(step < early)
        def _():
            enc_load(enc, step).wait()

        @pl.when((step >= early) & used(step))
        def _():
            enc_load(base, step).wait()
            act_load(step).wait()
            size = GROUP * slots
            here = pl.ds(pl.multiple_of(step * size, size), size)
            late = pl.ds(pl.multiple_of((step - early) * size, size), size)
            last = enc_v[here, :].astype(f32) + mm(act_v[late, :], w_down_in[...])
            enc_v[here, :] = last.astype(bf16)

        patch_row = lax.broadcasted_iota(jnp.int32, (input_grad.shape[1], slots), 0)
        rows = lax.broadcasted_iota(jnp.int32, (slots, slots), 0)
        cols = lax.broadcasted_iota(jnp.int32, (slots, slots), 1)
        puts, shifts = [], []
        for u in range(GROUP):
            f = step * GROUP + u
            head, count = lax.rem(starts[f], TILE), counts[f]
            picks = shifted_picks(picks_v[pl.ds(f, 1), :], head, count)
            puts.append((patch_row == picks).astype(f32).astype(bf16))
            shifts.append(((cols - rows == head) & (rows < count)).astype(f32).astype(bf16))
        for u in range(GROUP):
            f = step * GROUP + u
            window = pl.ds(pl.multiple_of(f * slots, slots), slots)
            grad_v[f] = mm(puts[u], d_in_v[window, :]).astype(bf16)
            at = pl.multiple_of(starts[f] - lax.rem(starts[f], TILE), TILE)
            out_v[f] = mm(shifts[u], enc_v[pl.ds(at, slots), :]).astype(bf16)
        for copy in stores(step):
            copy.start()
        return carry

    ahead = [
        pltpu.make_async_copy(src, dst, weight_sems.at[3 + k])
        for k, (src, dst) in enumerate(
            ((sums_a_hbm, sums_a), (sums_b_hbm, sums_b), (w_down_hbm, w_down_in))
        )
    ]
    for copy in ahead:
        copy.start()
    lax.fori_loop(0, steps, start_loads, 0)
    picks_v[...] = visible[...].T
    for copy in ahead:
        copy.wait()
    copies = []
    unblock(sums_a, up_at, up_v)
    copies.append(pltpu.make_async_copy(up_v, w_up, weight_sems.at[0]))
    copies[0].start()
    unblock_t(sums_a, down_at, down_v)
    copies.append(pltpu.make_async_copy(down_v, w_down, weight_sems.at[1]))
    copies[1].start()
    unblock(sums_b, 0, qkv_v)
    copies.append(pltpu.make_async_copy(qkv_v, w_qkv, weight_sems.at[2]))
    copies[2].start()
    unblock(sums_a, out_at, w_out)
    vectors = sums_a[pl.ds(at, 2 * TILE), :].astype(f32)
    at = 0
    for ref in (b_up, b_down, b_out, gain_mlp, shift_mlp):
        unblock_vector(vectors, at, ref)
        at += ref.shape[0] // LANES
    vectors = sums_b[pl.ds(3 * width * width // LANES, TILE), :].astype(f32)
    at = 0
    for ref, rows in ((b_query, 2), (b_value, 1), (gain_attn, 1), (shift_attn, 1)):
        unblock_vector(vectors, at, ref)
        at += rows * width // LANES
    lax.fori_loop(0, steps, unpack, 0)
    lax.fori_loop(0, steps, wait_stores, 0)
    for copy in copies:
        copy.wait()


def forward(sizes, args):
    (
        patches, visible, counts, upstream, w_qkv, b_query, b_value, w_out, b_out,
        w_up, b_up, w_down, b_down, gain_attn, shift_attn, gain_mlp, shift_mlp,
    ) = args
    fields, _, width = patches.shape
    slots, hidden = visible.shape[1], w_up.shape[1]
    cap = (fields * slots + ROWS - 1) // ROWS * ROWS
    tall = cap + ROWS
    vectors = (hidden + 4 * width) // LANES
    rows_a = padded_rows(sum_rows(width, hidden)[3] + vectors, sizes)
    shape = jax.ShapeDtypeStruct
    hbm = pl.BlockSpec(memory_space=pl.ANY)
    vmem = pl.BlockSpec(memory_space=pltpu.VMEM)
    smem = pl.BlockSpec(memory_space=pltpu.SMEM)
    windows = shape((fields, slots, width), bf16)
    return pl.pallas_call(
        functools.partial(forward_kernel, fields, slots, width, hidden),
        out_shape=[
            shape((fields,), jnp.int32),
            windows,
            windows,
            shape((fields, slots, 3 * width), bf16),
            windows,
            windows,
            windows,
            shape((cap, width), bf16),
            shape((cap, hidden), bf16),
            shape((rows_a, LANES), f32),
        ],
        in_specs=[smem, hbm, vmem, hbm, hbm, vmem, vmem, hbm, vmem, hbm, vmem, hbm] + [vmem] * 5,
        out_specs=[smem] + [hbm] * 9,
        scratch_shapes=[
            pltpu.VMEM((tall, width), bf16),
            pltpu.VMEM((tall, width), bf16),
            pltpu.VMEM((cap, 3 * width), bf16),
            pltpu.VMEM((tall, width), bf16),
            pltpu.VMEM((2, AHEAD, slots, width), bf16),
            pltpu.VMEM((2, ROWS, hidden), bf16),
            pltpu.VMEM((ROWS, hidden), bf16),
            pltpu.VMEM((4 * HEAD, 4 * HEAD), bf16),
            pltpu.VMEM((fields, slots), jnp.int32),
            pltpu.VMEM((8, hidden), f32),
            pltpu.VMEM((8, width), f32),
            pltpu.VMEM((8, width), f32),
            pltpu.VMEM((8, width), f32),
            pltpu.VMEM((8, width), f32),
            pltpu.SemaphoreType.DMA((6,)),
            pltpu.SemaphoreType.DMA((2,)),
            pltpu.SemaphoreType.DMA((2, fields // BATCH)),
            pltpu.SemaphoreType.DMA((2,)),
            pltpu.SemaphoreType.DMA((cap // ROWS,)),
            pltpu.VMEM(w_qkv.shape, bf16),
            pltpu.VMEM(w_out.shape, bf16),
            pltpu.VMEM(w_up.shape, bf16),
            pltpu.VMEM(w_down.shape, bf16),
            pltpu.SemaphoreType.DMA((4,)),
            pltpu.VMEM((rows_a, LANES), f32),
            pltpu.SemaphoreType.DMA,
        ],
        compiler_params=pltpu.CompilerParams(vmem_limit_bytes=VMEM_BYTES),
        name="forward_rows",
    )(
        counts, patches.reshape(-1, width), visible.T, upstream.reshape(-1, width),
        w_qkv, b_query, b_value, w_out, b_out, w_up, b_up, w_down, b_down, gain_attn, shift_attn, gain_mlp, shift_mlp,
    )


def backward(
    sizes, counts, starts, qkv, probs, mix, unit, att, x_rows, base, act, sums_a,
    w_qkv, gain, shift, w_down,
):
    fields, slots, width = mix.shape
    orders_a, orders_b = exchange_orders(sizes), direct_orders(sizes)
    rows_b = padded_rows((3 * width * width + 5 * width) // LANES, sizes)
    shape = jax.ShapeDtypeStruct
    hbm = pl.BlockSpec(memory_space=pl.ANY)
    vmem = pl.BlockSpec(memory_space=pltpu.VMEM)
    smem = pl.BlockSpec(memory_space=pltpu.SMEM)
    return pl.pallas_call(
        functools.partial(backward_kernel, orders_a, orders_b, fields, slots, width),
        out_shape=[
            shape((fields * slots, width), bf16),
            shape((act.shape[0] // SPLIT, width), bf16),
            shape(sums_a.shape, bf16),
            shape((rows_b, LANES), bf16),
        ],
        in_specs=[smem, smem] + [hbm] * 10 + [vmem] * 2 + [hbm],
        out_specs=[hbm] * 4,
        scratch_shapes=[
            pltpu.VMEM((fields * slots, 3 * width), bf16),
            pltpu.VMEM((4 * HEAD, 4 * HEAD), bf16),
            pltpu.VMEM((8, 3 * width), f32),
            pltpu.VMEM(sums_a.shape, f32),
            pltpu.VMEM((rows_b, LANES), f32),
            pltpu.VMEM(w_qkv.shape, bf16),
            pltpu.VMEM(w_down.shape, bf16),
            pltpu.SemaphoreType.DMA,
            pltpu.SemaphoreType.DMA((2,)),
            pltpu.SemaphoreType.DMA((2,)),
        ]
        + reducer_scratch(sums_a.shape[0], orders_a)
        + reducer_scratch(rows_b, orders_b),
        compiler_params=pltpu.CompilerParams(
            collective_id=0, has_side_effects=True, vmem_limit_bytes=VMEM_BYTES
        ),
        name="backward_rows",
    )(
        counts, starts, qkv, probs, mix, unit, att.reshape(-1, width), x_rows.reshape(-1, width),
        base, act, sums_a, w_qkv, gain, shift, w_down,
    )


def unpack_all(
    counts, starts, visible, d_in, enc, base, act, w_down, sums_a, sums_b, patch_rows, hidden
):
    (slots, fields), width = visible.shape, d_in.shape[1]
    shape = jax.ShapeDtypeStruct
    hbm = pl.BlockSpec(memory_space=pl.ANY)
    vmem = pl.BlockSpec(memory_space=pltpu.VMEM)
    smem = pl.BlockSpec(memory_space=pltpu.SMEM)
    vector = shape((width,), f32)
    return pl.pallas_call(
        functools.partial(unpack_kernel, fields, slots, width, hidden),
        out_shape=[
            shape((fields, slots, width), bf16),
            shape((fields, patch_rows, width), bf16),
            shape((width, 3 * width), f32), vector, vector,
            shape((width, width), f32), vector,
            shape((width, hidden), f32), shape((hidden,), f32),
            shape((hidden, width), f32), vector,
            vector, vector, vector, vector,
        ],
        in_specs=[smem, smem, vmem] + [hbm] * 7,
        out_specs=[hbm] * 3 + [vmem] * 4 + [hbm, vmem, hbm] + [vmem] * 5,
        scratch_shapes=[
            pltpu.VMEM((fields, slots), jnp.int32),
            pltpu.VMEM(d_in.shape, bf16),
            pltpu.VMEM(base.shape, bf16),
            pltpu.VMEM((fields, slots, width), bf16),
            pltpu.VMEM((fields, patch_rows, width), bf16),
            pltpu.VMEM((base.shape[0] - enc.shape[0], hidden), bf16),
            pltpu.VMEM((width, 3 * width), f32),
            pltpu.VMEM((width, hidden), f32),
            pltpu.VMEM((hidden, width), f32),
            pltpu.VMEM(sums_a.shape, bf16),
            pltpu.VMEM(sums_b.shape, bf16),
            pltpu.VMEM(w_down.shape, bf16),
            pltpu.SemaphoreType.DMA((3, fields // GROUP)),
            pltpu.SemaphoreType.DMA((6,)),
        ],
        compiler_params=pltpu.CompilerParams(vmem_limit_bytes=VMEM_BYTES),
        name="unpack_rows",
    )(counts, starts, visible, d_in, enc, base, act, w_down, sums_a, sums_b)


def per_device(sizes, *args):
    patches, visible, counts = args[:3]
    w_qkv, w_up, gain_attn, shift_attn = args[4], args[9], args[13], args[14]
    starts, x_rows, unit, qkv, probs, att, mix, base, act, sums_a = forward(sizes, args)
    d_in, enc, total_a, total_b = backward(
        sizes, counts, starts, qkv, probs, mix, unit, att, x_rows, base, act, sums_a,
        w_qkv, gain_attn, shift_attn, args[11],
    )
    return tuple(
        unpack_all(
            counts, starts, visible.T, d_in, enc, base, act, args[11], total_a, total_b, patches.shape[1], w_up.shape[1]
        )
    )


def solution(mesh):
    rows = P(("wide", "narrow"))
    return jax.shard_map(
        functools.partial(per_device, dict(mesh.shape)),
        mesh=mesh,
        in_specs=(rows,) * 4 + (P(),) * 13,
        out_specs=(rows,) * 2 + (P(),) * 13,
        check_vma=False,
    )
```
